32 devices in a mesh: tile: 8 (over z, y), acq: 4 (over x, core).
Axes of the slice: x: 2, y: 2, z: 4, core: 2. Of those that a mesh axis runs over, the one named last changes fastest.
Arguments:
- strips: float32 [192, 512, 1024], P('acq', 'tile'), may hold values from -6 to 6
- strip_quality: float32 [192], P('acq'), may hold values from 0.3 to 3
- valid_ranges: int32 [192, 4], P('acq'), may hold values from 0 to 1024, as said below
Outputs:
- mean_elev: float32 [512, 1024], P('tile', 'acq')
- covariance: float32 [10, 512, 1024], P(None, 'tile', 'acq')
The draws below stay inside these ranges and needn't reach their ends.
Inputs may be any that keep to these rules, and one draw needn't show every extreme that they name: `valid_ranges`: row and column ranges of each strip are non-empty, start in the lower half of the grid and hold at least half of its rows or columns; some strip starts at row and column 0 and ends at the last row and column.
All inputs are finite; a program needn't handle non-finite values.
Results may differ from the reference program's by a relative error of at most 0.0003.
Values sent between devices are 32-bit elements; how exact they have to be, the bound alone decides.
No kernel may reach another device: no remote copies, remote signals or barrier semaphores. Data moves between devices by JAX's collectives and lax.ppermute only.
A program may use at most 192 MiB of HBM per device.

```python
import math
import jax
import jax.numpy as jnp
from jax import lax

NC = 1024
NR = 512
STRIPS = 192


def draw_valid_ranges(key, part):
    keys = jax.random.split(key, 4)
    marker = jnp.arange(STRIPS) == 0
    row_low = jnp.where(marker, 0, jax.random.randint(keys[0], (STRIPS,), 0, NR // 2))
    row_span = jax.random.randint(keys[1], (STRIPS,), NR // 2, NR + 1)
    row_high = jnp.where(marker, NR, jnp.minimum(row_low + row_span, NR))
    col_low = jnp.where(marker, 0, jax.random.randint(keys[2], (STRIPS,), 0, NC // 2))
    col_span = jax.random.randint(keys[3], (STRIPS,), NC // 2, NC + 1)
    col_high = jnp.where(marker, NC, jnp.minimum(col_low + col_span, NC))
    return jnp.stack([row_low, row_high, col_low, col_high], axis=1).astype(jnp.int32)


def steps_of(own_key, dims, cuts, smallest, top_value):
    level = 1.0
    for axis_at, parts in cuts:
        heights = jax.random.uniform(jax.random.fold_in(jax.random.fold_in(own_key, 6), axis_at), (parts,), jnp.float32, smallest / len(cuts), top_value / len(cuts))
        level = level * jnp.repeat(jnp.exp(heights), dims[axis_at] // parts).reshape((-1,) + (1,) * (len(dims) - 1 - axis_at))
    return level


def scatter_about(rng, dims, scale, limit, shards=(), kind=jnp.bfloat16):
    drawn = scale * jax.random.normal(rng, dims, jnp.float32)
    if shards:
        drawn = drawn * steps_of(rng, dims, shards, -0.22, 0.18)
    return jnp.clip(drawn, -limit, limit).astype(kind)


def setup_inputs(seed: int = 0) -> dict:
    streams_of = jax.random.split(jax.random.key(seed), 4)
    strips = scatter_about(streams_of[0], (STRIPS, NR, NC), 1.0, 6.0, ((0, 4), (1, 8)), jnp.float32)
    strip_quality = jnp.clip(jnp.exp(math.log(3.0) - 2.3025851 * jax.random.uniform(streams_of[1], (STRIPS,), jnp.float32) ** steps_of(streams_of[1], (STRIPS,), ((0, 4),), -0.2, 0.2)), 0.3, 3.0)
    valid_ranges = draw_valid_ranges(jax.random.fold_in(streams_of[3], 71), 0)
    return {"strips": strips, "strip_quality": strip_quality, "valid_ranges": valid_ranges}


def stencils(padded, lat_cosine):
    row_count = padded.shape[-2] - 4
    col_count = padded.shape[-1]

    def rows_at(offset):
        return padded[..., offset:offset + row_count, :]

    elevation = rows_at(2)
    slope_y = (rows_at(0) - 8.0 * rows_at(1) + 8.0 * rows_at(3) - rows_at(4)) / 12.0
    second_y = (-rows_at(0) + 16.0 * rows_at(1) - 30.0 * elevation + 16.0 * rows_at(3) - rows_at(4)) / 12.0
    widths = [(0, 0)] * (elevation.ndim - 1) + [(2, 2)]
    widened = jnp.pad(elevation, widths)

    def cols_at(offset):
        return widened[..., offset:offset + col_count]

    slope_x = (cols_at(0) - 8.0 * cols_at(1) + 8.0 * cols_at(3) - cols_at(4)) / (12.0 * lat_cosine)
    second_x = (-cols_at(0) + 16.0 * cols_at(1) - 30.0 * elevation + 16.0 * cols_at(3) - cols_at(4)) / (12.0 * lat_cosine * lat_cosine)
    return elevation, slope_x, slope_y, second_x + second_y


def moment_terms(moment_grids, merge_weight):
    moment_addend_list = [merge_weight]
    for first_derivative in range(4):
        moment_addend_list.append(merge_weight * moment_grids[first_derivative])
    for first_derivative in range(4):
        for second_derivative in range(first_derivative, 4):
            moment_addend_list.append(merge_weight * moment_grids[first_derivative] * moment_grids[second_derivative])
    return moment_addend_list


def finalize(moments):
    denominator = jnp.maximum(moments[0], 1.0)
    weighted_means = [moments[1 + first_derivative] / denominator for first_derivative in range(4)]
    entries = []
    position = 5
    for first_derivative in range(4):
        for second_derivative in range(first_derivative, 4):
            entries.append(moments[position] / denominator - weighted_means[first_derivative] * weighted_means[second_derivative])
            position += 1
    return weighted_means[0], jnp.stack(entries)


def reference(strips, strip_quality, valid_ranges):
    latitude_degrees = -1.0 + 2.0 * (jnp.arange(NR).astype(jnp.float32) + 0.5) / NR
    lat_cosine = jnp.cos(latitude_degrees)[:, None]
    row_index = jnp.arange(NR, dtype=jnp.int32)[:, None]
    col_index = jnp.arange(NC, dtype=jnp.int32)[None, :]

    def accumulate(total, current):
        elevations, quality, extent = current
        padded = jnp.pad(elevations, ((2, 2), (0, 0)))
        moment_grids = stencils(padded, lat_cosine)
        inside = ((row_index >= extent[0]) & (row_index < extent[1]) & (col_index >= extent[2]) & (col_index < extent[3])).astype(jnp.float32)
        merge_weight = inside * quality / (1.0 + moment_grids[1] * moment_grids[1] + moment_grids[2] * moment_grids[2])
        return total + jnp.stack(moment_terms(moment_grids, merge_weight)), None

    initial = jnp.zeros((15, NR, NC), jnp.float32)
    total, unused = lax.scan(accumulate, initial, (strips, strip_quality, valid_ranges))
    return finalize(total)
```

```python
import functools
import jax
import jax.numpy as jnp
from jax import lax
from jax.experimental import pallas as pl
from jax.experimental.pallas import tpu as pltpu
from jax.sharding import PartitionSpec as P

MOMENTS = 15
FEATURES = 4
SUB = 8
LANES = 128
EDGE_ROWS = 4
VMEM_BYTES = 56 * 1024 * 1024
F32 = jnp.float32


def stencil_terms(z, rows, cols, inverse_square, mask):
    row_m2, row_m1, row_p1, row_p2 = rows
    col_m2, col_m1, col_p1, col_p2 = cols
    slope_y = 8.0 * (row_p1 - row_m1) - (row_p2 - row_m2)
    slope_x = 8.0 * (col_p1 - col_m1) - (col_p2 - col_m2)
    center = 30.0 * z
    second_y = 16.0 * (row_p1 + row_m1) - (row_p2 + row_m2) - center
    second_x = 16.0 * (col_p1 + col_m1) - (col_p2 + col_m2) - center
    curvature = second_x * inverse_square + second_y
    steepness = (144.0 + slope_y * slope_y) + slope_x * slope_x * inverse_square
    weight = mask / steepness
    features = (z, slope_x, slope_y, curvature)
    weighted = [weight * feature for feature in features]
    terms = [weight] + weighted
    for first in range(FEATURES):
        for second in range(first, FEATURES):
            terms.append(weighted[first] * features[second])
    return terms


def shifted_columns(z, left, right, lane):
    return (
        pltpu.roll(jnp.where(lane >= LANES - 2, left, z), 2, 1),
        pltpu.roll(jnp.where(lane == LANES - 1, left, z), 1, 1),
        pltpu.roll(jnp.where(lane == 0, right, z), LANES - 1, 1),
        pltpu.roll(jnp.where(lane < 2, right, z), LANES - 2, 1),
    )


def zero_terms():
    return tuple(jnp.zeros((SUB, LANES), F32) for _ in range(MOMENTS))


def halo_kernel(strips_ref, top_ref, bottom_ref, inner_ref, first_ref, last_ref, sems):
    strip_count, row_block, col_count = strips_ref.shape
    copies = []
    for tile in range(col_count // LANES):
        lanes = pl.ds(tile * LANES, LANES)
        for which, (start, target) in enumerate(((0, first_ref), (row_block - SUB, last_ref))):
            copies.append(
                pltpu.make_async_copy(
                    strips_ref.at[:, pl.ds(start, SUB), lanes], target.at[tile], sems.at[which, tile]
                )
            )
    for copy in copies:
        copy.start()
    first_rows = first_ref.reshape(col_count // LANES, strip_count * SUB, LANES)
    last_rows = last_ref.reshape(col_count // LANES, strip_count * SUB, LANES)
    for tile in range(col_count // LANES):
        copies[2 * tile].wait()
        copies[2 * tile + 1].wait()
        lanes = slice(tile * LANES, (tile + 1) * LANES)
        for group in range(strip_count // SUB):
            strips = slice(group * SUB, (group + 1) * SUB)
            for row in range(2):
                at = group * SUB * SUB
                top_ref[row, strips, lanes] = first_rows[tile, pl.ds(at + row, SUB, stride=SUB), :]
                bottom_ref[row, strips, lanes] = last_rows[tile, pl.ds(at + 6 + row, SUB, stride=SUB), :]
                inner_ref[row, strips, lanes] = first_rows[tile, pl.ds(at + 2 + row, SUB, stride=SUB), :]
                inner_ref[2 + row, strips, lanes] = last_rows[tile, pl.ds(at + 4 + row, SUB, stride=SUB), :]


def halo_rows(strips):
    strip_count, row_block, col_count = strips.shape
    tiles = col_count // LANES
    pair = jax.ShapeDtypeStruct((2, strip_count, col_count), F32)
    inner = jax.ShapeDtypeStruct((4, strip_count, col_count), F32)
    vmem = pl.BlockSpec(memory_space=pltpu.VMEM)
    return pl.pallas_call(
        halo_kernel,
        out_shape=(pair, pair, inner),
        in_specs=[pl.BlockSpec(memory_space=pl.ANY)],
        out_specs=(vmem, vmem, vmem),
        scratch_shapes=[
            pltpu.VMEM((tiles, strip_count, SUB, LANES), F32),
            pltpu.VMEM((tiles, strip_count, SUB, LANES), F32),
            pltpu.SemaphoreType.DMA((2, tiles)),
        ],
        compiler_params=pltpu.CompilerParams(vmem_limit_bytes=VMEM_BYTES),
        cost_estimate=pl.CostEstimate(flops=0, bytes_accessed=6 << 20, transcendentals=0),
        name="halo_rows",
    )(strips)


def moment_kernel(
    quality_ref, ranges_ref, cosine_ref, strips_ref, mine_ref, other_ref,
    elevation, row_mask, col_mask, sems, *, remote, first_row, row_count, unroll,
):
    strip_count, row_block, col_count = strips_ref.shape
    tiles = col_count // LANES
    half = tiles // 2
    quarter = half // 2
    position = lax.axis_index("acq")
    side = position // 2
    core = position % 2
    base = (1 - side if remote else side) * half
    row_start = lax.axis_index("tile") * row_block + first_row
    low = max(first_row - SUB, 0)
    high = min(first_row + row_count + SUB, row_block)
    offset = SUB - (first_row - low)

    def fetch(index, tile):
        return pltpu.make_async_copy(
            strips_ref.at[:, pl.ds(low, high - low), pl.ds(pl.multiple_of(tile * LANES, LANES), LANES)],
            elevation.at[:, index, pl.ds(offset, high - low), :],
            sems.at[index],
        )

    for index in range(1, half + 1):
        fetch(index, base + index - 1).start()
    has_left = base > 0
    has_right = base + half < tiles

    @pl.when(has_left)
    def _():
        fetch(0, base - 1).start()

    @pl.when(has_right)
    def _():
        fetch(half + 1, base + half).start()

    zero = jnp.zeros((SUB, LANES), F32)

    def blank(index):
        def body(strip, carry):
            for row in range(row_count // SUB + 2):
                elevation[strip, index, row * SUB:(row + 1) * SUB, :] = zero
            return carry

        lax.fori_loop(0, strip_count, body, 0)

    @pl.when(jnp.logical_not(has_left))
    def _():
        blank(0)

    @pl.when(jnp.logical_not(has_right))
    def _():
        blank(half + 1)

    def prepare(strip, carry):
        quality = quality_ref[strip]
        row_low, row_high = ranges_ref[strip, 0], ranges_ref[strip, 1]
        col_low, col_high = ranges_ref[strip, 2], ranges_ref[strip, 3]
        for tile in range(row_count // SUB):
            row = lax.broadcasted_iota(jnp.int32, (SUB, LANES), 0) + (row_start + tile * SUB)
            row_mask[strip, tile * SUB:(tile + 1) * SUB, :] = jnp.where(
                (row >= row_low) & (row < row_high), quality, 0.0
            )
        for tile in range(half):
            col = lax.broadcasted_iota(jnp.int32, (SUB, LANES), 1) + (base + tile) * LANES
            col_mask[strip, tile] = jnp.where((col >= col_low) & (col < col_high), 1.0, 0.0)
        if low == first_row:
            for tile in range(half + 2):
                elevation[strip, tile, 0:SUB, :] = zero
        if high == first_row + row_count:
            for tile in range(half + 2):
                elevation[strip, tile, SUB + row_count:2 * SUB + row_count, :] = zero
        return carry

    lax.fori_loop(0, strip_count, prepare, 0)

    @pl.when(has_left)
    def _():
        fetch(0, base - 1).wait()

    @pl.when(has_right)
    def _():
        fetch(half + 1, base + half).wait()

    for index in range(1, half + 1):
        fetch(index, base + index - 1).wait()

    lane = lax.broadcasted_iota(jnp.int32, (SUB, LANES), 1)
    for out_ref, owner in ((mine_ref, core), (other_ref, 1 - core)):

        def column_tile(tile, carry, out_ref=out_ref, owner=owner):
            at = owner * quarter + tile
            for row in range(row_count // SUB):
                rows = slice(row * SUB, (row + 1) * SUB)
                cosine = cosine_ref[first_row + row * SUB:first_row + (row + 1) * SUB, :]
                inverse_square = 1.0 / (cosine * cosine)

                def add_strip(strip, sums):
                    def load(shift):
                        start = SUB * (row + 1) + shift
                        return elevation[strip, at + 1, start:start + SUB, :]

                    z = load(0)
                    center = slice(SUB * (row + 1), SUB * (row + 2))
                    cols = shifted_columns(
                        z, elevation[strip, at, center, :], elevation[strip, at + 2, center, :], lane
                    )
                    mask = row_mask[strip, rows, :] * col_mask[strip, at]
                    shifts = (load(-2), load(-1), load(1), load(2))
                    terms = stencil_terms(z, shifts, cols, inverse_square, mask)
                    return tuple(total + term for total, term in zip(sums, terms))

                sums = lax.fori_loop(0, strip_count, add_strip, zero_terms(), unroll=unroll)
                lanes = pl.ds(pl.multiple_of(tile * LANES, LANES), LANES)
                for moment in range(MOMENTS):
                    out_ref[moment, rows, lanes] = sums[moment]
            return carry

        lax.fori_loop(0, quarter, column_tile, 0)


def moments_of(quality, ranges, cosine, strips, remote, first_row, row_count):
    strip_count, row_block, col_count = strips.shape
    half = col_count // LANES // 2
    out = jax.ShapeDtypeStruct((MOMENTS, row_count, col_count // 4), F32)
    vmem = pl.BlockSpec(memory_space=pltpu.VMEM)
    smem = pl.BlockSpec(memory_space=pltpu.SMEM)
    cells = strip_count * row_count * col_count // 2
    return pl.pallas_call(
        functools.partial(
            moment_kernel, remote=remote, first_row=first_row, row_count=row_count, unroll=16
        ),
        out_shape=(out, out),
        in_specs=[smem, smem, vmem, pl.BlockSpec(memory_space=pl.ANY)],
        out_specs=(vmem, vmem),
        scratch_shapes=[
            pltpu.VMEM((strip_count, half + 2, row_count + 2 * SUB, LANES), F32),
            pltpu.VMEM((strip_count, row_count, LANES), F32),
            pltpu.VMEM((strip_count, half, SUB, LANES), F32),
            pltpu.SemaphoreType.DMA((half + 2,)),
        ],
        compiler_params=pltpu.CompilerParams(vmem_limit_bytes=VMEM_BYTES),
        cost_estimate=pl.CostEstimate(flops=64 * cells, bytes_accessed=4 * cells, transcendentals=cells),
        name="moments_remote" if remote else "moments_own",
    )(quality, ranges, cosine, strips)


def edge_kernel(
    quality_ref, ranges_ref, cosine_ref, above_ref, top_ref, inner_ref, bottom_ref, below_ref,
    mine_ref, other_ref,
):
    pair, strip_count, col_count = top_ref.shape
    row_block = cosine_ref.shape[0]
    tiles = col_count // LANES
    quarter = tiles // 4
    position = lax.axis_index("acq")
    side = position // 2
    core = position % 2
    row_start = lax.axis_index("tile") * row_block
    lane = lax.broadcasted_iota(jnp.int32, (SUB, LANES), 1)
    sources = [(above_ref, 0), (above_ref, 1), (top_ref, 0), (top_ref, 1), (inner_ref, 0), (inner_ref, 1)]
    sources += [(inner_ref, 2), (inner_ref, 3), (bottom_ref, 0), (bottom_ref, 1), (below_ref, 0), (below_ref, 1)]
    edges = ((0, 2), (1, 3), (row_block - 2, 8), (row_block - 1, 9))
    for out_ref, owner in ((mine_ref, core), (other_ref, 1 - core)):
        for part, owner_side in enumerate((1 - side, side)):
            out_ref[part, MOMENTS * EDGE_ROWS:, :] = jnp.zeros(
                (out_ref.shape[1] - MOMENTS * EDGE_ROWS, quarter * LANES), F32
            )

            def column_tile(tile, carry, out_ref=out_ref, part=part, first=(owner_side * 2 + owner) * quarter):
                at = first + tile
                left_keep = jnp.where(at > 0, 1.0, 0.0)
                right_keep = jnp.where(at < tiles - 1, 1.0, 0.0)
                here = pl.ds(pl.multiple_of(at * LANES, LANES), LANES)
                before = pl.ds(pl.multiple_of(jnp.maximum(at - 1, 0) * LANES, LANES), LANES)
                after = pl.ds(pl.multiple_of(jnp.minimum(at + 1, tiles - 1) * LANES, LANES), LANES)
                col = lane + at * LANES
                out_lanes = pl.ds(pl.multiple_of(tile * LANES, LANES), LANES)
                for edge, (row, source) in enumerate(edges):
                    cosine = cosine_ref[row:row + 1, :]
                    inverse_square = 1.0 / (cosine * cosine)
                    sums = zero_terms()
                    for group in range(strip_count // SUB):
                        strips = slice(group * SUB, (group + 1) * SUB)

                        def load(shift, where):
                            ref, index = sources[source + shift]
                            return ref[index, strips, where]

                        z = load(0, here)
                        cols = shifted_columns(
                            z, load(0, before) * left_keep, load(0, after) * right_keep, lane
                        )
                        limits = [ranges_ref[kind, strips, :] for kind in range(4)]
                        inside = (limits[0] <= row_start + row) & (limits[1] > row_start + row)
                        inside = inside & (col >= limits[2]) & (col < limits[3])
                        mask = jnp.where(inside, quality_ref[strips, :], 0.0)
                        shifts = tuple(load(shift, here) for shift in (-2, -1, 1, 2))
                        terms = stencil_terms(z, shifts, cols, inverse_square, mask)
                        sums = [total + term for total, term in zip(sums, terms)]
                    for moment in range(MOMENTS):
                        spot = moment * EDGE_ROWS + edge
                        out_ref[part, spot:spot + 1, out_lanes] = jnp.sum(sums[moment], axis=0, keepdims=True)
                return carry

            lax.fori_loop(0, quarter, column_tile, 0)


def edge_moments(quality, ranges, cosine, above, top, inner, bottom, below):
    pair, strip_count, col_count = top.shape
    out = jax.ShapeDtypeStruct((2, -(-MOMENTS * EDGE_ROWS // SUB) * SUB, col_count // 4), F32)
    vmem = pl.BlockSpec(memory_space=pltpu.VMEM)
    cells = 4 * strip_count * col_count
    return pl.pallas_call(
        edge_kernel,
        out_shape=(out, out),
        in_specs=[vmem] * 8,
        out_specs=(vmem, vmem),
        compiler_params=pltpu.CompilerParams(vmem_limit_bytes=VMEM_BYTES),
        cost_estimate=pl.CostEstimate(flops=64 * cells, bytes_accessed=12 * cells, transcendentals=cells),
        name="moments_edge",
    )(quality, ranges, cosine, above, top, inner, bottom, below)


def finish_kernel(pieces, cosine_ref, mine_ref, core_ref, edge_mine_ref, edge_core_ref, edge_far_ref, *refs):
    far_refs = refs[:len(pieces)]
    mean_ref, covariance_ref = refs[len(pieces):]
    row_block, width = mean_ref.shape
    sub = lax.broadcasted_iota(jnp.int32, (SUB, LANES), 0)
    for first_row, far_ref in zip(pieces, far_refs):
        for tile_row in range(first_row, first_row + far_ref.shape[1], SUB):
            rows = slice(tile_row, tile_row + SUB)
            far_rows = slice(tile_row - first_row, tile_row - first_row + SUB)
            cosine = cosine_ref[rows, :]
            scales = (1.0, 1.0 / (12.0 * cosine), 1.0 / 12.0, 1.0 / 12.0)
            spots = {0: ((0, 0), (1, 1)), row_block - SUB: ((SUB - 2, 2), (SUB - 1, 3))}.get(tile_row, ())
            for tile in range(width // LANES):
                lanes = slice(tile * LANES, (tile + 1) * LANES)

                def total(moment):
                    value = (mine_ref[moment, rows, lanes] + core_ref[moment, rows, lanes]) + far_ref[moment, far_rows, lanes]
                    for at, edge in spots:
                        spot = moment * EDGE_ROWS + edge
                        spot = slice(spot, spot + 1)
                        line = (edge_mine_ref[1, spot, lanes] + edge_core_ref[1, spot, lanes]) + edge_far_ref[spot, lanes]
                        value = jnp.where(sub == at, line, value)
                    return value

                inverse = 144.0 / jnp.maximum(144.0 * total(0), 1.0)
                means = [total(1 + first) * inverse * scales[first] for first in range(FEATURES)]
                mean_ref[rows, lanes] = means[0]
                entry = 0
                for first in range(FEATURES):
                    for second in range(first, FEATURES):
                        scale = scales[first] * scales[second]
                        covariance_ref[entry, rows, lanes] = (
                            total(5 + entry) * inverse * scale - means[first] * means[second]
                        )
                        entry += 1


def finish(pieces, cosine, mine, core, edge_mine, edge_core, edge_far, far):
    moments, row_block, width = mine.shape
    vmem = pl.BlockSpec(memory_space=pltpu.VMEM)
    entries = FEATURES * (FEATURES + 1) // 2
    return pl.pallas_call(
        functools.partial(finish_kernel, pieces),
        out_shape=(
            jax.ShapeDtypeStruct((row_block, width), F32),
            jax.ShapeDtypeStruct((entries, row_block, width), F32),
        ),
        in_specs=[vmem] * (6 + len(far)),
        out_specs=(vmem, vmem),
        compiler_params=pltpu.CompilerParams(vmem_limit_bytes=VMEM_BYTES),
        name="finish",
    )(cosine, mine, core, edge_mine, edge_core, edge_far, *far)


def exchange(value, distance):
    count = lax.axis_size("acq")
    return lax.ppermute(value, "acq", [(source, source ^ distance) for source in range(count)])


def local(strips, strip_quality, valid_ranges):
    strip_count, row_block, col_count = strips.shape
    tile_count = lax.axis_size("tile")
    row_index = lax.axis_index("tile") * row_block + jnp.arange(row_block, dtype=jnp.int32)
    latitude = -1.0 + 2.0 * (row_index.astype(F32) + 0.5) / (row_block * tile_count)
    cosine = jnp.broadcast_to(jnp.cos(latitude)[:, None], (row_block, LANES))
    quality_lanes = jnp.broadcast_to(strip_quality[:, None], (strip_count, LANES))
    range_lanes = jnp.broadcast_to(valid_ranges.T[:, :, None], (4, strip_count, LANES))

    top, bottom, inner = halo_rows(strips)
    forward = [(i, i + 1) for i in range(tile_count - 1)]
    backward = [(target, source) for source, target in forward]
    above = lax.ppermute(bottom, "tile", forward)
    below = lax.ppermute(top, "tile", backward)

    piece_rows = row_block // 2
    pieces = tuple(range(0, row_block, piece_rows))
    far = []
    for first_row in pieces:
        mine, other = moments_of(strip_quality, valid_ranges, cosine, strips, True, first_row, piece_rows)
        far.append(exchange(mine + exchange(other, 1), 2))
    mine, other = moments_of(strip_quality, valid_ranges, cosine, strips, False, 0, row_block)
    core = exchange(other, 1)
    edge_mine, edge_other = edge_moments(quality_lanes, range_lanes, cosine, above, top, inner, bottom, below)
    edge_core = exchange(edge_other, 1)
    edge_far = exchange(edge_mine[0] + edge_core[0], 2)
    return finish(pieces, cosine, mine, core, edge_mine, edge_core, edge_far, far)


def solution(mesh):
    return jax.shard_map(
        local,
        mesh=mesh,
        in_specs=(P("acq", "tile", None), P("acq"), P("acq", None)),
        out_specs=(P("tile", "acq"), P(None, "tile", "acq")),
        check_vma=False,
    )
```

```python
import functools
import jax
import jax.numpy as jnp
from jax import lax
from jax.experimental import pallas as pl
from jax.experimental.pallas import tpu as pltpu
from jax.sharding import PartitionSpec as P

MOMENTS = 15
FEATURES = 4
SUB = 8
LANES = 128
EDGE_ROWS = 4
VMEM_BYTES = 56 * 1024 * 1024
F32 = jnp.float32
LOAD_PARTS = 4
SMALL_COST = pl.CostEstimate(flops=1, bytes_accessed=1, transcendentals=0)


def moment_terms(z, slope_x, second_x, rows, inverse_square, mask):
    row_m2, row_m1, row_p1, row_p2 = rows
    slope_y = 8.0 * (row_p1 - row_m1) - (row_p2 - row_m2)
    second_y = 16.0 * (row_p1 + row_m1) - (row_p2 + row_m2) - 30.0 * z
    curvature = second_x * inverse_square + second_y
    steepness = (144.0 + slope_y * slope_y) + slope_x * slope_x * inverse_square
    weight = mask / steepness
    features = (z, slope_x, slope_y, curvature)
    weighted = [weight * feature for feature in features]
    terms = [weight] + weighted
    for first in range(FEATURES):
        for second in range(first, FEATURES):
            terms.append(weighted[first] * features[second])
    return terms


def stencil_terms(z, rows, cols, inverse_square, mask):
    col_m2, col_m1, col_p1, col_p2 = cols
    slope_x = 8.0 * (col_p1 - col_m1) - (col_p2 - col_m2)
    second_x = 16.0 * (col_p1 + col_m1) - (col_p2 + col_m2) - 30.0 * z
    return moment_terms(z, slope_x, second_x, rows, inverse_square, mask)


def shifted_columns(z, left, right, lane):
    return (
        pltpu.roll(jnp.where(lane >= LANES - 2, left, z), 2, 1),
        pltpu.roll(jnp.where(lane == LANES - 1, left, z), 1, 1),
        pltpu.roll(jnp.where(lane == 0, right, z), LANES - 1, 1),
        pltpu.roll(jnp.where(lane < 2, right, z), LANES - 2, 1),
    )


def zero_terms():
    return tuple(jnp.zeros((SUB, LANES), F32) for _ in range(MOMENTS))


def halo_kernel(
    quality_ref, ranges_ref, strips_ref, top_ref, bottom_ref, inner_ref, cosine_ref, limits_ref,
    first_ref, last_ref, sems,
):
    strip_count, row_block, col_count = strips_ref.shape
    copies = []
    for tile in range(col_count // LANES):
        lanes = pl.ds(tile * LANES, LANES)
        for which, (start, target) in enumerate(((0, first_ref), (row_block - SUB, last_ref))):
            copies.append(
                pltpu.make_async_copy(
                    strips_ref.at[:, pl.ds(start, SUB), lanes], target.at[tile], sems.at[which, tile]
                )
            )
    for copy in copies:
        copy.start()
    total_rows = row_block * lax.axis_size("tile")
    row_start = lax.axis_index("tile") * row_block
    for tile in range(row_block // SUB):
        row = lax.broadcasted_iota(jnp.int32, (SUB, LANES), 0) + (row_start + tile * SUB)
        latitude = -1.0 + 2.0 * (row.astype(F32) + 0.5) / total_rows
        cosine_ref[tile * SUB:(tile + 1) * SUB, :] = jnp.cos(latitude)

    def spread(strip, carry):
        here = pl.ds(strip, 1)
        for kind in range(4):
            value = ranges_ref[kind, strip].astype(F32)
            limits_ref[kind, here, :] = jnp.full((1, LANES), value, F32)
        limits_ref[4, here, :] = jnp.full((1, LANES), quality_ref[strip], F32)
        return carry

    lax.fori_loop(0, strip_count, spread, 0)
    first_rows = first_ref.reshape(col_count // LANES, strip_count * SUB, LANES)
    last_rows = last_ref.reshape(col_count // LANES, strip_count * SUB, LANES)
    for tile in range(col_count // LANES):
        copies[2 * tile].wait()
        copies[2 * tile + 1].wait()
        lanes = slice(tile * LANES, (tile + 1) * LANES)
        for group in range(strip_count // SUB):
            strips = slice(group * SUB, (group + 1) * SUB)
            for row in range(2):
                at = group * SUB * SUB
                top_ref[row, strips, lanes] = first_rows[tile, pl.ds(at + row, SUB, stride=SUB), :]
                bottom_ref[row, strips, lanes] = last_rows[tile, pl.ds(at + 6 + row, SUB, stride=SUB), :]
                inner_ref[row, strips, lanes] = first_rows[tile, pl.ds(at + 2 + row, SUB, stride=SUB), :]
                inner_ref[2 + row, strips, lanes] = last_rows[tile, pl.ds(at + 4 + row, SUB, stride=SUB), :]


def halo_rows(quality, ranges, strips):
    strip_count, row_block, col_count = strips.shape
    tiles = col_count // LANES
    pair = jax.ShapeDtypeStruct((2, strip_count, col_count), F32)
    inner = jax.ShapeDtypeStruct((4, strip_count, col_count), F32)
    cosine = jax.ShapeDtypeStruct((row_block, LANES), F32)
    limits = jax.ShapeDtypeStruct((5, strip_count, LANES), F32)
    vmem = pl.BlockSpec(memory_space=pltpu.VMEM)
    smem = pl.BlockSpec(memory_space=pltpu.SMEM)
    return pl.pallas_call(
        halo_kernel,
        out_shape=(pair, pair, inner, cosine, limits),
        in_specs=[smem, smem, pl.BlockSpec(memory_space=pl.ANY)],
        out_specs=(vmem,) * 5,
        scratch_shapes=[
            pltpu.VMEM((tiles, strip_count, SUB, LANES), F32),
            pltpu.VMEM((tiles, strip_count, SUB, LANES), F32),
            pltpu.SemaphoreType.DMA((2, tiles)),
        ],
        compiler_params=pltpu.CompilerParams(vmem_limit_bytes=VMEM_BYTES),
        cost_estimate=SMALL_COST,
        name="halo_rows",
    )(quality, ranges, strips)


def column_weights():
    source = lax.broadcasted_iota(jnp.int32, (4 * LANES, 2 * LANES), 0)
    target = lax.broadcasted_iota(jnp.int32, (4 * LANES, 2 * LANES), 1)
    lane = source % LANES
    lane = jnp.where(source < 2 * LANES, lane, jnp.where(lane < LANES // 2, lane + LANES, lane - LANES))
    distance = lane - target % LANES
    near, far = jnp.abs(distance) == 1, jnp.abs(distance) == 2
    sign = jnp.where(distance > 0, 1.0, -1.0)
    slope = jnp.where(near, 8.0 * sign, jnp.where(far, -sign, 0.0))
    second = jnp.where(near, 16.0, jnp.where(far, -1.0, jnp.where(distance == 0, -30.0, 0.0)))
    return jnp.where(target < LANES, slope, second).astype(jnp.bfloat16)


def moment_kernel(
    quality_ref, ranges_ref, cosine_ref, strips_ref, first_order_ref, second_order_ref, mine_ref,
    *refs, remote, first_row, row_count, pieces,
):
    other_refs, token_ref = refs[:pieces], refs[pieces]
    elevation, high_part, low_part, row_mask, col_mask, weights, first_slot, second_slot, sems = refs[pieces + 1:]
    del first_order_ref, second_order_ref
    token_ref[...] = jnp.zeros((SUB, LANES), F32)
    strip_count, row_block, col_count = strips_ref.shape
    tiles = col_count // LANES
    half = tiles // 2
    quarter = half // 2
    position = lax.axis_index("acq")
    side = position // 2
    core = position % 2
    base = (1 - side if remote else side) * half
    row_start = lax.axis_index("tile") * row_block + first_row
    low = max(first_row - SUB, 0)
    high = min(first_row + row_count + SUB, row_block)
    offset = SUB - (first_row - low)

    part = strip_count // LOAD_PARTS

    def fetch(index, which):
        lanes = pl.ds(pl.multiple_of((base + index - 1) * LANES, LANES), LANES)
        strips = pl.ds(which * part, part)
        return pltpu.make_async_copy(
            strips_ref.at[strips, pl.ds(low, high - low), lanes],
            elevation.at[strips, index, pl.ds(offset, high - low), :],
            sems.at[index, which],
        )

    def present(index):
        return (base + index >= 1) & (base + index <= tiles)

    def start(index, which):
        @pl.when(present(index))
        def _():
            fetch(index, which).start()

    zero = jnp.zeros((SUB, LANES), F32)

    def blank(index):
        @pl.when(jnp.logical_not(present(index)))
        def _():
            def body(strip, carry):
                for row in range(1, row_count // SUB + 1):
                    elevation[strip, index, row * SUB:(row + 1) * SUB, :] = zero
                return carry

            lax.fori_loop(0, strip_count, body, 0)

    def arrive(index, which):
        @pl.when(present(index))
        def _():
            fetch(index, which).wait()

        def split(step, carry):
            strip = which * part + step
            value = elevation[strip, index, SUB:SUB + row_count, :]
            upper = value.astype(jnp.bfloat16)
            high_part[strip, index] = upper
            low_part[strip, index] = (value - upper.astype(F32)).astype(jnp.bfloat16)
            return carry

        lax.fori_loop(0, part, split, 0, unroll=4)

    initial = (1 - core) * quarter
    later = core * quarter
    final = later + 2 * core
    for which in range(LOAD_PARTS):
        for step in range(3):
            start(initial + step, which)
    blank(0)
    blank(half + 1)

    weights[...] = column_weights()

    def prepare(strip, carry):
        quality = quality_ref[strip]
        row_low, row_high = ranges_ref[0, strip], ranges_ref[1, strip]
        col_low, col_high = ranges_ref[2, strip], ranges_ref[3, strip]
        for tile in range(row_count // SUB):
            row = lax.broadcasted_iota(jnp.int32, (SUB, LANES), 0) + (row_start + tile * SUB)
            row_mask[strip, tile * SUB:(tile + 1) * SUB, :] = jnp.where(
                (row >= row_low) & (row < row_high), quality, 0.0
            )
        for tile in range(half):
            col = lax.broadcasted_iota(jnp.int32, (SUB, LANES), 1) + (base + tile) * LANES
            col_mask[strip, tile] = jnp.where((col >= col_low) & (col < col_high), 1.0, 0.0)
        if low == first_row:
            for tile in range(half + 2):
                elevation[strip, tile, 0:SUB, :] = zero
        if high == first_row + row_count:
            for tile in range(half + 2):
                elevation[strip, tile, SUB + row_count:2 * SUB + row_count, :] = zero
        return carry

    lax.fori_loop(0, strip_count, prepare, 0)

    tile_rows = row_count // SUB
    share = strip_count // tile_rows
    slots = (first_slot, second_slot)

    def columns_into(slot, at, first, count):
        strips = pl.ds(first, count)
        lane = lax.broadcasted_iota(jnp.int32, (count * row_count, LANES), 1)

        def load(ref, tile):
            return ref[strips, tile].reshape(count * row_count, LANES)

        edges = [
            jnp.where(lane < LANES // 2, load(ref, at + 1), load(ref, at - 1))
            for ref in (high_part, low_part)
        ]
        left = jnp.concatenate([load(high_part, at), load(low_part, at)] + edges, axis=1)
        product = jnp.dot(left, weights[...], preferred_element_type=F32)
        slots[slot][strips] = product.reshape(count, row_count, 2 * LANES)

    def column_tile(slot, at, following, store, lanes):
        def row_tile(tile, carry):
            row = pl.multiple_of(tile * SUB, SUB)
            cosine = cosine_ref[pl.ds(first_row + row, SUB), :]
            inverse_square = 1.0 / (cosine * cosine)

            if following is not None:
                columns_into(1 - slot, following, tile * share, share)
            unroll = strip_count if following is not None else 16

            def add_strips(chunk, sums):
                for index in range(unroll):
                    strip = chunk * unroll + index

                    def load(shift):
                        return elevation[strip, at, pl.ds(SUB + row + shift, SUB), :]

                    slope_x = slots[slot][strip, pl.ds(row, SUB), :LANES]
                    second_x = slots[slot][strip, pl.ds(row, SUB), LANES:]
                    mask = row_mask[strip, pl.ds(row, SUB), :] * col_mask[strip, at - 1]
                    shifts = (load(-2), load(-1), load(1), load(2))
                    terms = moment_terms(load(0), slope_x, second_x, shifts, inverse_square, mask)
                    sums = [total + term for total, term in zip(sums, terms)]
                return tuple(sums)

            if following is not None:
                sums = add_strips(0, zero_terms())
            else:
                sums = lax.fori_loop(0, strip_count // unroll, add_strips, zero_terms())
            for moment in range(MOMENTS):
                store(moment, pl.ds(row, SUB), lanes, sums[moment])
            return carry

        lax.fori_loop(0, tile_rows, row_tile, 0)

    for which in range(LOAD_PARTS):
        start(initial + 3, which)
    for which in range(LOAD_PARTS):
        for step in range(2):
            start(final + step, which)

    def first_columns(which, carry):
        for step in range(3):
            arrive(initial + step, which)
        columns_into(0, initial + 1, which * part, part)
        return carry

    lax.fori_loop(0, LOAD_PARTS, first_columns, 0)

    def arrive_whole(index):
        def body(which, carry):
            arrive(index, which)
            return carry

        lax.fori_loop(0, LOAD_PARTS, body, 0)

    def store_other(moment, rows, lanes, value):
        share = MOMENTS // pieces
        other_refs[moment // share][moment % share, rows, lanes] = value

    def store_mine(moment, rows, lanes, value):
        mine_ref[moment, rows, lanes] = value

    arrive_whole(initial + 3)
    column_tile(0, initial + 1, initial + 2, store_other, slice(0, LANES))
    arrive_whole(final)
    arrive_whole(final + 1)
    column_tile(1, initial + 2, later + 1, store_other, slice(LANES, 2 * LANES))
    column_tile(0, later + 1, later + 2, store_mine, slice(0, LANES))
    column_tile(1, later + 2, None, store_mine, slice(LANES, 2 * LANES))


def moments_of(quality, ranges, cosine, strips, order, remote, first_row, row_count, pieces):
    strip_count, row_block, col_count = strips.shape
    half = col_count // LANES // 2
    out = jax.ShapeDtypeStruct((MOMENTS, row_count, col_count // 4), F32)
    piece = jax.ShapeDtypeStruct((MOMENTS // pieces, row_count, col_count // 4), F32)
    token = jax.ShapeDtypeStruct((SUB, LANES), F32)
    vmem = pl.BlockSpec(memory_space=pltpu.VMEM)
    smem = pl.BlockSpec(memory_space=pltpu.SMEM)
    anywhere = pl.BlockSpec(memory_space=pl.ANY)
    parts = pltpu.VMEM((strip_count, half + 2, row_count, LANES), jnp.bfloat16)
    slot = pltpu.VMEM((strip_count, row_count, 2 * LANES), F32)
    return pl.pallas_call(
        functools.partial(moment_kernel, remote=remote, first_row=first_row, row_count=row_count, pieces=pieces),
        out_shape=(out,) + (piece,) * pieces + (token,),
        in_specs=[smem, smem, vmem, anywhere, anywhere, anywhere],
        out_specs=(vmem,) * (pieces + 2),
        scratch_shapes=[
            pltpu.VMEM((strip_count, half + 2, row_count + 2 * SUB, LANES), F32),
            parts,
            parts,
            pltpu.VMEM((strip_count, row_count, LANES), F32),
            pltpu.VMEM((strip_count, half, SUB, LANES), F32),
            pltpu.VMEM((4 * LANES, 2 * LANES), jnp.bfloat16),
            slot,
            slot,
            pltpu.SemaphoreType.DMA((half + 2, LOAD_PARTS)),
        ],
        compiler_params=pltpu.CompilerParams(vmem_limit_bytes=VMEM_BYTES),
        cost_estimate=SMALL_COST,
        name="moments_remote" if remote else "moments_own",
    )(quality, ranges, cosine, strips, *order)


def edge_kernel(
    limits_ref, cosine_ref, above_ref, top_ref, inner_ref, bottom_ref, below_ref,
    order_ref, mine_ref, other_ref, token_ref,
):
    del order_ref
    token_ref[...] = jnp.zeros((SUB, LANES), F32)
    pair, strip_count, col_count = top_ref.shape
    row_block = cosine_ref.shape[0]
    tiles = col_count // LANES
    quarter = tiles // 4
    position = lax.axis_index("acq")
    side = position // 2
    core = position % 2
    row_start = lax.axis_index("tile") * row_block
    lane = lax.broadcasted_iota(jnp.int32, (SUB, LANES), 1)
    sources = [(above_ref, 0), (above_ref, 1), (top_ref, 0), (top_ref, 1), (inner_ref, 0), (inner_ref, 1)]
    sources += [(inner_ref, 2), (inner_ref, 3), (bottom_ref, 0), (bottom_ref, 1), (below_ref, 0), (below_ref, 1)]
    edges = ((0, 2), (1, 3), (row_block - 2, 8), (row_block - 1, 9))
    for out_ref, owner in ((mine_ref, core), (other_ref, 1 - core)):
        for part, owner_side in enumerate((1 - side, side)):
            out_ref[part, MOMENTS * EDGE_ROWS:, :] = jnp.zeros(
                (out_ref.shape[1] - MOMENTS * EDGE_ROWS, quarter * LANES), F32
            )

            def column_tile(tile, carry, out_ref=out_ref, part=part, first=(owner_side * 2 + owner) * quarter):
                at = first + tile
                left_keep = jnp.where(at > 0, 1.0, 0.0)
                right_keep = jnp.where(at < tiles - 1, 1.0, 0.0)
                here = pl.ds(pl.multiple_of(at * LANES, LANES), LANES)
                before = pl.ds(pl.multiple_of(jnp.maximum(at - 1, 0) * LANES, LANES), LANES)
                after = pl.ds(pl.multiple_of(jnp.minimum(at + 1, tiles - 1) * LANES, LANES), LANES)
                col = (lane + at * LANES).astype(F32)
                out_lanes = pl.ds(pl.multiple_of(tile * LANES, LANES), LANES)
                for edge, (row, source) in enumerate(edges):
                    cosine = cosine_ref[row:row + 1, :]
                    inverse_square = 1.0 / (cosine * cosine)
                    sums = zero_terms()
                    for group in range(strip_count // SUB):
                        strips = slice(group * SUB, (group + 1) * SUB)

                        def load(shift, where):
                            ref, index = sources[source + shift]
                            return ref[index, strips, where]

                        z = load(0, here)
                        cols = shifted_columns(
                            z, load(0, before) * left_keep, load(0, after) * right_keep, lane
                        )
                        limits = [limits_ref[kind, strips, :] for kind in range(4)]
                        at_row = (row_start + row).astype(F32)
                        inside = (limits[0] <= at_row) & (limits[1] > at_row)
                        inside = inside & (col >= limits[2]) & (col < limits[3])
                        mask = jnp.where(inside, limits_ref[4, strips, :], 0.0)
                        shifts = tuple(load(shift, here) for shift in (-2, -1, 1, 2))
                        terms = stencil_terms(z, shifts, cols, inverse_square, mask)
                        sums = [total + term for total, term in zip(sums, terms)]
                    for moment in range(MOMENTS):
                        spot = moment * EDGE_ROWS + edge
                        out_ref[part, spot:spot + 1, out_lanes] = jnp.sum(sums[moment], axis=0, keepdims=True)
                return carry

            lax.fori_loop(0, quarter, column_tile, 0)


def edge_moments(limits, cosine, above, top, inner, bottom, below, order):
    pair, strip_count, col_count = top.shape
    out = jax.ShapeDtypeStruct((2, -(-MOMENTS * EDGE_ROWS // SUB) * SUB, col_count // 4), F32)
    vmem = pl.BlockSpec(memory_space=pltpu.VMEM)
    return pl.pallas_call(
        edge_kernel,
        out_shape=(out, out, jax.ShapeDtypeStruct((SUB, LANES), F32)),
        in_specs=[vmem] * 7 + [pl.BlockSpec(memory_space=pl.ANY)],
        out_specs=(vmem, vmem, vmem),
        compiler_params=pltpu.CompilerParams(vmem_limit_bytes=VMEM_BYTES),
        cost_estimate=SMALL_COST,
        name="moments_edge",
    )(limits, cosine, above, top, inner, bottom, below, order)


def finish_kernel(pieces, cosine_ref, mine_ref, edge_mine_ref, edge_core_ref, edge_far_ref, *refs):
    far_refs, core_refs = refs[:len(pieces)], refs[len(pieces):-2]
    mean_ref, covariance_ref = refs[-2:]
    row_block, width = mean_ref.shape
    share = MOMENTS // len(core_refs)
    sub = lax.broadcasted_iota(jnp.int32, (SUB, LANES), 0)
    for first_row, far_ref in zip(pieces, far_refs):
        for tile_row in range(first_row, first_row + far_ref.shape[1], SUB):
            rows = slice(tile_row, tile_row + SUB)
            far_rows = slice(tile_row - first_row, tile_row - first_row + SUB)
            cosine = cosine_ref[rows, :]
            scales = (1.0, 1.0 / (12.0 * cosine), 1.0 / 12.0, 1.0 / 12.0)
            spots = {0: ((0, 0), (1, 1)), row_block - SUB: ((SUB - 2, 2), (SUB - 1, 3))}.get(tile_row, ())
            for tile in range(width // LANES):
                lanes = slice(tile * LANES, (tile + 1) * LANES)

                def total(moment):
                    near = core_refs[moment // share][moment % share, rows, lanes]
                    value = (mine_ref[moment, rows, lanes] + near) + far_ref[moment, far_rows, lanes]
                    for at, edge in spots:
                        spot = moment * EDGE_ROWS + edge
                        spot = slice(spot, spot + 1)
                        line = (edge_mine_ref[1, spot, lanes] + edge_core_ref[1, spot, lanes]) + edge_far_ref[spot, lanes]
                        value = jnp.where(sub == at, line, value)
                    return value

                inverse = 144.0 / jnp.maximum(144.0 * total(0), 1.0)
                means = [total(1 + first) * inverse * scales[first] for first in range(FEATURES)]
                mean_ref[rows, lanes] = means[0]
                entry = 0
                for first in range(FEATURES):
                    for second in range(first, FEATURES):
                        scale = scales[first] * scales[second]
                        covariance_ref[entry, rows, lanes] = (
                            total(5 + entry) * inverse * scale - means[first] * means[second]
                        )
                        entry += 1


def finish(pieces, cosine, mine, edge_mine, edge_core, edge_far, far, core):
    moments, row_block, width = mine.shape
    vmem = pl.BlockSpec(memory_space=pltpu.VMEM)
    entries = FEATURES * (FEATURES + 1) // 2
    return pl.pallas_call(
        functools.partial(finish_kernel, pieces),
        out_shape=(
            jax.ShapeDtypeStruct((row_block, width), F32),
            jax.ShapeDtypeStruct((entries, row_block, width), F32),
        ),
        in_specs=[vmem] * (5 + len(far) + len(core)),
        out_specs=(vmem, vmem),
        compiler_params=pltpu.CompilerParams(vmem_limit_bytes=VMEM_BYTES),
        cost_estimate=SMALL_COST,
        name="finish",
    )(cosine, mine, edge_mine, edge_core, edge_far, *far, *core)


def exchange(value, distance):
    count = lax.axis_size("acq")
    return lax.ppermute(value, "acq", [(source, source ^ distance) for source in range(count)])


def local(strips, strip_quality, valid_ranges):
    strip_count, row_block, col_count = strips.shape
    tile_count = lax.axis_size("tile")
    ranges = valid_ranges.T
    piece_rows = row_block // 2
    pieces = tuple(range(0, row_block, piece_rows))

    top, bottom, inner, cosine, limits = halo_rows(strip_quality, ranges, strips)
    forward = [(i, i + 1) for i in range(tile_count - 1)]
    backward = [(target, source) for source, target in forward]
    above = lax.ppermute(bottom, "tile", forward)
    below = lax.ppermute(top, "tile", backward)

    def compute(order, remote, first_row, row_count, count):
        return moments_of(strip_quality, ranges, cosine, strips, order, remote, first_row, row_count, count)

    mine, other, token = compute((top, top), True, pieces[0], piece_rows, 1)
    far = [exchange(mine + exchange(other, 1), 2)]
    edge_mine, edge_other, token = edge_moments(limits, cosine, above, top, inner, bottom, below, token)
    edge_core = exchange(edge_other, 1)
    edge_far = exchange(edge_mine[0] + edge_core[0], 2)
    mine, other, token = compute((token, token), True, pieces[1], piece_rows, 1)
    far.append(exchange(mine + exchange(other, 1), 2))
    mine, *other, token = compute((token, token), False, 0, row_block, 3)
    core = [exchange(piece, 1) for piece in other]
    return finish(pieces, cosine, mine, edge_mine, edge_core, edge_far, far, core)


def solution(mesh):
    return jax.shard_map(
        local,
        mesh=mesh,
        in_specs=(P("acq", "tile", None), P("acq"), P("acq", None)),
        out_specs=(P("tile", "acq"), P(None, "tile", "acq")),
        check_vma=False,
    )
```

```python
import functools
import jax
import jax.numpy as jnp
from jax import lax
from jax.experimental import pallas as pl
from jax.experimental.pallas import tpu as pltpu
from jax.sharding import PartitionSpec as P

MOMENTS = 15
FEATURES = 4
SUB = 8
LANES = 128
EDGE_ROWS = 4
VMEM_BYTES = 50 * 1024 * 1024
SMALL_VMEM_BYTES = 50 * 1024 * 1024
F32 = jnp.float32
LOAD_PARTS = 4
PIECES = 3
SMALL_COST = pl.CostEstimate(flops=1, bytes_accessed=1, transcendentals=0)


def moment_terms(z, slope_x, second_x, rows, inverse_square, mask):
    row_m2, row_m1, row_p1, row_p2 = rows
    slope_y = 8.0 * (row_p1 - row_m1) - (row_p2 - row_m2)
    second_y = 16.0 * (row_p1 + row_m1) - (row_p2 + row_m2) - 30.0 * z
    curvature = second_x * inverse_square + second_y
    steepness = (144.0 + slope_y * slope_y) + slope_x * slope_x * inverse_square
    weight = mask / steepness
    features = (z, slope_x, slope_y, curvature)
    weighted = [weight * feature for feature in features]
    terms = [weight] + weighted
    for first in range(FEATURES):
        for second in range(first, FEATURES):
            terms.append(weighted[first] * features[second])
    return terms


def stencil_terms(z, rows, cols, inverse_square, mask):
    col_m2, col_m1, col_p1, col_p2 = cols
    slope_x = 8.0 * (col_p1 - col_m1) - (col_p2 - col_m2)
    second_x = 16.0 * (col_p1 + col_m1) - (col_p2 + col_m2) - 30.0 * z
    return moment_terms(z, slope_x, second_x, rows, inverse_square, mask)


def shifted_columns(z, left, right, lane):
    return (
        pltpu.roll(jnp.where(lane >= LANES - 2, left, z), 2, 1),
        pltpu.roll(jnp.where(lane == LANES - 1, left, z), 1, 1),
        pltpu.roll(jnp.where(lane == 0, right, z), LANES - 1, 1),
        pltpu.roll(jnp.where(lane < 2, right, z), LANES - 2, 1),
    )


def zero_terms():
    return tuple(jnp.zeros((SUB, LANES), F32) for _ in range(MOMENTS))


def halo_kernel(
    strips_ref, top_ref, bottom_ref, inner_ref, cosine_ref, token_ref, first_ref, last_ref, sems
):
    token_ref[...] = jnp.zeros((SUB, LANES), F32)
    strip_count, row_block, col_count = strips_ref.shape
    copies = []
    for tile in range(col_count // LANES):
        lanes = pl.ds(tile * LANES, LANES)
        for which, (start, target) in enumerate(((0, first_ref), (row_block - SUB, last_ref))):
            copies.append(
                pltpu.make_async_copy(
                    strips_ref.at[:, pl.ds(start, SUB), lanes], target.at[tile], sems.at[which, tile]
                )
            )
    for copy in copies:
        copy.start()
    total_rows = row_block * lax.axis_size("tile")
    row_start = lax.axis_index("tile") * row_block
    for tile in range(row_block // SUB):
        row = lax.broadcasted_iota(jnp.int32, (SUB, LANES), 0) + (row_start + tile * SUB)
        latitude = -1.0 + 2.0 * (row.astype(F32) + 0.5) / total_rows
        cosine_ref[tile * SUB:(tile + 1) * SUB, :] = jnp.cos(latitude)

    first_rows = first_ref.reshape(col_count // LANES, strip_count * SUB, LANES)
    last_rows = last_ref.reshape(col_count // LANES, strip_count * SUB, LANES)
    for tile in range(col_count // LANES):
        copies[2 * tile].wait()
        copies[2 * tile + 1].wait()
        lanes = slice(tile * LANES, (tile + 1) * LANES)
        for group in range(strip_count // SUB):
            strips = slice(group * SUB, (group + 1) * SUB)
            for row in range(2):
                at = group * SUB * SUB
                top_ref[row, strips, lanes] = first_rows[tile, pl.ds(at + row, SUB, stride=SUB), :]
                bottom_ref[row, strips, lanes] = last_rows[tile, pl.ds(at + 6 + row, SUB, stride=SUB), :]
                inner_ref[row, strips, lanes] = first_rows[tile, pl.ds(at + 2 + row, SUB, stride=SUB), :]
                inner_ref[2 + row, strips, lanes] = last_rows[tile, pl.ds(at + 4 + row, SUB, stride=SUB), :]


def halo_rows(strips):
    strip_count, row_block, col_count = strips.shape
    tiles = col_count // LANES
    pair = jax.ShapeDtypeStruct((2, strip_count, col_count), F32)
    inner = jax.ShapeDtypeStruct((4, strip_count, col_count), F32)
    cosine = jax.ShapeDtypeStruct((row_block, LANES), F32)
    vmem = pl.BlockSpec(memory_space=pltpu.VMEM)
    hbm = pl.BlockSpec(memory_space=pltpu.HBM)
    return pl.pallas_call(
        halo_kernel,
        out_shape=(pair, pair, inner, cosine, jax.ShapeDtypeStruct((SUB, LANES), F32)),
        in_specs=[hbm],
        out_specs=(vmem,) * 5,
        scratch_shapes=[
            pltpu.VMEM((tiles, strip_count, SUB, LANES), F32),
            pltpu.VMEM((tiles, strip_count, SUB, LANES), F32),
            pltpu.SemaphoreType.DMA((2, tiles)),
        ],
        compiler_params=pltpu.CompilerParams(vmem_limit_bytes=SMALL_VMEM_BYTES),
        cost_estimate=SMALL_COST,
        name="halo_rows",
    )(strips)


def column_weights():
    source = lax.broadcasted_iota(jnp.int32, (4 * LANES, 2 * LANES), 0)
    target = lax.broadcasted_iota(jnp.int32, (4 * LANES, 2 * LANES), 1)
    lane = source % LANES
    lane = jnp.where(source < 2 * LANES, lane, jnp.where(lane < LANES // 2, lane + LANES, lane - LANES))
    distance = lane - target % LANES
    near, far = jnp.abs(distance) == 1, jnp.abs(distance) == 2
    sign = jnp.where(distance > 0, 1.0, -1.0)
    slope = jnp.where(near, 8.0 * sign, jnp.where(far, -sign, 0.0))
    second = jnp.where(near, 16.0, jnp.where(far, -1.0, jnp.where(distance == 0, -30.0, 0.0)))
    return jnp.where(target < LANES, slope, second).astype(jnp.bfloat16)


def moment_kernel(*refs, remote, first_row, row_count, pieces, spread):
    if spread:
        small_sems = refs[-1]
        quality_ref, ranges_ref = refs[-3:-1]
        small_copies = [
            pltpu.make_async_copy(refs[kind], refs[kind - 3], small_sems.at[kind]) for kind in range(2)
        ]
        refs = refs[2:-3]
    else:
        limits_ref = refs[0]
        refs = refs[1:]
    cosine_ref, strips_ref, first_order_ref, second_order_ref, mine_ref = refs[:5]
    refs = refs[5:]
    other_refs, token_ref = refs[:pieces], refs[pieces]
    if spread:
        limits_ref = refs[pieces + 1]
        refs = refs[1:]
    elevation, high_part, low_part, row_mask, col_mask, weights, first_slot, second_slot, sems = refs[pieces + 1:]
    del first_order_ref, second_order_ref
    token_ref[...] = jnp.zeros((SUB, LANES), F32)
    strip_count, row_block, col_count = strips_ref.shape
    tiles = col_count // LANES
    half = tiles // 2
    quarter = half // 2
    position = lax.axis_index("acq")
    side = position // 2
    core = position % 2
    base = (1 - side if remote else side) * half
    row_start = lax.axis_index("tile") * row_block + first_row
    low = max(first_row - SUB, 0)
    high = min(first_row + row_count + SUB, row_block)
    offset = SUB - (first_row - low)

    part = strip_count // LOAD_PARTS

    def fetch(index, which):
        lanes = pl.ds(pl.multiple_of((base + index - 1) * LANES, LANES), LANES)
        strips = pl.ds(which * part, part)
        return pltpu.make_async_copy(
            strips_ref.at[strips, pl.ds(low, high - low), lanes],
            elevation.at[strips, index, pl.ds(offset, high - low), :],
            sems.at[index, which],
        )

    def present(index):
        return (base + index >= 1) & (base + index <= tiles)

    def start(index, which):
        @pl.when(present(index))
        def _():
            fetch(index, which).start()

    zero = jnp.zeros((SUB, LANES), F32)

    def blank(index):
        @pl.when(jnp.logical_not(present(index)))
        def _():
            def body(strip, carry):
                for row in range(1, row_count // SUB + 1):
                    elevation[strip, index, row * SUB:(row + 1) * SUB, :] = zero
                return carry

            lax.fori_loop(0, strip_count, body, 0)

    def arrive(index, which):
        @pl.when(present(index))
        def _():
            fetch(index, which).wait()

        def split(step, carry):
            strip = which * part + step
            value = elevation[strip, index, SUB:SUB + row_count, :]
            upper = value.astype(jnp.bfloat16)
            high_part[strip, index] = upper
            low_part[strip, index] = (value - upper.astype(F32)).astype(jnp.bfloat16)
            return carry

        lax.fori_loop(0, part, split, 0, unroll=4)

    initial = (1 - core) * quarter
    later = core * quarter
    final = later + 2 * core
    for which in range(LOAD_PARTS):
        for step in range(3):
            start(initial + step, which)
    if spread:
        for copy in small_copies:
            copy.start()
    blank(0)
    blank(half + 1)

    weights[...] = column_weights()

    def spread_out(strip, carry):
        here = pl.ds(strip, 1)
        for kind in range(4):
            value = ranges_ref[kind, strip].astype(F32)
            limits_ref[kind, here, :] = jnp.full((1, LANES), value, F32)
        limits_ref[4, here, :] = jnp.full((1, LANES), quality_ref[strip], F32)
        return carry

    if spread:
        for copy in small_copies:
            copy.wait()
        lax.fori_loop(0, strip_count, spread_out, 0)

    def prepare(strip, carry):
        row_low, row_high, col_low, col_high, quality = (
            limits_ref[kind, pl.ds(strip, 1), :] for kind in range(5)
        )
        for tile in range(row_count // SUB):
            row = (lax.broadcasted_iota(jnp.int32, (SUB, LANES), 0) + (row_start + tile * SUB)).astype(F32)
            row_mask[strip, tile * SUB:(tile + 1) * SUB, :] = jnp.where(
                (row >= row_low) & (row < row_high), quality, 0.0
            )
        for tile in range(half):
            col = (lax.broadcasted_iota(jnp.int32, (SUB, LANES), 1) + (base + tile) * LANES).astype(F32)
            col_mask[strip, tile] = jnp.where((col >= col_low) & (col < col_high), 1.0, 0.0)
        if low == first_row:
            for tile in range(half + 2):
                elevation[strip, tile, 0:SUB, :] = zero
        if high == first_row + row_count:
            for tile in range(half + 2):
                elevation[strip, tile, SUB + row_count:2 * SUB + row_count, :] = zero
        return carry

    lax.fori_loop(0, strip_count, prepare, 0)

    tile_rows = row_count // SUB
    share = strip_count // tile_rows
    slots = (first_slot, second_slot)

    def columns_into(slot, at, first, count):
        strips = pl.ds(first, count)
        lane = lax.broadcasted_iota(jnp.int32, (count * row_count, LANES), 1)

        def load(ref, tile):
            return ref[strips, tile].reshape(count * row_count, LANES)

        edges = [
            jnp.where(lane < LANES // 2, load(ref, at + 1), load(ref, at - 1))
            for ref in (high_part, low_part)
        ]
        left = jnp.concatenate([load(high_part, at), load(low_part, at)] + edges, axis=1)
        product = jnp.dot(left, weights[...], preferred_element_type=F32)
        slots[slot][strips] = product.reshape(count, row_count, 2 * LANES)

    def column_tile(slot, at, following, store, lanes):
        def row_tile(tile, carry):
            row = pl.multiple_of(tile * SUB, SUB)
            cosine = cosine_ref[pl.ds(first_row + row, SUB), :]
            inverse_square = 1.0 / (cosine * cosine)

            if following is not None:
                columns_into(1 - slot, following, tile * share, share)
            unroll = strip_count if following is not None else 16

            def add_strips(chunk, sums):
                for index in range(unroll):
                    strip = chunk * unroll + index

                    def load(shift):
                        return elevation[strip, at, pl.ds(SUB + row + shift, SUB), :]

                    slope_x = slots[slot][strip, pl.ds(row, SUB), :LANES]
                    second_x = slots[slot][strip, pl.ds(row, SUB), LANES:]
                    mask = row_mask[strip, pl.ds(row, SUB), :] * col_mask[strip, at - 1]
                    shifts = (load(-2), load(-1), load(1), load(2))
                    terms = moment_terms(load(0), slope_x, second_x, shifts, inverse_square, mask)
                    sums = [total + term for total, term in zip(sums, terms)]
                return tuple(sums)

            if following is not None:
                sums = add_strips(0, zero_terms())
            else:
                sums = lax.fori_loop(0, strip_count // unroll, add_strips, zero_terms())
            for moment in range(MOMENTS):
                store(moment, pl.ds(row, SUB), lanes, sums[moment])
            return carry

        lax.fori_loop(0, tile_rows, row_tile, 0)

    for which in range(LOAD_PARTS):
        start(initial + 3, which)
    for which in range(LOAD_PARTS):
        for step in range(2):
            start(final + step, which)

    def first_columns(which, carry):
        for step in range(3):
            arrive(initial + step, which)
        columns_into(0, initial + 1, which * part, part)
        return carry

    lax.fori_loop(0, LOAD_PARTS, first_columns, 0)

    def arrive_whole(index):
        def body(which, carry):
            arrive(index, which)
            return carry

        lax.fori_loop(0, LOAD_PARTS, body, 0)

    def store_other(moment, rows, lanes, value):
        share = MOMENTS // pieces
        other_refs[moment // share][moment % share, rows, lanes] = value

    def store_mine(moment, rows, lanes, value):
        mine_ref[moment, rows, lanes] = value

    arrive_whole(initial + 3)
    column_tile(0, initial + 1, initial + 2, store_other, slice(0, LANES))
    arrive_whole(final)
    arrive_whole(final + 1)
    column_tile(1, initial + 2, later + 1, store_other, slice(LANES, 2 * LANES))
    column_tile(0, later + 1, later + 2, store_mine, slice(0, LANES))
    column_tile(1, later + 2, None, store_mine, slice(LANES, 2 * LANES))


def moments_of(limits, cosine, strips, order, remote, first_row, row_count, pieces):
    spread = len(limits) == 2
    strip_count, row_block, col_count = strips.shape
    half = col_count // LANES // 2
    out = jax.ShapeDtypeStruct((MOMENTS, row_count, col_count // 4), F32)
    piece = jax.ShapeDtypeStruct((MOMENTS // pieces, row_count, col_count // 4), F32)
    token = jax.ShapeDtypeStruct((SUB, LANES), F32)
    vmem = pl.BlockSpec(memory_space=pltpu.VMEM)
    anywhere = pl.BlockSpec(memory_space=pl.ANY)
    lanes = jax.ShapeDtypeStruct((5, strip_count, LANES), F32)
    parts = pltpu.VMEM((strip_count, half + 2, row_count, LANES), jnp.bfloat16)
    slot = pltpu.VMEM((strip_count, row_count, 2 * LANES), F32)
    return pl.pallas_call(
        functools.partial(moment_kernel, remote=remote, first_row=first_row, row_count=row_count, pieces=pieces, spread=spread),
        out_shape=(out,) + (piece,) * pieces + (token,) + (lanes,) * spread,
        in_specs=[anywhere] * 2 * spread + [vmem] * (2 - spread) + [anywhere, vmem, vmem],
        out_specs=(vmem,) * (pieces + 2 + spread),
        scratch_shapes=[
            pltpu.VMEM((strip_count, half + 2, row_count + 2 * SUB, LANES), F32),
            parts,
            parts,
            pltpu.VMEM((strip_count, row_count, LANES), F32),
            pltpu.VMEM((strip_count, half, SUB, LANES), F32),
            pltpu.VMEM((4 * LANES, 2 * LANES), jnp.bfloat16),
            slot,
            slot,
            pltpu.SemaphoreType.DMA((half + 2, LOAD_PARTS)),
        ]
        + [
            pltpu.SMEM((strip_count,), F32),
            pltpu.SMEM((4, strip_count), jnp.int32),
            pltpu.SemaphoreType.DMA((2,)),
        ]
        * spread,
        compiler_params=pltpu.CompilerParams(vmem_limit_bytes=VMEM_BYTES),
        cost_estimate=SMALL_COST,
        name="moments_remote" if remote else "moments_own",
    )(*limits, cosine, strips, *order)


def edge_kernel(
    limits_ref, cosine_ref, above_ref, top_ref, inner_ref, bottom_ref, below_ref,
    first_order_ref, second_order_ref, mine_ref, other_ref, token_ref,
):
    del first_order_ref, second_order_ref
    token_ref[...] = jnp.zeros((SUB, LANES), F32)
    pair, strip_count, col_count = top_ref.shape
    row_block = cosine_ref.shape[0]
    tiles = col_count // LANES
    quarter = tiles // 4
    position = lax.axis_index("acq")
    side = position // 2
    core = position % 2
    row_start = lax.axis_index("tile") * row_block
    lane = lax.broadcasted_iota(jnp.int32, (SUB, LANES), 1)
    sources = [(above_ref, 0), (above_ref, 1), (top_ref, 0), (top_ref, 1), (inner_ref, 0), (inner_ref, 1)]
    sources += [(inner_ref, 2), (inner_ref, 3), (bottom_ref, 0), (bottom_ref, 1), (below_ref, 0), (below_ref, 1)]
    edges = ((0, 2), (1, 3), (row_block - 2, 8), (row_block - 1, 9))
    for out_ref, owner in ((mine_ref, core), (other_ref, 1 - core)):
        for part, owner_side in enumerate((1 - side, side)):
            out_ref[part, MOMENTS * EDGE_ROWS:, :] = jnp.zeros(
                (out_ref.shape[1] - MOMENTS * EDGE_ROWS, quarter * LANES), F32
            )

            def column_tile(tile, carry, out_ref=out_ref, part=part, first=(owner_side * 2 + owner) * quarter):
                at = first + tile
                left_keep = jnp.where(at > 0, 1.0, 0.0)
                right_keep = jnp.where(at < tiles - 1, 1.0, 0.0)
                here = pl.ds(pl.multiple_of(at * LANES, LANES), LANES)
                before = pl.ds(pl.multiple_of(jnp.maximum(at - 1, 0) * LANES, LANES), LANES)
                after = pl.ds(pl.multiple_of(jnp.minimum(at + 1, tiles - 1) * LANES, LANES), LANES)
                col = (lane + at * LANES).astype(F32)
                out_lanes = pl.ds(pl.multiple_of(tile * LANES, LANES), LANES)
                for edge, (row, source) in enumerate(edges):
                    cosine = cosine_ref[row:row + 1, :]
                    inverse_square = 1.0 / (cosine * cosine)
                    sums = zero_terms()
                    for group in range(strip_count // SUB):
                        strips = slice(group * SUB, (group + 1) * SUB)

                        def load(shift, where):
                            ref, index = sources[source + shift]
                            return ref[index, strips, where]

                        z = load(0, here)
                        cols = shifted_columns(
                            z, load(0, before) * left_keep, load(0, after) * right_keep, lane
                        )
                        limits = [limits_ref[kind, strips, :] for kind in range(4)]
                        at_row = (row_start + row).astype(F32)
                        inside = (limits[0] <= at_row) & (limits[1] > at_row)
                        inside = inside & (col >= limits[2]) & (col < limits[3])
                        mask = jnp.where(inside, limits_ref[4, strips, :], 0.0)
                        shifts = tuple(load(shift, here) for shift in (-2, -1, 1, 2))
                        terms = stencil_terms(z, shifts, cols, inverse_square, mask)
                        sums = [total + term for total, term in zip(sums, terms)]
                    for moment in range(MOMENTS):
                        spot = moment * EDGE_ROWS + edge
                        out_ref[part, spot:spot + 1, out_lanes] = jnp.sum(sums[moment], axis=0, keepdims=True)
                return carry

            lax.fori_loop(0, quarter, column_tile, 0)


def edge_moments(limits, cosine, above, top, inner, bottom, below, *order):
    pair, strip_count, col_count = top.shape
    out = jax.ShapeDtypeStruct((2, -(-MOMENTS * EDGE_ROWS // SUB) * SUB, col_count // 4), F32)
    vmem = pl.BlockSpec(memory_space=pltpu.VMEM)
    return pl.pallas_call(
        edge_kernel,
        out_shape=(out, out, jax.ShapeDtypeStruct((SUB, LANES), F32)),
        in_specs=[vmem] * 9,
        out_specs=(vmem, vmem, vmem),
        compiler_params=pltpu.CompilerParams(vmem_limit_bytes=SMALL_VMEM_BYTES),
        cost_estimate=SMALL_COST,
        name="moments_edge",
    )(limits, cosine, above, top, inner, bottom, below, *order)


def combine_kernel(mine_ref, *refs, pieces, edges):
    near_refs, rest = refs[:pieces], refs[pieces:]
    out_ref, token_ref = rest[-2:]
    token_ref[...] = jnp.zeros((SUB, LANES), F32)
    share, row_count, width = near_refs[0].shape
    for piece, near_ref in enumerate(near_refs):
        for moment in range(share):
            at = piece * share + moment
            out_ref[at * row_count:(at + 1) * row_count, :] = mine_ref[at] + near_ref[moment]
    if edges:
        edge_mine_ref, edge_core_ref = rest[:2]
        out_ref[pieces * share * row_count:, :] = edge_mine_ref[0] + edge_core_ref[0]


def combine(mine, near, edges, order):
    moments, row_count, width = mine.shape
    rows = moments * row_count + sum(edge.shape[1] for edge in edges[:1])
    vmem = pl.BlockSpec(memory_space=pltpu.VMEM)
    return pl.pallas_call(
        functools.partial(combine_kernel, pieces=len(near), edges=bool(edges)),
        out_shape=(jax.ShapeDtypeStruct((rows, width), F32), jax.ShapeDtypeStruct((SUB, LANES), F32)),
        in_specs=[vmem] * (1 + len(near) + len(edges) + len(order)),
        out_specs=(vmem, vmem),
        compiler_params=pltpu.CompilerParams(vmem_limit_bytes=SMALL_VMEM_BYTES),
        cost_estimate=SMALL_COST,
        name="combine",
    )(mine, *near, *edges, *order)


def finish_kernel(pieces, cosine_ref, mine_ref, edge_mine_ref, edge_core_ref, *refs):
    far_refs, core_refs = refs[:len(pieces)], refs[len(pieces):-2]
    mean_ref, covariance_ref = refs[-2:]
    row_block, width = mean_ref.shape
    share = MOMENTS // len(core_refs)
    sub = lax.broadcasted_iota(jnp.int32, (SUB, LANES), 0)
    piece_rows = row_block // len(pieces)
    edge_start = MOMENTS * piece_rows
    for first_row, far_ref in zip(pieces, far_refs):
        for tile_row in range(first_row, first_row + piece_rows, SUB):
            rows = slice(tile_row, tile_row + SUB)
            cosine = cosine_ref[rows, :]
            scales = (1.0, 1.0 / (12.0 * cosine), 1.0 / 12.0, 1.0 / 12.0)
            spots = {0: ((0, 0), (1, 1)), row_block - SUB: ((SUB - 2, 2), (SUB - 1, 3))}.get(tile_row, ())
            for tile in range(width // LANES):
                lanes = slice(tile * LANES, (tile + 1) * LANES)

                def total(moment):
                    near = core_refs[moment // share][moment % share, rows, lanes]
                    far_row = moment * piece_rows + tile_row - first_row
                    value = (mine_ref[moment, rows, lanes] + near) + far_ref[far_row:far_row + SUB, lanes]
                    for at, edge in spots:
                        spot = moment * EDGE_ROWS + edge
                        edge_far = far_refs[-1][edge_start + spot:edge_start + spot + 1, lanes]
                        spot = slice(spot, spot + 1)
                        line = (edge_mine_ref[1, spot, lanes] + edge_core_ref[1, spot, lanes]) + edge_far
                        value = jnp.where(sub == at, line, value)
                    return value

                inverse = 144.0 / jnp.maximum(144.0 * total(0), 1.0)
                means = [total(1 + first) * inverse * scales[first] for first in range(FEATURES)]
                mean_ref[rows, lanes] = means[0]
                entry = 0
                for first in range(FEATURES):
                    for second in range(first, FEATURES):
                        scale = scales[first] * scales[second]
                        covariance_ref[entry, rows, lanes] = (
                            total(5 + entry) * inverse * scale - means[first] * means[second]
                        )
                        entry += 1


def finish(pieces, cosine, mine, edge_mine, edge_core, far, core):
    moments, row_block, width = mine.shape
    vmem = pl.BlockSpec(memory_space=pltpu.VMEM)
    entries = FEATURES * (FEATURES + 1) // 2
    return pl.pallas_call(
        functools.partial(finish_kernel, pieces),
        out_shape=(
            jax.ShapeDtypeStruct((row_block, width), F32),
            jax.ShapeDtypeStruct((entries, row_block, width), F32),
        ),
        in_specs=[vmem] * (4 + len(far) + len(core)),
        out_specs=(vmem, vmem),
        compiler_params=pltpu.CompilerParams(vmem_limit_bytes=SMALL_VMEM_BYTES),
        cost_estimate=SMALL_COST,
        name="finish",
    )(cosine, mine, edge_mine, edge_core, *far, *core)


def exchange(value, distance):
    count = lax.axis_size("acq")
    return lax.ppermute(value, "acq", [(source, source ^ distance) for source in range(count)])


def local(strips, strip_quality, valid_ranges):
    strip_count, row_block, col_count = strips.shape
    tile_count = lax.axis_size("tile")
    ranges = valid_ranges.T
    piece_rows = row_block // 2
    pieces = tuple(range(0, row_block, piece_rows))

    top, bottom, inner, cosine, token = halo_rows(strips)
    forward = [(i, i + 1) for i in range(tile_count - 1)]
    backward = [(target, source) for source, target in forward]
    above = lax.ppermute(bottom, "tile", forward)
    below = lax.ppermute(top, "tile", backward)

    def compute(order, remote, first_row, row_count, source):
        return moments_of(source, cosine, strips, order, remote, first_row, row_count, PIECES)

    def swap(parts):
        return [exchange(part, 1) for part in parts]

    mine, *other, token, limits = compute((token, token), True, pieces[0], piece_rows, (strip_quality, ranges))
    payload, token = combine(mine, swap(other), (), (above, below))
    far = [exchange(payload, 2)]
    mine, *other, token = compute((token, token), True, pieces[1], piece_rows, (limits,))
    near = swap(other)
    edge_mine, edge_other, token = edge_moments(limits, cosine, above, top, inner, bottom, below, token, far[0])
    edge_core = exchange(edge_other, 1)
    payload, token = combine(mine, near, (edge_mine, edge_core), (token,))
    far.append(exchange(payload, 2))
    mine, *other, token = compute((token, token), False, 0, row_block, (limits,))
    return finish(pieces, cosine, mine, edge_mine, edge_core, far, swap(other))


def solution(mesh):
    return jax.shard_map(
        local,
        mesh=mesh,
        in_specs=(P("acq", "tile", None), P("acq"), P("acq", None)),
        out_specs=(P("tile", "acq"), P(None, "tile", "acq")),
        check_vma=False,
    )
```

```python
import functools
import jax
import jax.numpy as jnp
from jax import lax
from jax.experimental import pallas as pl
from jax.experimental.pallas import tpu as pltpu
from jax.sharding import PartitionSpec as P

MOMENTS = 15
FEATURES = 4
SUB = 8
LANES = 128
EDGE_ROWS = 4
VMEM_BYTES = 50 * 1024 * 1024
SMALL_VMEM_BYTES = 50 * 1024 * 1024
F32 = jnp.float32
LOAD_PARTS = 4
PIECES = 3
SMALL_COST = pl.CostEstimate(flops=1, bytes_accessed=1, transcendentals=0)


def moment_terms(z, slope_x, second_x, rows, inverse_square, mask):
    row_m2, row_m1, row_p1, row_p2 = rows
    slope_y = 8.0 * (row_p1 - row_m1) - (row_p2 - row_m2)
    second_y = 16.0 * (row_p1 + row_m1) - (row_p2 + row_m2) - 30.0 * z
    curvature = second_x * inverse_square + second_y
    steepness = (144.0 + slope_y * slope_y) + slope_x * slope_x * inverse_square
    weight = mask / steepness
    features = (z, slope_x, slope_y, curvature)
    weighted = [weight * feature for feature in features]
    terms = [weight] + weighted
    for first in range(FEATURES):
        for second in range(first, FEATURES):
            terms.append(weighted[first] * features[second])
    return terms


def stencil_terms(z, rows, cols, inverse_square, mask):
    col_m2, col_m1, col_p1, col_p2 = cols
    slope_x = 8.0 * (col_p1 - col_m1) - (col_p2 - col_m2)
    second_x = 16.0 * (col_p1 + col_m1) - (col_p2 + col_m2) - 30.0 * z
    return moment_terms(z, slope_x, second_x, rows, inverse_square, mask)


def shifted_columns(z, left, right, lane):
    return (
        pltpu.roll(jnp.where(lane >= LANES - 2, left, z), 2, 1),
        pltpu.roll(jnp.where(lane == LANES - 1, left, z), 1, 1),
        pltpu.roll(jnp.where(lane == 0, right, z), LANES - 1, 1),
        pltpu.roll(jnp.where(lane < 2, right, z), LANES - 2, 1),
    )


def zero_terms():
    return tuple(jnp.zeros((SUB, LANES), F32) for _ in range(MOMENTS))


def halo_kernel(
    strips_ref, top_ref, bottom_ref, inner_ref, cosine_ref, token_ref, first_ref, last_ref, sems
):
    token_ref[...] = jnp.zeros((SUB, LANES), F32)
    strip_count, row_block, col_count = strips_ref.shape
    copies = []
    for tile in range(col_count // LANES):
        lanes = pl.ds(tile * LANES, LANES)
        for which, (start, target) in enumerate(((0, first_ref), (row_block - SUB, last_ref))):
            copies.append(
                pltpu.make_async_copy(
                    strips_ref.at[:, pl.ds(start, SUB), lanes], target.at[tile], sems.at[which, tile]
                )
            )
    for copy in copies:
        copy.start()
    total_rows = row_block * lax.axis_size("tile")
    row_start = lax.axis_index("tile") * row_block
    for tile in range(row_block // SUB):
        row = lax.broadcasted_iota(jnp.int32, (SUB, LANES), 0) + (row_start + tile * SUB)
        latitude = -1.0 + 2.0 * (row.astype(F32) + 0.5) / total_rows
        cosine_ref[tile * SUB:(tile + 1) * SUB, :] = jnp.cos(latitude)

    first_rows = first_ref.reshape(col_count // LANES, strip_count * SUB, LANES)
    last_rows = last_ref.reshape(col_count // LANES, strip_count * SUB, LANES)
    for tile in range(col_count // LANES):
        copies[2 * tile].wait()
        copies[2 * tile + 1].wait()
        lanes = slice(tile * LANES, (tile + 1) * LANES)
        for group in range(strip_count // SUB):
            strips = slice(group * SUB, (group + 1) * SUB)
            for row in range(2):
                at = group * SUB * SUB
                top_ref[row, strips, lanes] = first_rows[tile, pl.ds(at + row, SUB, stride=SUB), :]
                bottom_ref[row, strips, lanes] = last_rows[tile, pl.ds(at + 6 + row, SUB, stride=SUB), :]
                inner_ref[row, strips, lanes] = first_rows[tile, pl.ds(at + 2 + row, SUB, stride=SUB), :]
                inner_ref[2 + row, strips, lanes] = last_rows[tile, pl.ds(at + 4 + row, SUB, stride=SUB), :]


def halo_rows(strips):
    strip_count, row_block, col_count = strips.shape
    tiles = col_count // LANES
    pair = jax.ShapeDtypeStruct((2, strip_count, col_count), F32)
    inner = jax.ShapeDtypeStruct((4, strip_count, col_count), F32)
    cosine = jax.ShapeDtypeStruct((row_block, LANES), F32)
    vmem = pl.BlockSpec(memory_space=pltpu.VMEM)
    hbm = pl.BlockSpec(memory_space=pltpu.HBM)
    return pl.pallas_call(
        halo_kernel,
        out_shape=(pair, pair, inner, cosine, jax.ShapeDtypeStruct((SUB, LANES), F32)),
        in_specs=[hbm],
        out_specs=(vmem,) * 5,
        scratch_shapes=[
            pltpu.VMEM((tiles, strip_count, SUB, LANES), F32),
            pltpu.VMEM((tiles, strip_count, SUB, LANES), F32),
            pltpu.SemaphoreType.DMA((2, tiles)),
        ],
        compiler_params=pltpu.CompilerParams(vmem_limit_bytes=SMALL_VMEM_BYTES),
        cost_estimate=SMALL_COST,
        name="halo_rows",
    )(strips)


def column_weights():
    source = lax.broadcasted_iota(jnp.int32, (4 * LANES, 2 * LANES), 0)
    target = lax.broadcasted_iota(jnp.int32, (4 * LANES, 2 * LANES), 1)
    lane = source % LANES
    lane = jnp.where(source < 2 * LANES, lane, jnp.where(lane < LANES // 2, lane + LANES, lane - LANES))
    distance = lane - target % LANES
    near, far = jnp.abs(distance) == 1, jnp.abs(distance) == 2
    sign = jnp.where(distance > 0, 1.0, -1.0)
    slope = jnp.where(near, 8.0 * sign, jnp.where(far, -sign, 0.0))
    second = jnp.where(near, 16.0, jnp.where(far, -1.0, jnp.where(distance == 0, -30.0, 0.0)))
    return jnp.where(target < LANES, slope, second).astype(jnp.bfloat16)


def moment_kernel(*refs, remote, first_row, row_count, pieces, spread):
    if spread:
        small_sems = refs[-1]
        quality_ref, ranges_ref = refs[-3:-1]
        small_copies = [
            pltpu.make_async_copy(refs[kind], refs[kind - 3], small_sems.at[kind]) for kind in range(2)
        ]
        refs = refs[2:-3]
    else:
        limits_ref = refs[0]
        refs = refs[1:]
    cosine_ref, strips_ref, first_order_ref, second_order_ref, mine_ref = refs[:5]
    refs = refs[5:]
    other_refs, token_ref = refs[:pieces], refs[pieces]
    if spread:
        limits_ref = refs[pieces + 1]
        refs = refs[1:]
    elevation, high_part, low_part, row_mask, col_mask, weights, first_slot, second_slot, sems = refs[pieces + 1:]
    del first_order_ref, second_order_ref
    token_ref[...] = jnp.zeros((SUB, LANES), F32)
    strip_count, row_block, col_count = strips_ref.shape
    tiles = col_count // LANES
    half = tiles // 2
    quarter = half // 2
    position = lax.axis_index("acq")
    side = position // 2
    core = position % 2
    base = (1 - side if remote else side) * half
    row_start = lax.axis_index("tile") * row_block + first_row
    low = max(first_row - SUB, 0)
    high = min(first_row + row_count + SUB, row_block)
    offset = SUB - (first_row - low)

    part = strip_count // LOAD_PARTS

    def fetch(index, which):
        lanes = pl.ds(pl.multiple_of((base + index - 1) * LANES, LANES), LANES)
        strips = pl.ds(which * part, part)
        return pltpu.make_async_copy(
            strips_ref.at[strips, pl.ds(low, high - low), lanes],
            elevation.at[strips, index, pl.ds(offset, high - low), :],
            sems.at[index, which],
        )

    def present(index):
        return (base + index >= 1) & (base + index <= tiles)

    def start(index, which):
        @pl.when(present(index))
        def _():
            fetch(index, which).start()

    zero = jnp.zeros((SUB, LANES), F32)

    def blank(index):
        @pl.when(jnp.logical_not(present(index)))
        def _():
            def body(strip, carry):
                for row in range(1, row_count // SUB + 1):
                    elevation[strip, index, row * SUB:(row + 1) * SUB, :] = zero
                return carry

            lax.fori_loop(0, strip_count, body, 0)

    def arrive(index, which):
        @pl.when(present(index))
        def _():
            fetch(index, which).wait()

        def split(step, carry):
            strip = which * part + step
            value = elevation[strip, index, SUB:SUB + row_count, :]
            upper = value.astype(jnp.bfloat16)
            high_part[strip, index] = upper
            low_part[strip, index] = (value - upper.astype(F32)).astype(jnp.bfloat16)
            return carry

        lax.fori_loop(0, part, split, 0, unroll=4)

    initial = (1 - core) * quarter
    later = core * quarter
    final = later + 2 * core
    for which in range(LOAD_PARTS):
        for step in range(3):
            start(initial + step, which)
    if spread:
        for copy in small_copies:
            copy.start()
    blank(0)
    blank(half + 1)

    weights[...] = column_weights()

    def spread_out(strip, carry):
        here = pl.ds(strip, 1)
        for kind in range(4):
            value = ranges_ref[kind, strip].astype(F32)
            limits_ref[kind, here, :] = jnp.full((1, LANES), value, F32)
        limits_ref[4, here, :] = jnp.full((1, LANES), quality_ref[strip], F32)
        return carry

    if spread:
        for copy in small_copies:
            copy.wait()
        lax.fori_loop(0, strip_count, spread_out, 0)

    def prepare(strip, carry):
        row_low, row_high, col_low, col_high, quality = (
            limits_ref[kind, pl.ds(strip, 1), :] for kind in range(5)
        )
        for tile in range(row_count // SUB):
            row = (lax.broadcasted_iota(jnp.int32, (SUB, LANES), 0) + (row_start + tile * SUB)).astype(F32)
            row_mask[strip, tile * SUB:(tile + 1) * SUB, :] = jnp.where(
                (row >= row_low) & (row < row_high), quality, 0.0
            )
        for tile in range(half):
            col = (lax.broadcasted_iota(jnp.int32, (SUB, LANES), 1) + (base + tile) * LANES).astype(F32)
            col_mask[strip, tile] = jnp.where((col >= col_low) & (col < col_high), 1.0, 0.0)
        if low == first_row:
            for tile in range(half + 2):
                elevation[strip, tile, 0:SUB, :] = zero
        if high == first_row + row_count:
            for tile in range(half + 2):
                elevation[strip, tile, SUB + row_count:2 * SUB + row_count, :] = zero
        return carry

    lax.fori_loop(0, strip_count, prepare, 0)

    tile_rows = row_count // SUB
    share = strip_count // tile_rows
    slots = (first_slot, second_slot)

    def columns_into(slot, at, first, count):
        strips = pl.ds(first, count)
        lane = lax.broadcasted_iota(jnp.int32, (count * row_count, LANES), 1)

        def load(ref, tile):
            return ref[strips, tile].reshape(count * row_count, LANES)

        edges = [
            jnp.where(lane < LANES // 2, load(ref, at + 1), load(ref, at - 1))
            for ref in (high_part, low_part)
        ]
        left = jnp.concatenate([load(high_part, at), load(low_part, at)] + edges, axis=1)
        product = jnp.dot(left, weights[...], preferred_element_type=F32)
        slots[slot][strips] = product.reshape(count, row_count, 2 * LANES)

    def column_tile(slot, at, following, store, lanes):
        def row_tile(tile, carry):
            row = pl.multiple_of(tile * SUB, SUB)
            cosine = cosine_ref[pl.ds(first_row + row, SUB), :]
            inverse_square = 1.0 / (cosine * cosine)

            if following is not None:
                columns_into(1 - slot, following, tile * share, share)
            unroll = strip_count if following is not None else 16

            def add_strips(chunk, sums):
                for index in range(unroll):
                    strip = chunk * unroll + index

                    def load(shift):
                        return elevation[strip, at, pl.ds(SUB + row + shift, SUB), :]

                    slope_x = slots[slot][strip, pl.ds(row, SUB), :LANES]
                    second_x = slots[slot][strip, pl.ds(row, SUB), LANES:]
                    mask = row_mask[strip, pl.ds(row, SUB), :] * col_mask[strip, at - 1]
                    shifts = (load(-2), load(-1), load(1), load(2))
                    terms = moment_terms(load(0), slope_x, second_x, shifts, inverse_square, mask)
                    sums = [total + term for total, term in zip(sums, terms)]
                return tuple(sums)

            if following is not None:
                sums = add_strips(0, zero_terms())
            else:
                sums = lax.fori_loop(0, strip_count // unroll, add_strips, zero_terms())
            for moment in range(MOMENTS):
                store(moment, pl.ds(row, SUB), lanes, sums[moment])
            return carry

        lax.fori_loop(0, tile_rows, row_tile, 0)

    for which in range(LOAD_PARTS):
        start(initial + 3, which)
    for which in range(LOAD_PARTS):
        for step in range(2):
            start(final + step, which)

    def first_columns(which, carry):
        for step in range(3):
            arrive(initial + step, which)
        columns_into(0, initial + 1, which * part, part)
        return carry

    lax.fori_loop(0, LOAD_PARTS, first_columns, 0)

    def arrive_whole(index):
        def body(which, carry):
            arrive(index, which)
            return carry

        lax.fori_loop(0, LOAD_PARTS, body, 0)

    def store_other(moment, rows, lanes, value):
        share = MOMENTS // pieces
        other_refs[moment // share][moment % share, rows, lanes] = value

    def store_mine(moment, rows, lanes, value):
        mine_ref[moment, rows, lanes] = value

    arrive_whole(initial + 3)
    column_tile(0, initial + 1, initial + 2, store_other, slice(0, LANES))
    arrive_whole(final)
    arrive_whole(final + 1)
    column_tile(1, initial + 2, later + 1, store_other, slice(LANES, 2 * LANES))
    column_tile(0, later + 1, later + 2, store_mine, slice(0, LANES))
    column_tile(1, later + 2, None, store_mine, slice(LANES, 2 * LANES))


def moments_of(limits, cosine, strips, order, remote, first_row, row_count, pieces):
    spread = len(limits) == 2
    strip_count, row_block, col_count = strips.shape
    half = col_count // LANES // 2
    out = jax.ShapeDtypeStruct((MOMENTS, row_count, col_count // 4), F32)
    piece = jax.ShapeDtypeStruct((MOMENTS // pieces, row_count, col_count // 4), F32)
    token = jax.ShapeDtypeStruct((SUB, LANES), F32)
    vmem = pl.BlockSpec(memory_space=pltpu.VMEM)
    anywhere = pl.BlockSpec(memory_space=pl.ANY)
    lanes = jax.ShapeDtypeStruct((5, strip_count, LANES), F32)
    parts = pltpu.VMEM((strip_count, half + 2, row_count, LANES), jnp.bfloat16)
    slot = pltpu.VMEM((strip_count, row_count, 2 * LANES), F32)
    return pl.pallas_call(
        functools.partial(moment_kernel, remote=remote, first_row=first_row, row_count=row_count, pieces=pieces, spread=spread),
        out_shape=(out,) + (piece,) * pieces + (token,) + (lanes,) * spread,
        in_specs=[anywhere] * 2 * spread + [vmem] * (2 - spread) + [anywhere, vmem, vmem],
        out_specs=(vmem,) * (pieces + 2 + spread),
        scratch_shapes=[
            pltpu.VMEM((strip_count, half + 2, row_count + 2 * SUB, LANES), F32),
            parts,
            parts,
            pltpu.VMEM((strip_count, row_count, LANES), F32),
            pltpu.VMEM((strip_count, half, SUB, LANES), F32),
            pltpu.VMEM((4 * LANES, 2 * LANES), jnp.bfloat16),
            slot,
            slot,
            pltpu.SemaphoreType.DMA((half + 2, LOAD_PARTS)),
        ]
        + [
            pltpu.SMEM((strip_count,), F32),
            pltpu.SMEM((4, strip_count), jnp.int32),
            pltpu.SemaphoreType.DMA((2,)),
        ]
        * spread,
        compiler_params=pltpu.CompilerParams(vmem_limit_bytes=VMEM_BYTES),
        cost_estimate=SMALL_COST,
        name="moments_remote" if remote else "moments_own",
    )(*limits, cosine, strips, *order)


def edge_kernel(
    limits_ref, cosine_ref, above_ref, top_ref, inner_ref, bottom_ref, below_ref,
    first_order_ref, second_order_ref, mine_ref, other_ref, token_ref,
):
    del first_order_ref, second_order_ref
    token_ref[...] = jnp.zeros((SUB, LANES), F32)
    pair, strip_count, col_count = top_ref.shape
    row_block = cosine_ref.shape[0]
    tiles = col_count // LANES
    quarter = tiles // 4
    position = lax.axis_index("acq")
    side = position // 2
    core = position % 2
    row_start = lax.axis_index("tile") * row_block
    lane = lax.broadcasted_iota(jnp.int32, (SUB, LANES), 1)
    sources = [(above_ref, 0), (above_ref, 1), (top_ref, 0), (top_ref, 1), (inner_ref, 0), (inner_ref, 1)]
    sources += [(inner_ref, 2), (inner_ref, 3), (bottom_ref, 0), (bottom_ref, 1), (below_ref, 0), (below_ref, 1)]
    edges = ((0, 2), (1, 3), (row_block - 2, 8), (row_block - 1, 9))
    for out_ref, owner in ((mine_ref, core), (other_ref, 1 - core)):
        for part, owner_side in enumerate((1 - side, side)):
            out_ref[part, MOMENTS * EDGE_ROWS:, :] = jnp.zeros(
                (out_ref.shape[1] - MOMENTS * EDGE_ROWS, quarter * LANES), F32
            )

            def column_tile(tile, carry, out_ref=out_ref, part=part, first=(owner_side * 2 + owner) * quarter):
                at = first + tile
                left_keep = jnp.where(at > 0, 1.0, 0.0)
                right_keep = jnp.where(at < tiles - 1, 1.0, 0.0)
                here = pl.ds(pl.multiple_of(at * LANES, LANES), LANES)
                before = pl.ds(pl.multiple_of(jnp.maximum(at - 1, 0) * LANES, LANES), LANES)
                after = pl.ds(pl.multiple_of(jnp.minimum(at + 1, tiles - 1) * LANES, LANES), LANES)
                col = (lane + at * LANES).astype(F32)
                out_lanes = pl.ds(pl.multiple_of(tile * LANES, LANES), LANES)
                for edge, (row, source) in enumerate(edges):
                    cosine = cosine_ref[row:row + 1, :]
                    inverse_square = 1.0 / (cosine * cosine)
                    sums = zero_terms()
                    for group in range(strip_count // SUB):
                        strips = slice(group * SUB, (group + 1) * SUB)

                        def load(shift, where):
                            ref, index = sources[source + shift]
                            return ref[index, strips, where]

                        z = load(0, here)
                        cols = shifted_columns(
                            z, load(0, before) * left_keep, load(0, after) * right_keep, lane
                        )
                        limits = [limits_ref[kind, strips, :] for kind in range(4)]
                        at_row = (row_start + row).astype(F32)
                        inside = (limits[0] <= at_row) & (limits[1] > at_row)
                        inside = inside & (col >= limits[2]) & (col < limits[3])
                        mask = jnp.where(inside, limits_ref[4, strips, :], 0.0)
                        shifts = tuple(load(shift, here) for shift in (-2, -1, 1, 2))
                        terms = stencil_terms(z, shifts, cols, inverse_square, mask)
                        sums = [total + term for total, term in zip(sums, terms)]
                    for moment in range(MOMENTS):
                        spot = moment * EDGE_ROWS + edge
                        out_ref[part, spot:spot + 1, out_lanes] = jnp.sum(sums[moment], axis=0, keepdims=True)
                return carry

            lax.fori_loop(0, quarter, column_tile, 0)


def edge_moments(limits, cosine, above, top, inner, bottom, below, *order):
    pair, strip_count, col_count = top.shape
    out = jax.ShapeDtypeStruct((2, -(-MOMENTS * EDGE_ROWS // SUB) * SUB, col_count // 4), F32)
    vmem = pl.BlockSpec(memory_space=pltpu.VMEM)
    return pl.pallas_call(
        edge_kernel,
        out_shape=(out, out, jax.ShapeDtypeStruct((SUB, LANES), F32)),
        in_specs=[vmem] * 9,
        out_specs=(vmem, vmem, vmem),
        compiler_params=pltpu.CompilerParams(vmem_limit_bytes=SMALL_VMEM_BYTES),
        cost_estimate=SMALL_COST,
        name="moments_edge",
    )(limits, cosine, above, top, inner, bottom, below, *order)


def combine_kernel(mine_ref, *refs, pieces, edges):
    near_refs, rest = refs[:pieces], refs[pieces:]
    out_ref, token_ref = rest[-2:]
    token_ref[...] = jnp.zeros((SUB, LANES), F32)
    share, row_count, width = near_refs[0].shape
    for piece, near_ref in enumerate(near_refs):
        for moment in range(share):
            at = piece * share + moment
            out_ref[at * row_count:(at + 1) * row_count, :] = mine_ref[at] + near_ref[moment]
    if edges:
        edge_mine_ref, edge_core_ref = rest[:2]
        out_ref[pieces * share * row_count:, :] = edge_mine_ref[0] + edge_core_ref[0]


def combine(mine, near, edges, order):
    moments, row_count, width = mine.shape
    rows = moments * row_count + sum(edge.shape[1] for edge in edges[:1])
    vmem = pl.BlockSpec(memory_space=pltpu.VMEM)
    return pl.pallas_call(
        functools.partial(combine_kernel, pieces=len(near), edges=bool(edges)),
        out_shape=(jax.ShapeDtypeStruct((rows, width), F32), jax.ShapeDtypeStruct((SUB, LANES), F32)),
        in_specs=[vmem] * (1 + len(near) + len(edges) + len(order)),
        out_specs=(vmem, vmem),
        compiler_params=pltpu.CompilerParams(vmem_limit_bytes=SMALL_VMEM_BYTES),
        cost_estimate=SMALL_COST,
        name="combine",
    )(mine, *near, *edges, *order)


def finish_kernel(pieces, cosine_ref, mine_ref, edge_mine_ref, edge_core_ref, *refs):
    far_refs, core_refs = refs[:len(pieces)], refs[len(pieces):-2]
    mean_ref, covariance_ref = refs[-2:]
    row_block, width = mean_ref.shape
    share = MOMENTS // len(core_refs)
    sub = lax.broadcasted_iota(jnp.int32, (SUB, LANES), 0)
    piece_rows = row_block // len(pieces)
    edge_start = MOMENTS * piece_rows
    for first_row, far_ref in zip(pieces, far_refs):
        for tile_row in range(first_row, first_row + piece_rows, SUB):
            rows = slice(tile_row, tile_row + SUB)
            cosine = cosine_ref[rows, :]
            scales = (1.0, 1.0 / (12.0 * cosine), 1.0 / 12.0, 1.0 / 12.0)
            spots = {0: ((0, 0), (1, 1)), row_block - SUB: ((SUB - 2, 2), (SUB - 1, 3))}.get(tile_row, ())
            for tile in range(width // LANES):
                lanes = slice(tile * LANES, (tile + 1) * LANES)

                def total(moment):
                    near = core_refs[moment // share][moment % share, rows, lanes]
                    far_row = moment * piece_rows + tile_row - first_row
                    value = (mine_ref[moment, rows, lanes] + near) + far_ref[far_row:far_row + SUB, lanes]
                    for at, edge in spots:
                        spot = moment * EDGE_ROWS + edge
                        edge_far = far_refs[-1][edge_start + spot:edge_start + spot + 1, lanes]
                        spot = slice(spot, spot + 1)
                        line = (edge_mine_ref[1, spot, lanes] + edge_core_ref[1, spot, lanes]) + edge_far
                        value = jnp.where(sub == at, line, value)
                    return value

                inverse = 144.0 / jnp.maximum(144.0 * total(0), 1.0)
                means = [total(1 + first) * inverse * scales[first] for first in range(FEATURES)]
                mean_ref[rows, lanes] = means[0]
                entry = 0
                for first in range(FEATURES):
                    for second in range(first, FEATURES):
                        scale = scales[first] * scales[second]
                        covariance_ref[entry, rows, lanes] = (
                            total(5 + entry) * inverse * scale - means[first] * means[second]
                        )
                        entry += 1


def finish(pieces, cosine, mine, edge_mine, edge_core, far, core):
    moments, row_block, width = mine.shape
    vmem = pl.BlockSpec(memory_space=pltpu.VMEM)
    entries = FEATURES * (FEATURES + 1) // 2
    return pl.pallas_call(
        functools.partial(finish_kernel, pieces),
        out_shape=(
            jax.ShapeDtypeStruct((row_block, width), F32),
            jax.ShapeDtypeStruct((entries, row_block, width), F32),
        ),
        in_specs=[vmem] * (4 + len(far) + len(core)),
        out_specs=(vmem, vmem),
        compiler_params=pltpu.CompilerParams(vmem_limit_bytes=SMALL_VMEM_BYTES),
        cost_estimate=SMALL_COST,
        name="finish",
    )(cosine, mine, edge_mine, edge_core, *far, *core)


def exchange(value, distance):
    count = lax.axis_size("acq")
    return lax.ppermute(value, "acq", [(source, source ^ distance) for source in range(count)])


def local(strips, strip_quality, valid_ranges):
    strip_count, row_block, col_count = strips.shape
    tile_count = lax.axis_size("tile")
    ranges = valid_ranges.T

    top, bottom, inner, cosine, token = halo_rows(strips)
    forward = [(i, i + 1) for i in range(tile_count - 1)]
    backward = [(target, source) for source, target in forward]
    above = lax.ppermute(bottom, "tile", forward)
    below = lax.ppermute(top, "tile", backward)

    def compute(order, remote, first_row, row_count, source):
        return moments_of(source, cosine, strips, order, remote, first_row, row_count, PIECES)

    def swap(parts):
        return [exchange(part, 1) for part in parts]

    mine, *other, token, limits = compute((token, token), True, 0, row_block, (strip_quality, ranges))
    near = swap(other)
    edge_mine, edge_other, token = edge_moments(limits, cosine, above, top, inner, bottom, below, token, token)
    edge_core = exchange(edge_other, 1)
    payload, token = combine(mine, near, (edge_mine, edge_core), (token,))
    far = exchange(payload, 2)
    mine, *other, token = compute((token, token), False, 0, row_block, (limits,))
    return finish((0,), cosine, mine, edge_mine, edge_core, [far], swap(other))


def solution(mesh):
    return jax.shard_map(
        local,
        mesh=mesh,
        in_specs=(P("acq", "tile", None), P("acq"), P("acq", None)),
        out_specs=(P("tile", "acq"), P(None, "tile", "acq")),
        check_vma=False,
    )
```

```python
import functools
import jax
import jax.numpy as jnp
from jax import lax
from jax.experimental import pallas as pl
from jax.experimental.pallas import tpu as pltpu
from jax.sharding import PartitionSpec as P

MOMENTS = 14
FEATURES = 4
SUB = 8
LANES = 128
EDGE_ROWS = 4
VMEM_BYTES = 50 * 1024 * 1024
SMALL_VMEM_BYTES = 50 * 1024 * 1024
F32 = jnp.float32
LOAD_PARTS = 4
PIECES = 2
SMALL_COST = pl.CostEstimate(flops=1, bytes_accessed=1, transcendentals=0)


def moment_terms(z, slope_x, second_x, rows, inverse_square, mask):
    row_m2, row_m1, row_p1, row_p2 = rows
    slope_y = 8.0 * (row_p1 - row_m1) - (row_p2 - row_m2)
    second_y = 16.0 * (row_p1 + row_m1) - (row_p2 + row_m2) - 30.0 * z
    curvature = second_x * inverse_square + second_y
    steepness = (144.0 + slope_y * slope_y) + slope_x * slope_x * inverse_square
    weight = mask / steepness
    features = (z, slope_x, slope_y, curvature)
    weighted = [weight * feature for feature in features]
    terms = list(weighted)
    for first in range(FEATURES):
        for second in range(first, FEATURES):
            terms.append(weighted[first] * features[second])
    return terms


def stencil_terms(z, rows, cols, inverse_square, mask):
    col_m2, col_m1, col_p1, col_p2 = cols
    slope_x = 8.0 * (col_p1 - col_m1) - (col_p2 - col_m2)
    second_x = 16.0 * (col_p1 + col_m1) - (col_p2 + col_m2) - 30.0 * z
    return moment_terms(z, slope_x, second_x, rows, inverse_square, mask)


def shifted_columns(z, left, right, lane):
    return (
        pltpu.roll(jnp.where(lane >= LANES - 2, left, z), 2, 1),
        pltpu.roll(jnp.where(lane == LANES - 1, left, z), 1, 1),
        pltpu.roll(jnp.where(lane == 0, right, z), LANES - 1, 1),
        pltpu.roll(jnp.where(lane < 2, right, z), LANES - 2, 1),
    )


def zero_terms():
    return tuple(jnp.zeros((SUB, LANES), F32) for _ in range(MOMENTS))


def halo_kernel(
    strips_ref, top_ref, bottom_ref, inner_ref, cosine_ref, token_ref, first_ref, last_ref, sems
):
    token_ref[...] = jnp.zeros((SUB, LANES), F32)
    strip_count, row_block, col_count = strips_ref.shape
    copies = []
    for tile in range(col_count // LANES):
        lanes = pl.ds(tile * LANES, LANES)
        for which, (start, target) in enumerate(((0, first_ref), (row_block - SUB, last_ref))):
            copies.append(
                pltpu.make_async_copy(
                    strips_ref.at[:, pl.ds(start, SUB), lanes], target.at[tile], sems.at[which, tile]
                )
            )
    for copy in copies:
        copy.start()
    total_rows = row_block * lax.axis_size("tile")
    row_start = lax.axis_index("tile") * row_block
    for tile in range(row_block // SUB):
        row = lax.broadcasted_iota(jnp.int32, (SUB, LANES), 0) + (row_start + tile * SUB)
        latitude = -1.0 + 2.0 * (row.astype(F32) + 0.5) / total_rows
        cosine_ref[tile * SUB:(tile + 1) * SUB, :] = jnp.cos(latitude)

    first_rows = first_ref.reshape(col_count // LANES, strip_count * SUB, LANES)
    last_rows = last_ref.reshape(col_count // LANES, strip_count * SUB, LANES)
    for tile in range(col_count // LANES):
        copies[2 * tile].wait()
        copies[2 * tile + 1].wait()
        lanes = slice(tile * LANES, (tile + 1) * LANES)
        for group in range(strip_count // SUB):
            strips = slice(group * SUB, (group + 1) * SUB)
            for row in range(2):
                at = group * SUB * SUB
                top_ref[row, strips, lanes] = first_rows[tile, pl.ds(at + row, SUB, stride=SUB), :]
                bottom_ref[row, strips, lanes] = last_rows[tile, pl.ds(at + 6 + row, SUB, stride=SUB), :]
                inner_ref[row, strips, lanes] = first_rows[tile, pl.ds(at + 2 + row, SUB, stride=SUB), :]
                inner_ref[2 + row, strips, lanes] = last_rows[tile, pl.ds(at + 4 + row, SUB, stride=SUB), :]


def halo_rows(strips):
    strip_count, row_block, col_count = strips.shape
    tiles = col_count // LANES
    pair = jax.ShapeDtypeStruct((2, strip_count, col_count), F32)
    inner = jax.ShapeDtypeStruct((4, strip_count, col_count), F32)
    cosine = jax.ShapeDtypeStruct((row_block, LANES), F32)
    vmem = pl.BlockSpec(memory_space=pltpu.VMEM)
    hbm = pl.BlockSpec(memory_space=pltpu.HBM)
    return pl.pallas_call(
        halo_kernel,
        out_shape=(pair, pair, inner, cosine, jax.ShapeDtypeStruct((SUB, LANES), F32)),
        in_specs=[hbm],
        out_specs=(vmem,) * 5,
        scratch_shapes=[
            pltpu.VMEM((tiles, strip_count, SUB, LANES), F32),
            pltpu.VMEM((tiles, strip_count, SUB, LANES), F32),
            pltpu.SemaphoreType.DMA((2, tiles)),
        ],
        compiler_params=pltpu.CompilerParams(vmem_limit_bytes=SMALL_VMEM_BYTES),
        cost_estimate=SMALL_COST,
        name="halo_rows",
    )(strips)


def column_weights():
    source = lax.broadcasted_iota(jnp.int32, (4 * LANES, 2 * LANES), 0)
    target = lax.broadcasted_iota(jnp.int32, (4 * LANES, 2 * LANES), 1)
    lane = source % LANES
    lane = jnp.where(source < 2 * LANES, lane, jnp.where(lane < LANES // 2, lane + LANES, lane - LANES))
    distance = lane - target % LANES
    near, far = jnp.abs(distance) == 1, jnp.abs(distance) == 2
    sign = jnp.where(distance > 0, 1.0, -1.0)
    slope = jnp.where(near, 8.0 * sign, jnp.where(far, -sign, 0.0))
    second = jnp.where(near, 16.0, jnp.where(far, -1.0, jnp.where(distance == 0, -30.0, 0.0)))
    return jnp.where(target < LANES, slope, second).astype(jnp.bfloat16)


def moment_kernel(*refs, remote, first_row, row_count, pieces, spread):
    if spread:
        small_sems = refs[-1]
        quality_ref, ranges_ref = refs[-3:-1]
        small_copies = [
            pltpu.make_async_copy(refs[kind], refs[kind - 3], small_sems.at[kind]) for kind in range(2)
        ]
        refs = refs[2:-3]
    else:
        limits_ref = refs[0]
        refs = refs[1:]
    cosine_ref, strips_ref, first_order_ref, second_order_ref, mine_ref = refs[:5]
    refs = refs[5:]
    other_refs, token_ref = refs[:pieces], refs[pieces]
    if spread:
        limits_ref, compact_ref = refs[pieces + 1:pieces + 3]
        refs = refs[2:]
    elevation, high_part, low_part, row_mask, col_mask, weights, first_slot, second_slot, sems = refs[pieces + 1:]
    del first_order_ref, second_order_ref
    token_ref[...] = jnp.zeros((SUB, LANES), F32)
    strip_count, row_block, col_count = strips_ref.shape
    tiles = col_count // LANES
    half = tiles // 2
    quarter = half // 2
    position = lax.axis_index("acq")
    side = position // 2
    core = position % 2
    base = (1 - side if remote else side) * half
    row_start = lax.axis_index("tile") * row_block + first_row
    low = max(first_row - SUB, 0)
    high = min(first_row + row_count + SUB, row_block)
    offset = SUB - (first_row - low)

    part = strip_count // LOAD_PARTS

    def fetch(index, which):
        lanes = pl.ds(pl.multiple_of((base + index - 1) * LANES, LANES), LANES)
        strips = pl.ds(which * part, part)
        return pltpu.make_async_copy(
            strips_ref.at[strips, pl.ds(low, high - low), lanes],
            elevation.at[strips, index, pl.ds(offset, high - low), :],
            sems.at[index, which],
        )

    def present(index):
        return (base + index >= 1) & (base + index <= tiles)

    def start(index, which):
        @pl.when(present(index))
        def _():
            fetch(index, which).start()

    zero = jnp.zeros((SUB, LANES), F32)

    def blank(index):
        @pl.when(jnp.logical_not(present(index)))
        def _():
            def body(strip, carry):
                for row in range(1, row_count // SUB + 1):
                    elevation[strip, index, row * SUB:(row + 1) * SUB, :] = zero
                return carry

            lax.fori_loop(0, strip_count, body, 0)

    def arrive(index, which):
        @pl.when(present(index))
        def _():
            fetch(index, which).wait()

        def split(step, carry):
            strip = which * part + step
            value = elevation[strip, index, SUB:SUB + row_count, :]
            upper = value.astype(jnp.bfloat16)
            high_part[strip, index] = upper
            low_part[strip, index] = (value - upper.astype(F32)).astype(jnp.bfloat16)
            return carry

        lax.fori_loop(0, part, split, 0, unroll=4)

    initial = (1 - core) * quarter
    later = core * quarter
    final = later + 2 * core
    for which in range(LOAD_PARTS):
        for step in range(3):
            start(initial + step, which)
    if spread:
        for copy in small_copies:
            copy.start()
    blank(0)
    blank(half + 1)

    weights[...] = column_weights()

    def spread_out(strip, rows):
        here = pl.ds(strip, 1)
        values = [ranges_ref[kind, strip].astype(F32) for kind in range(4)] + [quality_ref[strip]]
        lane = lax.broadcasted_iota(jnp.int32, (1, LANES), 1)
        for kind, value in enumerate(values):
            limits_ref[kind, here, :] = jnp.full((1, LANES), value, F32)
        return tuple(jnp.where(lane == strip, value, row) for row, value in zip(rows, values))

    if spread:
        for copy in small_copies:
            copy.wait()
        rows = lax.fori_loop(0, strip_count, spread_out, (jnp.zeros((1, LANES), F32),) * 5)
        compact_ref[...] = jnp.zeros((SUB, 2 * LANES), F32)
        for kind, row in enumerate(rows):
            compact_ref[kind:kind + 1, :LANES] = row

    def prepare(strip, carry):
        row_low, row_high, col_low, col_high, quality = (
            limits_ref[kind, pl.ds(strip, 1), :] for kind in range(5)
        )
        for tile in range(row_count // SUB):
            row = (lax.broadcasted_iota(jnp.int32, (SUB, LANES), 0) + (row_start + tile * SUB)).astype(F32)
            row_mask[strip, tile * SUB:(tile + 1) * SUB, :] = jnp.where(
                (row >= row_low) & (row < row_high), quality, 0.0
            )
        for tile in range(half):
            col = (lax.broadcasted_iota(jnp.int32, (SUB, LANES), 1) + (base + tile) * LANES).astype(F32)
            col_mask[strip, tile] = jnp.where((col >= col_low) & (col < col_high), 1.0, 0.0)
        if low == first_row:
            for tile in range(half + 2):
                elevation[strip, tile, 0:SUB, :] = zero
        if high == first_row + row_count:
            for tile in range(half + 2):
                elevation[strip, tile, SUB + row_count:2 * SUB + row_count, :] = zero
        return carry

    lax.fori_loop(0, strip_count, prepare, 0)

    tile_rows = row_count // SUB
    share = strip_count // tile_rows
    slots = (first_slot, second_slot)

    def columns_into(slot, at, first, count):
        strips = pl.ds(first, count)
        lane = lax.broadcasted_iota(jnp.int32, (count * row_count, LANES), 1)

        def load(ref, tile):
            return ref[strips, tile].reshape(count * row_count, LANES)

        edges = [
            jnp.where(lane < LANES // 2, load(ref, at + 1), load(ref, at - 1))
            for ref in (high_part, low_part)
        ]
        left = jnp.concatenate([load(high_part, at), load(low_part, at)] + edges, axis=1)
        product = jnp.dot(left, weights[...], preferred_element_type=F32)
        slots[slot][strips] = product.reshape(count, row_count, 2 * LANES)

    def column_tile(slot, at, following, store, lanes):
        def row_tile(tile, carry):
            row = pl.multiple_of(tile * SUB, SUB)
            cosine = cosine_ref[pl.ds(first_row + row, SUB), :]
            inverse_square = 1.0 / (cosine * cosine)

            unroll = strip_count if following is not None else 16

            def add_strips(chunk, sums):
                for index in range(unroll):
                    if following is not None and index in (0, 16):
                        columns_into(1 - slot, following, tile * share + (share // 2) * (index > 0), share // 2)
                    strip = chunk * unroll + index

                    def load(shift):
                        return elevation[strip, at, pl.ds(SUB + row + shift, SUB), :]

                    slope_x = slots[slot][strip, pl.ds(row, SUB), :LANES]
                    second_x = slots[slot][strip, pl.ds(row, SUB), LANES:]
                    mask = row_mask[strip, pl.ds(row, SUB), :] * col_mask[strip, at - 1]
                    shifts = (load(-2), load(-1), load(1), load(2))
                    terms = moment_terms(load(0), slope_x, second_x, shifts, inverse_square, mask)
                    sums = [total + term for total, term in zip(sums, terms)]
                return tuple(sums)

            if following is not None:
                sums = add_strips(0, zero_terms())
            else:
                sums = lax.fori_loop(0, strip_count // unroll, add_strips, zero_terms())
            for moment in range(MOMENTS):
                store(moment, pl.ds(row, SUB), lanes, sums[moment])
            return carry

        lax.fori_loop(0, tile_rows, row_tile, 0)

    for which in range(LOAD_PARTS):
        start(initial + 3, which)
    for which in range(LOAD_PARTS):
        for step in range(2):
            start(final + step, which)

    def first_columns(which, carry):
        for step in range(3):
            arrive(initial + step, which)
        for step in range(2):
            columns_into(0, initial + 1, which * part + step * (part // 2), part // 2)
        return carry

    lax.fori_loop(0, LOAD_PARTS, first_columns, 0)

    def arrive_whole(index):
        def body(which, carry):
            arrive(index, which)
            return carry

        lax.fori_loop(0, LOAD_PARTS, body, 0)

    def store_other(moment, rows, lanes, value):
        share = MOMENTS // pieces
        other_refs[moment // share][moment % share, rows, lanes] = value

    def store_mine(moment, rows, lanes, value):
        mine_ref[moment, rows, lanes] = value

    arrive_whole(initial + 3)
    column_tile(0, initial + 1, initial + 2, store_other, slice(0, LANES))
    arrive_whole(final)
    arrive_whole(final + 1)
    column_tile(1, initial + 2, later + 1, store_other, slice(LANES, 2 * LANES))
    column_tile(0, later + 1, later + 2, store_mine, slice(0, LANES))
    column_tile(1, later + 2, None, store_mine, slice(LANES, 2 * LANES))


def moments_of(limits, cosine, strips, order, remote, first_row, row_count, pieces):
    spread = len(limits) == 2
    strip_count, row_block, col_count = strips.shape
    half = col_count // LANES // 2
    out = jax.ShapeDtypeStruct((MOMENTS, row_count, col_count // 4), F32)
    piece = jax.ShapeDtypeStruct((MOMENTS // pieces, row_count, col_count // 4), F32)
    token = jax.ShapeDtypeStruct((SUB, LANES), F32)
    vmem = pl.BlockSpec(memory_space=pltpu.VMEM)
    anywhere = pl.BlockSpec(memory_space=pl.ANY)
    lanes = jax.ShapeDtypeStruct((5, strip_count, LANES), F32)
    compact = jax.ShapeDtypeStruct((SUB, 2 * LANES), F32)
    parts = pltpu.VMEM((strip_count, half + 2, row_count, LANES), jnp.bfloat16)
    slot = pltpu.VMEM((strip_count, row_count, 2 * LANES), F32)
    return pl.pallas_call(
        functools.partial(moment_kernel, remote=remote, first_row=first_row, row_count=row_count, pieces=pieces, spread=spread),
        out_shape=(out,) + (piece,) * pieces + (token,) + (lanes, compact) * spread,
        in_specs=[anywhere] * 2 * spread + [vmem] * (2 - spread) + [anywhere, vmem, vmem],
        out_specs=(vmem,) * (pieces + 2 + 2 * spread),
        scratch_shapes=[
            pltpu.VMEM((strip_count, half + 2, row_count + 2 * SUB, LANES), F32),
            parts,
            parts,
            pltpu.VMEM((strip_count, row_count, LANES), F32),
            pltpu.VMEM((strip_count, half, SUB, LANES), F32),
            pltpu.VMEM((4 * LANES, 2 * LANES), jnp.bfloat16),
            slot,
            slot,
            pltpu.SemaphoreType.DMA((half + 2, LOAD_PARTS)),
        ]
        + [
            pltpu.SMEM((strip_count,), F32),
            pltpu.SMEM((4, strip_count), jnp.int32),
            pltpu.SemaphoreType.DMA((2,)),
        ]
        * spread,
        compiler_params=pltpu.CompilerParams(vmem_limit_bytes=VMEM_BYTES),
        cost_estimate=SMALL_COST,
        name="moments_remote" if remote else "moments_own",
    )(*limits, cosine, strips, *order)


def edge_kernel(
    limits_ref, compact_ref, cosine_ref, above_ref, top_ref, inner_ref, bottom_ref, below_ref,
    first_order_ref, second_order_ref, mine_ref, other_ref, token_ref,
):
    del first_order_ref, second_order_ref
    token_ref[...] = jnp.zeros((SUB, LANES), F32)
    pair, strip_count, col_count = top_ref.shape
    row_block = cosine_ref.shape[0]
    tiles = col_count // LANES
    quarter = tiles // 4
    position = lax.axis_index("acq")
    side = position // 2
    core = position % 2
    row_start = lax.axis_index("tile") * row_block
    lane = lax.broadcasted_iota(jnp.int32, (SUB, LANES), 1)
    sources = [(above_ref, 0), (above_ref, 1), (top_ref, 0), (top_ref, 1), (inner_ref, 0), (inner_ref, 1)]
    sources += [(inner_ref, 2), (inner_ref, 3), (bottom_ref, 0), (bottom_ref, 1), (below_ref, 0), (below_ref, 1)]
    edges = ((0, 2), (1, 3), (row_block - 2, 8), (row_block - 1, 9))
    for out_ref, owner in ((mine_ref, core), (other_ref, 1 - core)):
        for part, owner_side in enumerate((1 - side, side)):
            out_ref[part, MOMENTS * EDGE_ROWS:MOMENTS * EDGE_ROWS + SUB, :] = compact_ref[...]

            def column_tile(tile, carry, out_ref=out_ref, part=part, first=(owner_side * 2 + owner) * quarter):
                at = first + tile
                left_keep = jnp.where(at > 0, 1.0, 0.0)
                right_keep = jnp.where(at < tiles - 1, 1.0, 0.0)
                here = pl.ds(pl.multiple_of(at * LANES, LANES), LANES)
                before = pl.ds(pl.multiple_of(jnp.maximum(at - 1, 0) * LANES, LANES), LANES)
                after = pl.ds(pl.multiple_of(jnp.minimum(at + 1, tiles - 1) * LANES, LANES), LANES)
                col = (lane + at * LANES).astype(F32)
                out_lanes = pl.ds(pl.multiple_of(tile * LANES, LANES), LANES)
                for edge, (row, source) in enumerate(edges):
                    cosine = cosine_ref[row:row + 1, :]
                    inverse_square = 1.0 / (cosine * cosine)
                    sums = zero_terms()
                    for group in range(strip_count // SUB):
                        strips = slice(group * SUB, (group + 1) * SUB)

                        def load(shift, where):
                            ref, index = sources[source + shift]
                            return ref[index, strips, where]

                        z = load(0, here)
                        cols = shifted_columns(
                            z, load(0, before) * left_keep, load(0, after) * right_keep, lane
                        )
                        limits = [limits_ref[kind, strips, :] for kind in range(4)]
                        at_row = (row_start + row).astype(F32)
                        inside = (limits[0] <= at_row) & (limits[1] > at_row)
                        inside = inside & (col >= limits[2]) & (col < limits[3])
                        mask = jnp.where(inside, limits_ref[4, strips, :], 0.0)
                        shifts = tuple(load(shift, here) for shift in (-2, -1, 1, 2))
                        terms = stencil_terms(z, shifts, cols, inverse_square, mask)
                        sums = [total + term for total, term in zip(sums, terms)]
                    for moment in range(MOMENTS):
                        spot = moment * EDGE_ROWS + edge
                        out_ref[part, spot:spot + 1, out_lanes] = jnp.sum(sums[moment], axis=0, keepdims=True)
                return carry

            lax.fori_loop(0, quarter, column_tile, 0)


def edge_moments(limits, compact, cosine, above, top, inner, bottom, below, *order):
    pair, strip_count, col_count = top.shape
    out = jax.ShapeDtypeStruct((2, MOMENTS * EDGE_ROWS + SUB, col_count // 4), F32)
    vmem = pl.BlockSpec(memory_space=pltpu.VMEM)
    return pl.pallas_call(
        edge_kernel,
        out_shape=(out, out, jax.ShapeDtypeStruct((SUB, LANES), F32)),
        in_specs=[vmem] * 10,
        out_specs=(vmem, vmem, vmem),
        compiler_params=pltpu.CompilerParams(vmem_limit_bytes=SMALL_VMEM_BYTES),
        cost_estimate=SMALL_COST,
        name="moments_edge",
    )(limits, compact, cosine, above, top, inner, bottom, below, *order)


def combine_kernel(mine_ref, *refs, pieces, edges):
    near_refs, rest = refs[:pieces], refs[pieces:]
    out_ref, token_ref = rest[-2:]
    token_ref[...] = jnp.zeros((SUB, LANES), F32)
    share, row_count, width = near_refs[0].shape
    for piece, near_ref in enumerate(near_refs):
        for moment in range(share):
            at = piece * share + moment
            out_ref[at * row_count:(at + 1) * row_count, :] = mine_ref[at] + near_ref[moment]
    if edges:
        edge_mine_ref, edge_core_ref = rest[:2]
        start, count = pieces * share * row_count, MOMENTS * EDGE_ROWS
        out_ref[start:start + count, :] = edge_mine_ref[0, :count] + edge_core_ref[0, :count]
        out_ref[start + count:start + count + SUB, :] = edge_mine_ref[0, count:]
        out_ref[start + count + SUB:, :] = edge_core_ref[0, count:]


def combine(mine, near, edges, order):
    moments, row_count, width = mine.shape
    rows = moments * row_count + sum(edge.shape[1] + SUB for edge in edges[:1])
    vmem = pl.BlockSpec(memory_space=pltpu.VMEM)
    return pl.pallas_call(
        functools.partial(combine_kernel, pieces=len(near), edges=bool(edges)),
        out_shape=(jax.ShapeDtypeStruct((rows, width), F32), jax.ShapeDtypeStruct((SUB, LANES), F32)),
        in_specs=[vmem] * (1 + len(near) + len(edges) + len(order)),
        out_specs=(vmem, vmem),
        compiler_params=pltpu.CompilerParams(vmem_limit_bytes=SMALL_VMEM_BYTES),
        cost_estimate=SMALL_COST,
        name="combine",
    )(mine, *near, *edges, *order)


def finish_kernel(pieces, cosine_ref, mine_ref, edge_mine_ref, edge_core_ref, *refs):
    far_refs, core_refs = refs[:len(pieces)], refs[len(pieces):-3]
    mean_ref, covariance_ref, available_ref = refs[-3:]
    row_block, width = mean_ref.shape
    share = MOMENTS // len(core_refs)
    edge_start = MOMENTS * row_block
    compact_start = edge_start + MOMENTS * EDGE_ROWS
    at_row = lax.broadcasted_iota(jnp.int32, (row_block, LANES), 0) + lax.axis_index("tile") * row_block
    at_col = lax.broadcasted_iota(jnp.int32, (width, LANES), 0) + lax.axis_index("acq") * width
    at_row, at_col = at_row.astype(F32), at_col.astype(F32)
    near_start = compact_start - edge_start
    compacts = [ref[1, near_start:near_start + SUB, :LANES] for ref in (edge_mine_ref, edge_core_ref)]
    compacts += [far_refs[-1][compact_start + SUB * part:compact_start + SUB * (part + 1), :LANES] for part in range(2)]
    rows_in, cols_in = [], []
    for compact in compacts:
        row_low, row_high, col_low, col_high, quality = (compact[kind:kind + 1, :] for kind in range(5))
        rows_in.append(jnp.where((at_row >= row_low) & (at_row < row_high), quality, 0.0))
        cols_in.append(jnp.where((at_col >= col_low) & (at_col < col_high), 1.0, 0.0))
    available = lax.dot_general(
        jnp.concatenate(rows_in, axis=1), jnp.concatenate(cols_in, axis=1), (((1,), (1,)), ((), ())),
        precision=lax.Precision.HIGHEST, preferred_element_type=F32,
    )
    available_ref[...] = available
    sub = lax.broadcasted_iota(jnp.int32, (SUB, LANES), 0)
    piece_rows = row_block // len(pieces)
    for first_row, far_ref in zip(pieces, far_refs):
        for tile_row in range(first_row, first_row + piece_rows, SUB):
            rows = slice(tile_row, tile_row + SUB)
            cosine = cosine_ref[rows, :]
            scales = (1.0, 1.0 / (12.0 * cosine), 1.0 / 12.0, 1.0 / 12.0)
            spots = {0: ((0, 0), (1, 1)), row_block - SUB: ((SUB - 2, 2), (SUB - 1, 3))}.get(tile_row, ())
            for tile in range(width // LANES):
                lanes = slice(tile * LANES, (tile + 1) * LANES)

                def total(moment):
                    near = core_refs[moment // share][moment % share, rows, lanes]
                    far_row = moment * piece_rows + tile_row - first_row
                    value = (mine_ref[moment, rows, lanes] + near) + far_ref[far_row:far_row + SUB, lanes]
                    for at, edge in spots:
                        spot = moment * EDGE_ROWS + edge
                        edge_far = far_refs[-1][edge_start + spot:edge_start + spot + 1, lanes]
                        spot = slice(spot, spot + 1)
                        line = (edge_mine_ref[1, spot, lanes] + edge_core_ref[1, spot, lanes]) + edge_far
                        value = jnp.where(sub == at, line, value)
                    return value

                along, across = total(FEATURES + 4), total(FEATURES + 7)
                steep = along / (cosine * cosine) + across
                inverse = 144.0 / jnp.maximum(available_ref[rows, lanes] - steep, 1.0)
                means = [total(first) * inverse * scales[first] for first in range(FEATURES)]
                mean_ref[rows, lanes] = means[0]
                entry = 0
                for first in range(FEATURES):
                    for second in range(first, FEATURES):
                        scale = scales[first] * scales[second]
                        covariance_ref[entry, rows, lanes] = (
                            total(FEATURES + entry) * inverse * scale - means[first] * means[second]
                        )
                        entry += 1


def finish(pieces, cosine, mine, edge_mine, edge_core, far, core):
    moments, row_block, width = mine.shape
    vmem = pl.BlockSpec(memory_space=pltpu.VMEM)
    entries = FEATURES * (FEATURES + 1) // 2
    return pl.pallas_call(
        functools.partial(finish_kernel, pieces),
        out_shape=(
            jax.ShapeDtypeStruct((row_block, width), F32),
            jax.ShapeDtypeStruct((entries, row_block, width), F32),
        ),
        in_specs=[vmem] * (4 + len(far) + len(core)),
        out_specs=(vmem, vmem),
        scratch_shapes=[pltpu.VMEM((row_block, width), F32)],
        compiler_params=pltpu.CompilerParams(vmem_limit_bytes=SMALL_VMEM_BYTES),
        cost_estimate=SMALL_COST,
        name="finish",
    )(cosine, mine, edge_mine, edge_core, *far, *core)


def exchange(value, distance):
    count = lax.axis_size("acq")
    return lax.ppermute(value, "acq", [(source, source ^ distance) for source in range(count)])


def local(strips, strip_quality, valid_ranges):
    strip_count, row_block, col_count = strips.shape
    tile_count = lax.axis_size("tile")
    ranges = valid_ranges.T

    top, bottom, inner, cosine, token = halo_rows(strips)
    forward = [(i, i + 1) for i in range(tile_count - 1)]
    backward = [(target, source) for source, target in forward]
    above = lax.ppermute(bottom, "tile", forward)
    below = lax.ppermute(top, "tile", backward)

    def compute(order, remote, first_row, row_count, source):
        return moments_of(source, cosine, strips, order, remote, first_row, row_count, PIECES)

    def swap(parts):
        return [exchange(part, 1) for part in parts]

    mine, *other, token, limits, compact = compute((token, token), True, 0, row_block, (strip_quality, ranges))
    near = swap(other)
    edge_mine, edge_other, token = edge_moments(
        limits, compact, cosine, above, top, inner, bottom, below, token, token
    )
    edge_core = exchange(edge_other, 1)
    payload, token = combine(mine, near, (edge_mine, edge_core), (token,))
    far = exchange(payload, 2)
    mine, *other, token = compute((token, token), False, 0, row_block, (limits,))
    return finish((0,), cosine, mine, edge_mine, edge_core, [far], swap(other))


def solution(mesh):
    return jax.shard_map(
        local,
        mesh=mesh,
        in_specs=(P("acq", "tile", None), P("acq"), P("acq", None)),
        out_specs=(P("tile", "acq"), P(None, "tile", "acq")),
        check_vma=False,
    )
```

```python
import functools
import jax
import jax.numpy as jnp
from jax import lax
from jax.experimental import pallas as pl
from jax.experimental.pallas import tpu as pltpu
from jax.sharding import PartitionSpec as P

MOMENTS = 14
FEATURES = 4
SUB = 8
LANES = 128
EDGE_ROWS = 4
VMEM_BYTES = 50 * 1024 * 1024
SMALL_VMEM_BYTES = 50 * 1024 * 1024
F32 = jnp.float32
LOAD_PARTS = 4
PIECES = 2
SMALL_COST = pl.CostEstimate(flops=1, bytes_accessed=1, transcendentals=0)


def moment_terms(z, slope_x, second_x, rows, inverse_square, mask):
    row_m2, row_m1, row_p1, row_p2 = rows
    slope_y = 8.0 * (row_p1 - row_m1) - (row_p2 - row_m2)
    second_y = 16.0 * (row_p1 + row_m1) - (row_p2 + row_m2) - 30.0 * z
    curvature = second_x * inverse_square + second_y
    steepness = (144.0 + slope_y * slope_y) + slope_x * slope_x * inverse_square
    weight = mask / steepness
    features = (z, slope_x, slope_y, curvature)
    weighted = [weight * feature for feature in features]
    terms = list(weighted)
    for first in range(FEATURES):
        for second in range(first, FEATURES):
            terms.append(weighted[first] * features[second])
    return terms


def stencil_terms(z, rows, cols, inverse_square, mask):
    col_m2, col_m1, col_p1, col_p2 = cols
    slope_x = 8.0 * (col_p1 - col_m1) - (col_p2 - col_m2)
    second_x = 16.0 * (col_p1 + col_m1) - (col_p2 + col_m2) - 30.0 * z
    return moment_terms(z, slope_x, second_x, rows, inverse_square, mask)


def shifted_columns(z, left, right, lane):
    return (
        pltpu.roll(jnp.where(lane >= LANES - 2, left, z), 2, 1),
        pltpu.roll(jnp.where(lane == LANES - 1, left, z), 1, 1),
        pltpu.roll(jnp.where(lane == 0, right, z), LANES - 1, 1),
        pltpu.roll(jnp.where(lane < 2, right, z), LANES - 2, 1),
    )


def zero_terms():
    return tuple(jnp.zeros((SUB, LANES), F32) for _ in range(MOMENTS))


def halo_kernel(
    strips_ref, top_ref, bottom_ref, inner_ref, cosine_ref, weights_ref, token_ref,
    first_ref, last_ref, sems,
):
    token_ref[...] = jnp.zeros((SUB, LANES), F32)
    strip_count, row_block, col_count = strips_ref.shape
    copies = []
    for tile in range(col_count // LANES):
        lanes = pl.ds(tile * LANES, LANES)
        for which, (start, target) in enumerate(((0, first_ref), (row_block - SUB, last_ref))):
            copies.append(
                pltpu.make_async_copy(
                    strips_ref.at[:, pl.ds(start, SUB), lanes], target.at[tile], sems.at[which, tile]
                )
            )
    for copy in copies:
        copy.start()
    weights_ref[...] = column_weights()
    total_rows = row_block * lax.axis_size("tile")
    row_start = lax.axis_index("tile") * row_block
    for tile in range(row_block // SUB):
        row = lax.broadcasted_iota(jnp.int32, (SUB, LANES), 0) + (row_start + tile * SUB)
        latitude = -1.0 + 2.0 * (row.astype(F32) + 0.5) / total_rows
        cosine_ref[tile * SUB:(tile + 1) * SUB, :] = jnp.cos(latitude)

    first_rows = first_ref.reshape(col_count // LANES, strip_count * SUB, LANES)
    last_rows = last_ref.reshape(col_count // LANES, strip_count * SUB, LANES)
    for tile in range(col_count // LANES):
        copies[2 * tile].wait()
        copies[2 * tile + 1].wait()
        lanes = slice(tile * LANES, (tile + 1) * LANES)
        for group in range(strip_count // SUB):
            strips = slice(group * SUB, (group + 1) * SUB)
            for row in range(2):
                at = group * SUB * SUB
                top_ref[row, strips, lanes] = first_rows[tile, pl.ds(at + row, SUB, stride=SUB), :]
                bottom_ref[row, strips, lanes] = last_rows[tile, pl.ds(at + 6 + row, SUB, stride=SUB), :]
                inner_ref[row, strips, lanes] = first_rows[tile, pl.ds(at + 2 + row, SUB, stride=SUB), :]
                inner_ref[2 + row, strips, lanes] = last_rows[tile, pl.ds(at + 4 + row, SUB, stride=SUB), :]


def halo_rows(strips):
    strip_count, row_block, col_count = strips.shape
    tiles = col_count // LANES
    pair = jax.ShapeDtypeStruct((2, strip_count, col_count), F32)
    inner = jax.ShapeDtypeStruct((4, strip_count, col_count), F32)
    cosine = jax.ShapeDtypeStruct((row_block, LANES), F32)
    weights = jax.ShapeDtypeStruct((4 * LANES, 2 * LANES), jnp.bfloat16)
    vmem = pl.BlockSpec(memory_space=pltpu.VMEM)
    hbm = pl.BlockSpec(memory_space=pltpu.HBM)
    return pl.pallas_call(
        halo_kernel,
        out_shape=(pair, pair, inner, cosine, weights, jax.ShapeDtypeStruct((SUB, LANES), F32)),
        in_specs=[hbm],
        out_specs=(vmem,) * 6,
        scratch_shapes=[
            pltpu.VMEM((tiles, strip_count, SUB, LANES), F32),
            pltpu.VMEM((tiles, strip_count, SUB, LANES), F32),
            pltpu.SemaphoreType.DMA((2, tiles)),
        ],
        compiler_params=pltpu.CompilerParams(vmem_limit_bytes=SMALL_VMEM_BYTES),
        cost_estimate=SMALL_COST,
        name="halo_rows",
    )(strips)


def column_weights():
    source = lax.broadcasted_iota(jnp.int32, (4 * LANES, 2 * LANES), 0)
    target = lax.broadcasted_iota(jnp.int32, (4 * LANES, 2 * LANES), 1)
    lane = source % LANES
    lane = jnp.where(source < 2 * LANES, lane, jnp.where(lane < LANES // 2, lane + LANES, lane - LANES))
    distance = lane - target % LANES
    near, far = jnp.abs(distance) == 1, jnp.abs(distance) == 2
    sign = jnp.where(distance > 0, 1.0, -1.0)
    slope = jnp.where(near, 8.0 * sign, jnp.where(far, -sign, 0.0))
    second = jnp.where(near, 16.0, jnp.where(far, -1.0, jnp.where(distance == 0, -30.0, 0.0)))
    return jnp.where(target < LANES, slope, second).astype(jnp.bfloat16)


def moment_kernel(*refs, remote, first_row, row_count, pieces, spread):
    if spread:
        small_sems = refs[-1]
        quality_ref, ranges_ref = refs[-3:-1]
        small_copies = [
            pltpu.make_async_copy(refs[kind], refs[kind - 3], small_sems.at[kind]) for kind in range(2)
        ]
        refs = refs[2:-3]
    else:
        limits_ref, row_mask = refs[:2]
        refs = refs[2:]
    cosine_ref, weights, strips_ref, first_order_ref, second_order_ref, mine_ref = refs[:6]
    refs = refs[6:]
    other_refs, token_ref = refs[:pieces], refs[pieces]
    if spread:
        limits_ref, compact_ref, row_mask = refs[pieces + 1:pieces + 4]
        refs = refs[3:]
    elevation, high_part, low_part, col_mask, first_slot, second_slot, sems = refs[pieces + 1:]
    del first_order_ref, second_order_ref
    token_ref[...] = jnp.zeros((SUB, LANES), F32)
    strip_count, row_block, col_count = strips_ref.shape
    tiles = col_count // LANES
    half = tiles // 2
    quarter = half // 2
    position = lax.axis_index("acq")
    side = position // 2
    core = position % 2
    base = (1 - side if remote else side) * half
    row_start = lax.axis_index("tile") * row_block + first_row
    low = max(first_row - SUB, 0)
    high = min(first_row + row_count + SUB, row_block)
    offset = SUB - (first_row - low)

    part = strip_count // LOAD_PARTS

    def fetch(index, which):
        lanes = pl.ds(pl.multiple_of((base + index - 1) * LANES, LANES), LANES)
        strips = pl.ds(which * part, part)
        return pltpu.make_async_copy(
            strips_ref.at[strips, pl.ds(low, high - low), lanes],
            elevation.at[strips, index, pl.ds(offset, high - low), :],
            sems.at[index, which],
        )

    def present(index):
        return (base + index >= 1) & (base + index <= tiles)

    def start(index, which):
        @pl.when(present(index))
        def _():
            fetch(index, which).start()

    zero = jnp.zeros((SUB, LANES), F32)

    def blank(index):
        @pl.when(jnp.logical_not(present(index)))
        def _():
            def body(strip, carry):
                for row in range(1, row_count // SUB + 1):
                    elevation[strip, index, row * SUB:(row + 1) * SUB, :] = zero
                return carry

            lax.fori_loop(0, strip_count, body, 0)

    def arrive(index, which):
        @pl.when(present(index))
        def _():
            fetch(index, which).wait()

        def split(step, carry):
            strip = which * part + step
            value = elevation[strip, index, SUB:SUB + row_count, :]
            upper = value.astype(jnp.bfloat16)
            high_part[strip, index] = upper
            low_part[strip, index] = (value - upper.astype(F32)).astype(jnp.bfloat16)
            return carry

        lax.fori_loop(0, part, split, 0, unroll=4)

    initial = (1 - core) * quarter
    later = core * quarter
    final = later + 2 * core
    for which in range(LOAD_PARTS):
        for step in range(3):
            start(initial + step, which)
    if spread:
        for copy in small_copies:
            copy.start()
    blank(0)
    blank(half + 1)

    def spread_out(strip, rows):
        here = pl.ds(strip, 1)
        values = [ranges_ref[kind, strip].astype(F32) for kind in range(4)] + [quality_ref[strip]]
        lane = lax.broadcasted_iota(jnp.int32, (1, LANES), 1)
        for kind, value in enumerate(values):
            limits_ref[kind, here, :] = jnp.full((1, LANES), value, F32)
        return tuple(jnp.where(lane == strip, value, row) for row, value in zip(rows, values))

    if spread:
        for copy in small_copies:
            copy.wait()
        rows = lax.fori_loop(0, strip_count, spread_out, (jnp.zeros((1, LANES), F32),) * 5)
        compact_ref[...] = jnp.zeros((SUB, 2 * LANES), F32)
        for kind, row in enumerate(rows):
            compact_ref[kind:kind + 1, :LANES] = row

    def prepare(strip, carry):
        row_low, row_high, col_low, col_high, quality = (
            limits_ref[kind, pl.ds(strip, 1), :] for kind in range(5)
        )
        for tile in range(row_count // SUB if spread else 0):
            row = (lax.broadcasted_iota(jnp.int32, (SUB, LANES), 0) + (row_start + tile * SUB)).astype(F32)
            row_mask[strip, tile * SUB:(tile + 1) * SUB, :] = jnp.where(
                (row >= row_low) & (row < row_high), quality, 0.0
            )
        for tile in range(half):
            col = (lax.broadcasted_iota(jnp.int32, (SUB, LANES), 1) + (base + tile) * LANES).astype(F32)
            col_mask[strip, tile] = jnp.where((col >= col_low) & (col < col_high), 1.0, 0.0)
        if low == first_row:
            for tile in range(half + 2):
                elevation[strip, tile, 0:SUB, :] = zero
        if high == first_row + row_count:
            for tile in range(half + 2):
                elevation[strip, tile, SUB + row_count:2 * SUB + row_count, :] = zero
        return carry

    lax.fori_loop(0, strip_count, prepare, 0)

    tile_rows = row_count // SUB
    share = strip_count // tile_rows
    slots = (first_slot, second_slot)

    def columns_into(slot, at, first, count):
        strips = pl.ds(first, count)
        lane = lax.broadcasted_iota(jnp.int32, (count * row_count, LANES), 1)

        def load(ref, tile):
            return ref[strips, tile].reshape(count * row_count, LANES)

        edges = [
            jnp.where(lane < LANES // 2, load(ref, at + 1), load(ref, at - 1))
            for ref in (high_part, low_part)
        ]
        left = jnp.concatenate([load(high_part, at), load(low_part, at)] + edges, axis=1)
        product = jnp.dot(left, weights[...], preferred_element_type=F32)
        slots[slot][strips] = product.reshape(count, row_count, 2 * LANES)

    def column_tile(slot, at, following, store, lanes):
        def row_tile(tile, carry):
            row = pl.multiple_of(tile * SUB, SUB)
            cosine = cosine_ref[pl.ds(first_row + row, SUB), :]
            inverse_square = 1.0 / (cosine * cosine)

            unroll = strip_count if following is not None else 16

            def add_strips(chunk, sums):
                for index in range(unroll):
                    if following is not None and index in (0, 16):
                        columns_into(1 - slot, following, tile * share + (share // 2) * (index > 0), share // 2)
                    strip = chunk * unroll + index

                    def load(shift):
                        return elevation[strip, at, pl.ds(SUB + row + shift, SUB), :]

                    slope_x = slots[slot][strip, pl.ds(row, SUB), :LANES]
                    second_x = slots[slot][strip, pl.ds(row, SUB), LANES:]
                    mask = row_mask[strip, pl.ds(row, SUB), :] * col_mask[strip, at - 1]
                    shifts = (load(-2), load(-1), load(1), load(2))
                    terms = moment_terms(load(0), slope_x, second_x, shifts, inverse_square, mask)
                    sums = [total + term for total, term in zip(sums, terms)]
                return tuple(sums)

            if following is not None:
                sums = add_strips(0, zero_terms())
            else:
                sums = lax.fori_loop(0, strip_count // unroll, add_strips, zero_terms())
            for moment in range(MOMENTS):
                store(moment, pl.ds(row, SUB), lanes, sums[moment])
            return carry

        lax.fori_loop(0, tile_rows, row_tile, 0)

    for which in range(LOAD_PARTS):
        start(initial + 3, which)
    for which in range(LOAD_PARTS):
        for step in range(2):
            start(final + step, which)

    def first_columns(which, carry):
        for step in range(3):
            arrive(initial + step, which)
        for step in range(2):
            columns_into(0, initial + 1, which * part + step * (part // 2), part // 2)
        return carry

    lax.fori_loop(0, LOAD_PARTS, first_columns, 0)

    def arrive_whole(index):
        def body(which, carry):
            arrive(index, which)
            return carry

        lax.fori_loop(0, LOAD_PARTS, body, 0)

    def store_other(moment, rows, lanes, value):
        share = MOMENTS // pieces
        other_refs[moment // share][moment % share, rows, lanes] = value

    def store_mine(moment, rows, lanes, value):
        mine_ref[moment, rows, lanes] = value

    arrive_whole(initial + 3)
    column_tile(0, initial + 1, initial + 2, store_other, slice(0, LANES))
    arrive_whole(final)
    arrive_whole(final + 1)
    column_tile(1, initial + 2, later + 1, store_other, slice(LANES, 2 * LANES))
    column_tile(0, later + 1, later + 2, store_mine, slice(0, LANES))
    column_tile(1, later + 2, None, store_mine, slice(LANES, 2 * LANES))


def moments_of(limits, spread, cosine, weights, strips, order, remote, first_row, row_count, pieces):
    strip_count, row_block, col_count = strips.shape
    half = col_count // LANES // 2
    out = jax.ShapeDtypeStruct((MOMENTS, row_count, col_count // 4), F32)
    piece = jax.ShapeDtypeStruct((MOMENTS // pieces, row_count, col_count // 4), F32)
    token = jax.ShapeDtypeStruct((SUB, LANES), F32)
    vmem = pl.BlockSpec(memory_space=pltpu.VMEM)
    anywhere = pl.BlockSpec(memory_space=pl.ANY)
    lanes = jax.ShapeDtypeStruct((5, strip_count, LANES), F32)
    compact = jax.ShapeDtypeStruct((SUB, 2 * LANES), F32)
    mask = jax.ShapeDtypeStruct((strip_count, row_count, LANES), F32)
    parts = pltpu.VMEM((strip_count, half + 2, row_count, LANES), jnp.bfloat16)
    slot = pltpu.VMEM((strip_count, row_count, 2 * LANES), F32)
    return pl.pallas_call(
        functools.partial(moment_kernel, remote=remote, first_row=first_row, row_count=row_count, pieces=pieces, spread=spread),
        out_shape=(out,) + (piece,) * pieces + (token,) + (lanes, compact, mask) * spread,
        in_specs=[anywhere if spread else vmem] * 2 + [vmem, vmem, anywhere, vmem, vmem],
        out_specs=(vmem,) * (pieces + 2 + 3 * spread),
        scratch_shapes=[
            pltpu.VMEM((strip_count, half + 2, row_count + 2 * SUB, LANES), F32),
            parts,
            parts,
            pltpu.VMEM((strip_count, half, SUB, LANES), F32),
            slot,
            slot,
            pltpu.SemaphoreType.DMA((half + 2, LOAD_PARTS)),
        ]
        + [
            pltpu.SMEM((strip_count,), F32),
            pltpu.SMEM((4, strip_count), jnp.int32),
            pltpu.SemaphoreType.DMA((2,)),
        ]
        * spread,
        compiler_params=pltpu.CompilerParams(vmem_limit_bytes=VMEM_BYTES),
        cost_estimate=SMALL_COST,
        name="moments_remote" if remote else "moments_own",
    )(*limits, cosine, weights, strips, *order)


def edge_kernel(
    limits_ref, compact_ref, cosine_ref, above_ref, top_ref, inner_ref, bottom_ref, below_ref,
    order_ref, mine_ref, other_ref, token_ref, *, remote,
):
    del order_ref
    token_ref[...] = jnp.zeros((SUB, LANES), F32)
    pair, strip_count, col_count = top_ref.shape
    row_block = cosine_ref.shape[0]
    tiles = col_count // LANES
    quarter = tiles // 4
    position = lax.axis_index("acq")
    side = position // 2
    core = position % 2
    row_start = lax.axis_index("tile") * row_block
    lane = lax.broadcasted_iota(jnp.int32, (SUB, LANES), 1)
    sources = [(above_ref, 0), (above_ref, 1), (top_ref, 0), (top_ref, 1), (inner_ref, 0), (inner_ref, 1)]
    sources += [(inner_ref, 2), (inner_ref, 3), (bottom_ref, 0), (bottom_ref, 1), (below_ref, 0), (below_ref, 1)]
    edges = ((0, 2), (1, 3), (row_block - 2, 8), (row_block - 1, 9))
    for out_ref, owner in ((mine_ref, core), (other_ref, 1 - core)):
        for part, owner_side in enumerate((1 - side if remote else side,)):
            out_ref[part, MOMENTS * EDGE_ROWS:MOMENTS * EDGE_ROWS + SUB, :] = compact_ref[...]

            def column_tile(tile, carry, out_ref=out_ref, part=part, first=(owner_side * 2 + owner) * quarter):
                at = first + tile
                left_keep = jnp.where(at > 0, 1.0, 0.0)
                right_keep = jnp.where(at < tiles - 1, 1.0, 0.0)
                here = pl.ds(pl.multiple_of(at * LANES, LANES), LANES)
                before = pl.ds(pl.multiple_of(jnp.maximum(at - 1, 0) * LANES, LANES), LANES)
                after = pl.ds(pl.multiple_of(jnp.minimum(at + 1, tiles - 1) * LANES, LANES), LANES)
                col = (lane + at * LANES).astype(F32)
                out_lanes = pl.ds(pl.multiple_of(tile * LANES, LANES), LANES)
                for edge, (row, source) in enumerate(edges):
                    cosine = cosine_ref[row:row + 1, :]
                    inverse_square = 1.0 / (cosine * cosine)
                    sums = zero_terms()
                    for group in range(strip_count // SUB):
                        strips = slice(group * SUB, (group + 1) * SUB)

                        def load(shift, where):
                            ref, index = sources[source + shift]
                            return ref[index, strips, where]

                        z = load(0, here)
                        cols = shifted_columns(
                            z, load(0, before) * left_keep, load(0, after) * right_keep, lane
                        )
                        limits = [limits_ref[kind, strips, :] for kind in range(4)]
                        at_row = (row_start + row).astype(F32)
                        inside = (limits[0] <= at_row) & (limits[1] > at_row)
                        inside = inside & (col >= limits[2]) & (col < limits[3])
                        mask = jnp.where(inside, limits_ref[4, strips, :], 0.0)
                        shifts = tuple(load(shift, here) for shift in (-2, -1, 1, 2))
                        terms = stencil_terms(z, shifts, cols, inverse_square, mask)
                        sums = [total + term for total, term in zip(sums, terms)]
                    for moment in range(MOMENTS):
                        spot = moment * EDGE_ROWS + edge
                        out_ref[part, spot:spot + 1, out_lanes] = jnp.sum(sums[moment], axis=0, keepdims=True)
                return carry

            lax.fori_loop(0, quarter, column_tile, 0)


def edge_moments(limits, compact, cosine, above, top, inner, bottom, below, order, remote):
    pair, strip_count, col_count = top.shape
    out = jax.ShapeDtypeStruct((1, MOMENTS * EDGE_ROWS + SUB, col_count // 4), F32)
    vmem = pl.BlockSpec(memory_space=pltpu.VMEM)
    return pl.pallas_call(
        functools.partial(edge_kernel, remote=remote),
        out_shape=(out, out, jax.ShapeDtypeStruct((SUB, LANES), F32)),
        in_specs=[vmem] * 9,
        out_specs=(vmem, vmem, vmem),
        compiler_params=pltpu.CompilerParams(vmem_limit_bytes=SMALL_VMEM_BYTES),
        cost_estimate=SMALL_COST,
        name="edges_remote" if remote else "edges_own",
    )(limits, compact, cosine, above, top, inner, bottom, below, order)


def combine_kernel(mine_ref, *refs, pieces, edges):
    near_refs, rest = refs[:pieces], refs[pieces:]
    out_ref, token_ref = rest[-2:]
    token_ref[...] = jnp.zeros((SUB, LANES), F32)
    share, row_count, width = near_refs[0].shape
    for piece, near_ref in enumerate(near_refs):
        for moment in range(share):
            at = piece * share + moment
            out_ref[at * row_count:(at + 1) * row_count, :] = mine_ref[at] + near_ref[moment]
    if edges:
        edge_mine_ref, edge_core_ref = rest[:2]
        start, count = pieces * share * row_count, MOMENTS * EDGE_ROWS
        out_ref[start:start + count, :] = edge_mine_ref[0, :count] + edge_core_ref[0, :count]
        out_ref[start + count:start + count + SUB, :] = edge_mine_ref[0, count:]
        out_ref[start + count + SUB:, :] = edge_core_ref[0, count:]


def combine(mine, near, edges, order):
    moments, row_count, width = mine.shape
    rows = moments * row_count + sum(edge.shape[1] + SUB for edge in edges[:1])
    vmem = pl.BlockSpec(memory_space=pltpu.VMEM)
    return pl.pallas_call(
        functools.partial(combine_kernel, pieces=len(near), edges=bool(edges)),
        out_shape=(jax.ShapeDtypeStruct((rows, width), F32), jax.ShapeDtypeStruct((SUB, LANES), F32)),
        in_specs=[vmem] * (1 + len(near) + len(edges) + len(order)),
        out_specs=(vmem, vmem),
        compiler_params=pltpu.CompilerParams(vmem_limit_bytes=SMALL_VMEM_BYTES),
        cost_estimate=SMALL_COST,
        name="combine",
    )(mine, *near, *edges, *order)


def finish_kernel(pieces, cosine_ref, mine_ref, edge_mine_ref, edge_core_ref, *refs):
    far_refs, core_refs = refs[:len(pieces)], refs[len(pieces):-6]
    mean_out, covariance_out, mean_ref, covariance_ref, available_ref, sems = refs[-6:]
    row_block, width = mean_ref.shape
    share = MOMENTS // len(core_refs)
    edge_start = MOMENTS * row_block
    compact_start = edge_start + MOMENTS * EDGE_ROWS
    at_row = lax.broadcasted_iota(jnp.int32, (row_block, LANES), 0) + lax.axis_index("tile") * row_block
    at_col = lax.broadcasted_iota(jnp.int32, (width, LANES), 0) + lax.axis_index("acq") * width
    at_row, at_col = at_row.astype(F32), at_col.astype(F32)
    near_start = compact_start - edge_start
    compacts = [ref[0, near_start:near_start + SUB, :LANES] for ref in (edge_mine_ref, edge_core_ref)]
    compacts += [far_refs[-1][compact_start + SUB * part:compact_start + SUB * (part + 1), :LANES] for part in range(2)]
    rows_in, cols_in = [], []
    for compact in compacts:
        row_low, row_high, col_low, col_high, quality = (compact[kind:kind + 1, :] for kind in range(5))
        rows_in.append(jnp.where((at_row >= row_low) & (at_row < row_high), quality, 0.0))
        cols_in.append(jnp.where((at_col >= col_low) & (at_col < col_high), 1.0, 0.0))
    available = lax.dot_general(
        jnp.concatenate(rows_in, axis=1), jnp.concatenate(cols_in, axis=1), (((1,), (1,)), ((), ())),
        precision=lax.Precision.HIGHEST, preferred_element_type=F32,
    )
    available_ref[...] = available
    sub = lax.broadcasted_iota(jnp.int32, (SUB, LANES), 0)
    piece_rows = row_block // len(pieces)
    copies = []
    for first_row, far_ref in zip(pieces, far_refs):
        for tile_row in range(first_row, first_row + piece_rows, SUB):
            rows = slice(tile_row, tile_row + SUB)
            cosine = cosine_ref[rows, :]
            scales = (1.0, 1.0 / (12.0 * cosine), 1.0 / 12.0, 1.0 / 12.0)
            spots = {0: ((0, 0), (1, 1)), row_block - SUB: ((SUB - 2, 2), (SUB - 1, 3))}.get(tile_row, ())
            for tile in range(width // LANES):
                lanes = slice(tile * LANES, (tile + 1) * LANES)

                def total(moment):
                    near = core_refs[moment // share][moment % share, rows, lanes]
                    far_row = moment * piece_rows + tile_row - first_row
                    value = (mine_ref[moment, rows, lanes] + near) + far_ref[far_row:far_row + SUB, lanes]
                    for at, edge in spots:
                        spot = moment * EDGE_ROWS + edge
                        edge_far = far_refs[-1][edge_start + spot:edge_start + spot + 1, lanes]
                        spot = slice(spot, spot + 1)
                        line = (edge_mine_ref[0, spot, lanes] + edge_core_ref[0, spot, lanes]) + edge_far
                        value = jnp.where(sub == at, line, value)
                    return value

                along, across = total(FEATURES + 4), total(FEATURES + 7)
                steep = along / (cosine * cosine) + across
                inverse = 144.0 / jnp.maximum(available_ref[rows, lanes] - steep, 1.0)
                means = [total(first) * inverse * scales[first] for first in range(FEATURES)]
                mean_ref[rows, lanes] = means[0]
                entry = 0
                for first in range(FEATURES):
                    for second in range(first, FEATURES):
                        scale = scales[first] * scales[second]
                        covariance_ref[entry, rows, lanes] = (
                            total(FEATURES + entry) * inverse * scale - means[first] * means[second]
                        )
                        entry += 1
            if (tile_row + SUB) % (row_block // 2) == 0:
                which = tile_row // (row_block // 2)
                block = pl.ds(which * (row_block // 2), row_block // 2)
                copies += [
                    pltpu.make_async_copy(mean_ref.at[block], mean_out.at[block], sems.at[0, which]),
                    pltpu.make_async_copy(
                        covariance_ref.at[:, block], covariance_out.at[:, block], sems.at[1, which]
                    ),
                ]
                for copy in copies[-2:]:
                    copy.start()
    for copy in copies:
        copy.wait()


def finish(pieces, cosine, mine, edge_mine, edge_core, far, core):
    moments, row_block, width = mine.shape
    vmem = pl.BlockSpec(memory_space=pltpu.VMEM)
    entries = FEATURES * (FEATURES + 1) // 2
    return pl.pallas_call(
        functools.partial(finish_kernel, pieces),
        out_shape=(
            jax.ShapeDtypeStruct((row_block, width), F32),
            jax.ShapeDtypeStruct((entries, row_block, width), F32),
        ),
        in_specs=[vmem] * (4 + len(far) + len(core)),
        out_specs=(pl.BlockSpec(memory_space=pl.ANY),) * 2,
        scratch_shapes=[
            pltpu.VMEM((row_block, width), F32),
            pltpu.VMEM((entries, row_block, width), F32),
            pltpu.VMEM((row_block, width), F32),
            pltpu.SemaphoreType.DMA((2, 2)),
        ],
        compiler_params=pltpu.CompilerParams(vmem_limit_bytes=SMALL_VMEM_BYTES),
        cost_estimate=SMALL_COST,
        name="finish",
    )(cosine, mine, edge_mine, edge_core, *far, *core)


def exchange(value, distance):
    count = lax.axis_size("acq")
    return lax.ppermute(value, "acq", [(source, source ^ distance) for source in range(count)])


def local(strips, strip_quality, valid_ranges):
    strip_count, row_block, col_count = strips.shape
    tile_count = lax.axis_size("tile")
    ranges = valid_ranges.T

    top, bottom, inner, cosine, weights, token = halo_rows(strips)
    forward = [(i, i + 1) for i in range(tile_count - 1)]
    backward = [(target, source) for source, target in forward]
    above = lax.ppermute(bottom, "tile", forward)
    below = lax.ppermute(top, "tile", backward)

    def compute(order, remote, source):
        return moments_of(source, remote, cosine, weights, strips, order, remote, 0, row_block, PIECES)

    def edges(order, remote):
        return edge_moments(limits, compact, cosine, above, top, inner, bottom, below, order, remote)

    def swap(parts):
        return [exchange(part, 1) for part in parts]

    mine, *other, token, limits, compact, mask = compute((token, token), True, (strip_quality, ranges))
    near = swap(other)
    edge_mine, edge_other, token = edges(token, True)
    payload, token = combine(mine, near, (edge_mine, exchange(edge_other, 1)), (token,))
    far = exchange(payload, 2)
    edge_mine, edge_other, token = edges(token, False)
    mine, *other, token = compute((token, token), False, (limits, mask))
    return finish((0,), cosine, mine, edge_mine, exchange(edge_other, 1), [far], swap(other))


def solution(mesh):
    return jax.shard_map(
        local,
        mesh=mesh,
        in_specs=(P("acq", "tile", None), P("acq"), P("acq", None)),
        out_specs=(P("tile", "acq"), P(None, "tile", "acq")),
        check_vma=False,
    )
```

```python
import functools
import jax
import jax.numpy as jnp
from jax import lax
from jax.experimental import pallas as pl
from jax.experimental.pallas import tpu as pltpu
from jax.sharding import PartitionSpec as P

MOMENTS = 14
FEATURES = 4
SUB = 8
LANES = 128
EDGE_ROWS = 4
VMEM_BYTES = 50 * 1024 * 1024
SMALL_VMEM_BYTES = 50 * 1024 * 1024
F32 = jnp.float32
LOAD_PARTS = 4
PIECES = 2
SMALL_COST = pl.CostEstimate(flops=1, bytes_accessed=1, transcendentals=0)


def moment_terms(z, slope_x, second_x, rows, inverse_square, mask):
    row_m2, row_m1, row_p1, row_p2 = rows
    slope_y = 8.0 * (row_p1 - row_m1) - (row_p2 - row_m2)
    second_y = 16.0 * (row_p1 + row_m1) - (row_p2 + row_m2) - 30.0 * z
    curvature = second_x * inverse_square + second_y
    steepness = (144.0 + slope_y * slope_y) + slope_x * slope_x * inverse_square
    weight = mask / steepness
    features = (z, slope_x, slope_y, curvature)
    weighted = [weight * feature for feature in features]
    terms = list(weighted)
    for first in range(FEATURES):
        for second in range(first, FEATURES):
            terms.append(weighted[first] * features[second])
    return terms


def stencil_terms(z, rows, cols, inverse_square, mask):
    col_m2, col_m1, col_p1, col_p2 = cols
    slope_x = 8.0 * (col_p1 - col_m1) - (col_p2 - col_m2)
    second_x = 16.0 * (col_p1 + col_m1) - (col_p2 + col_m2) - 30.0 * z
    return moment_terms(z, slope_x, second_x, rows, inverse_square, mask)


def shifted_columns(z, left, right, lane):
    return (
        pltpu.roll(jnp.where(lane >= LANES - 2, left, z), 2, 1),
        pltpu.roll(jnp.where(lane == LANES - 1, left, z), 1, 1),
        pltpu.roll(jnp.where(lane == 0, right, z), LANES - 1, 1),
        pltpu.roll(jnp.where(lane < 2, right, z), LANES - 2, 1),
    )


def zero_terms():
    return tuple(jnp.zeros((SUB, LANES), F32) for _ in range(MOMENTS))


def halo_kernel(
    strips_ref, first_out, second_out, inner_ref, cosine_ref, weights_ref, token_ref,
    first_ref, last_ref, sems,
):
    token_ref[...] = jnp.zeros((SUB, LANES), F32)
    strip_count, row_block, col_count = strips_ref.shape
    copies = []
    for tile in range(col_count // LANES):
        lanes = pl.ds(tile * LANES, LANES)
        for which, (start, target) in enumerate(((0, first_ref), (row_block - SUB, last_ref))):
            copies.append(
                pltpu.make_async_copy(
                    strips_ref.at[:, pl.ds(start, SUB), lanes], target.at[tile], sems.at[which, tile]
                )
            )
    for copy in copies:
        copy.start()
    weights_ref[...] = column_weights()
    total_rows = row_block * lax.axis_size("tile")
    row_start = lax.axis_index("tile") * row_block
    even = lax.axis_index("tile") % 2 == 0
    for tile in range(row_block // SUB):
        row = lax.broadcasted_iota(jnp.int32, (SUB, LANES), 0) + (row_start + tile * SUB)
        latitude = -1.0 + 2.0 * (row.astype(F32) + 0.5) / total_rows
        cosine_ref[tile * SUB:(tile + 1) * SUB, :] = jnp.cos(latitude)

    first_rows = first_ref.reshape(col_count // LANES, strip_count * SUB, LANES)
    last_rows = last_ref.reshape(col_count // LANES, strip_count * SUB, LANES)
    for tile in range(col_count // LANES):
        copies[2 * tile].wait()
        copies[2 * tile + 1].wait()
        lanes = slice(tile * LANES, (tile + 1) * LANES)
        for group in range(strip_count // SUB):
            strips = slice(group * SUB, (group + 1) * SUB)
            for row in range(2):
                at = group * SUB * SUB
                top = first_rows[tile, pl.ds(at + row, SUB, stride=SUB), :]
                bottom = last_rows[tile, pl.ds(at + 6 + row, SUB, stride=SUB), :]
                first_out[row, strips, lanes] = jnp.where(even, bottom, top)
                second_out[row, strips, lanes] = jnp.where(even, top, bottom)
                inner_ref[row, strips, lanes] = first_rows[tile, pl.ds(at + 2 + row, SUB, stride=SUB), :]
                inner_ref[2 + row, strips, lanes] = last_rows[tile, pl.ds(at + 4 + row, SUB, stride=SUB), :]


def halo_rows(strips):
    strip_count, row_block, col_count = strips.shape
    tiles = col_count // LANES
    pair = jax.ShapeDtypeStruct((2, strip_count, col_count), F32)
    inner = jax.ShapeDtypeStruct((4, strip_count, col_count), F32)
    cosine = jax.ShapeDtypeStruct((row_block, LANES), F32)
    weights = jax.ShapeDtypeStruct((4 * LANES, 2 * LANES), jnp.bfloat16)
    vmem = pl.BlockSpec(memory_space=pltpu.VMEM)
    hbm = pl.BlockSpec(memory_space=pltpu.HBM)
    return pl.pallas_call(
        halo_kernel,
        out_shape=(pair, pair, inner, cosine, weights, jax.ShapeDtypeStruct((SUB, LANES), F32)),
        in_specs=[hbm],
        out_specs=(vmem,) * 6,
        scratch_shapes=[
            pltpu.VMEM((tiles, strip_count, SUB, LANES), F32),
            pltpu.VMEM((tiles, strip_count, SUB, LANES), F32),
            pltpu.SemaphoreType.DMA((2, tiles)),
        ],
        compiler_params=pltpu.CompilerParams(vmem_limit_bytes=SMALL_VMEM_BYTES),
        cost_estimate=SMALL_COST,
        name="halo_rows",
    )(strips)


def column_weights():
    source = lax.broadcasted_iota(jnp.int32, (4 * LANES, 2 * LANES), 0)
    target = lax.broadcasted_iota(jnp.int32, (4 * LANES, 2 * LANES), 1)
    lane = source % LANES
    lane = jnp.where(source < 2 * LANES, lane, jnp.where(lane < LANES // 2, lane + LANES, lane - LANES))
    distance = lane - target % LANES
    near, far = jnp.abs(distance) == 1, jnp.abs(distance) == 2
    sign = jnp.where(distance > 0, 1.0, -1.0)
    slope = jnp.where(near, 8.0 * sign, jnp.where(far, -sign, 0.0))
    second = jnp.where(near, 16.0, jnp.where(far, -1.0, jnp.where(distance == 0, -30.0, 0.0)))
    return jnp.where(target < LANES, slope, second).astype(jnp.bfloat16)


def moment_kernel(*refs, remote, first_row, row_count, pieces, spread):
    if spread:
        small_sems = refs[-1]
        quality_ref, ranges_ref = refs[-3:-1]
        small_copies = [
            pltpu.make_async_copy(refs[kind], refs[kind - 3], small_sems.at[kind]) for kind in range(2)
        ]
        refs = refs[2:-3]
    else:
        limits_ref, row_mask = refs[:2]
        refs = refs[2:]
    cosine_ref, weights, strips_ref, first_order_ref, second_order_ref, mine_ref = refs[:6]
    refs = refs[6:]
    other_refs, token_ref = refs[:pieces], refs[pieces]
    if spread:
        limits_ref, compact_ref, row_mask = refs[pieces + 1:pieces + 4]
        refs = refs[3:]
    elevation, high_part, low_part, col_mask, first_slot, second_slot, sems = refs[pieces + 1:]
    del first_order_ref, second_order_ref
    token_ref[...] = jnp.zeros((SUB, LANES), F32)
    strip_count, row_block, col_count = strips_ref.shape
    tiles = col_count // LANES
    half = tiles // 2
    quarter = half // 2
    position = lax.axis_index("acq")
    side = position // 2
    core = position % 2
    base = (1 - side if remote else side) * half
    row_start = lax.axis_index("tile") * row_block + first_row
    low = max(first_row - SUB, 0)
    high = min(first_row + row_count + SUB, row_block)
    offset = SUB - (first_row - low)

    part = strip_count // LOAD_PARTS

    def fetch(index, which):
        lanes = pl.ds(pl.multiple_of((base + index - 1) * LANES, LANES), LANES)
        strips = pl.ds(which * part, part)
        return pltpu.make_async_copy(
            strips_ref.at[strips, pl.ds(low, high - low), lanes],
            elevation.at[strips, index, pl.ds(offset, high - low), :],
            sems.at[index, which],
        )

    def present(index):
        return (base + index >= 1) & (base + index <= tiles)

    def start(index, which):
        @pl.when(present(index))
        def _():
            fetch(index, which).start()

    zero = jnp.zeros((SUB, LANES), F32)

    def blank(index):
        @pl.when(jnp.logical_not(present(index)))
        def _():
            def body(strip, carry):
                for row in range(1, row_count // SUB + 1):
                    elevation[strip, index, row * SUB:(row + 1) * SUB, :] = zero
                return carry

            lax.fori_loop(0, strip_count, body, 0)

    def arrive(index, which):
        @pl.when(present(index))
        def _():
            fetch(index, which).wait()

        def split(step, carry):
            strip = which * part + step
            value = elevation[strip, index, SUB:SUB + row_count, :]
            upper = value.astype(jnp.bfloat16)
            high_part[strip, index] = upper
            low_part[strip, index] = (value - upper.astype(F32)).astype(jnp.bfloat16)
            return carry

        lax.fori_loop(0, part, split, 0, unroll=4)

    initial = (1 - core) * quarter
    later = core * quarter
    final = later + 2 * core
    for which in range(LOAD_PARTS):
        for step in range(3):
            start(initial + step, which)
    if spread:
        for copy in small_copies:
            copy.start()
    blank(0)
    blank(half + 1)

    def spread_out(strip, rows):
        here = pl.ds(strip, 1)
        values = [ranges_ref[kind, strip].astype(F32) for kind in range(4)] + [quality_ref[strip]]
        lane = lax.broadcasted_iota(jnp.int32, (1, LANES), 1)
        for kind, value in enumerate(values):
            limits_ref[kind, here, :] = jnp.full((1, LANES), value, F32)
        return tuple(jnp.where(lane == strip, value, row) for row, value in zip(rows, values))

    if spread:
        for copy in small_copies:
            copy.wait()
        rows = lax.fori_loop(0, strip_count, spread_out, (jnp.zeros((1, LANES), F32),) * 5)
        compact_ref[...] = jnp.zeros((SUB, 2 * LANES), F32)
        for kind, row in enumerate(rows):
            compact_ref[kind:kind + 1, :LANES] = row

    def prepare(strip, carry):
        row_low, row_high, col_low, col_high, quality = (
            limits_ref[kind, pl.ds(strip, 1), :] for kind in range(5)
        )
        for tile in range(row_count // SUB if spread else 0):
            row = (lax.broadcasted_iota(jnp.int32, (SUB, LANES), 0) + (row_start + tile * SUB)).astype(F32)
            row_mask[strip, tile * SUB:(tile + 1) * SUB, :] = jnp.where(
                (row >= row_low) & (row < row_high), quality, 0.0
            )
        for tile in range(half):
            col = (lax.broadcasted_iota(jnp.int32, (SUB, LANES), 1) + (base + tile) * LANES).astype(F32)
            col_mask[strip, tile] = jnp.where((col >= col_low) & (col < col_high), 1.0, 0.0)
        if low == first_row:
            for tile in range(half + 2):
                elevation[strip, tile, 0:SUB, :] = zero
        if high == first_row + row_count:
            for tile in range(half + 2):
                elevation[strip, tile, SUB + row_count:2 * SUB + row_count, :] = zero
        return carry

    lax.fori_loop(0, strip_count, prepare, 0)

    tile_rows = row_count // SUB
    share = strip_count // tile_rows
    slots = (first_slot, second_slot)

    def columns_into(slot, at, first, count):
        strips = pl.ds(first, count)
        lane = lax.broadcasted_iota(jnp.int32, (count * row_count, LANES), 1)

        def load(ref, tile):
            return ref[strips, tile].reshape(count * row_count, LANES)

        edges = [
            jnp.where(lane < LANES // 2, load(ref, at + 1), load(ref, at - 1))
            for ref in (high_part, low_part)
        ]
        left = jnp.concatenate([load(high_part, at), load(low_part, at)] + edges, axis=1)
        product = jnp.dot(left, weights[...], preferred_element_type=F32)
        slots[slot][strips] = product.reshape(count, row_count, 2 * LANES)

    def column_tile(slot, at, following, store, lanes):
        def row_tile(tile, carry):
            row = pl.multiple_of(tile * SUB, SUB)
            cosine = cosine_ref[pl.ds(first_row + row, SUB), :]
            inverse_square = 1.0 / (cosine * cosine)

            unroll = strip_count if following is not None else 16

            def add_strips(chunk, sums):
                for index in range(unroll):
                    if following is not None and index in (0, 16):
                        columns_into(1 - slot, following, tile * share + (share // 2) * (index > 0), share // 2)
                    strip = chunk * unroll + index

                    def load(shift):
                        return elevation[strip, at, pl.ds(SUB + row + shift, SUB), :]

                    slope_x = slots[slot][strip, pl.ds(row, SUB), :LANES]
                    second_x = slots[slot][strip, pl.ds(row, SUB), LANES:]
                    mask = row_mask[strip, pl.ds(row, SUB), :] * col_mask[strip, at - 1]
                    shifts = (load(-2), load(-1), load(1), load(2))
                    terms = moment_terms(load(0), slope_x, second_x, shifts, inverse_square, mask)
                    sums = [total + term for total, term in zip(sums, terms)]
                return tuple(sums)

            if following is not None:
                sums = add_strips(0, zero_terms())
            else:
                sums = lax.fori_loop(0, strip_count // unroll, add_strips, zero_terms())
            for moment in range(MOMENTS):
                store(moment, pl.ds(row, SUB), lanes, sums[moment])
            return carry

        lax.fori_loop(0, tile_rows, row_tile, 0)

    for which in range(LOAD_PARTS):
        start(initial + 3, which)
    for which in range(LOAD_PARTS):
        for step in range(2):
            start(final + step, which)

    def first_columns(which, carry):
        for step in range(3):
            arrive(initial + step, which)
        for step in range(2):
            columns_into(0, initial + 1, which * part + step * (part // 2), part // 2)
        return carry

    lax.fori_loop(0, LOAD_PARTS, first_columns, 0)

    def arrive_whole(index):
        def body(which, carry):
            arrive(index, which)
            return carry

        lax.fori_loop(0, LOAD_PARTS, body, 0)

    def store_other(moment, rows, lanes, value):
        share = MOMENTS // pieces
        other_refs[moment // share][moment % share, rows, lanes] = value

    def store_mine(moment, rows, lanes, value):
        mine_ref[moment, rows, lanes] = value

    arrive_whole(initial + 3)
    column_tile(0, initial + 1, initial + 2, store_other, slice(0, LANES))
    arrive_whole(final)
    arrive_whole(final + 1)
    column_tile(1, initial + 2, later + 1, store_other, slice(LANES, 2 * LANES))
    column_tile(0, later + 1, later + 2, store_mine, slice(0, LANES))
    column_tile(1, later + 2, None, store_mine, slice(LANES, 2 * LANES))


def moments_of(limits, spread, cosine, weights, strips, order, remote, first_row, row_count, pieces):
    strip_count, row_block, col_count = strips.shape
    half = col_count // LANES // 2
    out = jax.ShapeDtypeStruct((MOMENTS, row_count, col_count // 4), F32)
    piece = jax.ShapeDtypeStruct((MOMENTS // pieces, row_count, col_count // 4), F32)
    token = jax.ShapeDtypeStruct((SUB, LANES), F32)
    vmem = pl.BlockSpec(memory_space=pltpu.VMEM)
    anywhere = pl.BlockSpec(memory_space=pl.ANY)
    lanes = jax.ShapeDtypeStruct((5, strip_count, LANES), F32)
    compact = jax.ShapeDtypeStruct((SUB, 2 * LANES), F32)
    mask = jax.ShapeDtypeStruct((strip_count, row_count, LANES), F32)
    parts = pltpu.VMEM((strip_count, half + 2, row_count, LANES), jnp.bfloat16)
    slot = pltpu.VMEM((strip_count, row_count, 2 * LANES), F32)
    return pl.pallas_call(
        functools.partial(moment_kernel, remote=remote, first_row=first_row, row_count=row_count, pieces=pieces, spread=spread),
        out_shape=(out,) + (piece,) * pieces + (token,) + (lanes, compact, mask) * spread,
        in_specs=[anywhere if spread else vmem] * 2 + [vmem, vmem, anywhere, vmem, vmem],
        out_specs=(vmem,) * (pieces + 2 + 3 * spread),
        scratch_shapes=[
            pltpu.VMEM((strip_count, half + 2, row_count + 2 * SUB, LANES), F32),
            parts,
            parts,
            pltpu.VMEM((strip_count, half, SUB, LANES), F32),
            slot,
            slot,
            pltpu.SemaphoreType.DMA((half + 2, LOAD_PARTS)),
        ]
        + [
            pltpu.SMEM((strip_count,), F32),
            pltpu.SMEM((4, strip_count), jnp.int32),
            pltpu.SemaphoreType.DMA((2,)),
        ]
        * spread,
        compiler_params=pltpu.CompilerParams(vmem_limit_bytes=VMEM_BYTES),
        cost_estimate=SMALL_COST,
        name="moments_remote" if remote else "moments_own",
    )(*limits, cosine, weights, strips, *order)


def edge_kernel(
    limits_ref, compact_ref, cosine_ref, first_in, second_in, first_out, second_out, inner_ref,
    order_ref, mine_ref, other_ref, token_ref, *, remote,
):
    del order_ref
    token_ref[...] = jnp.zeros((SUB, LANES), F32)
    pair, strip_count, col_count = first_out.shape
    row_block = cosine_ref.shape[0]
    even = lax.axis_index("tile") % 2 == 0
    tiles = col_count // LANES
    quarter = tiles // 4
    position = lax.axis_index("acq")
    side = position // 2
    core = position % 2
    row_start = lax.axis_index("tile") * row_block
    lane = lax.broadcasted_iota(jnp.int32, (SUB, LANES), 1)
    above, top = (second_in, first_in), (second_out, first_out)
    below, bottom = (first_in, second_in), (first_out, second_out)
    inner = (inner_ref,)
    sources = [(above, 0), (above, 1), (top, 0), (top, 1), (inner, 0), (inner, 1)]
    sources += [(inner, 2), (inner, 3), (bottom, 0), (bottom, 1), (below, 0), (below, 1)]
    edges = ((0, 2), (1, 3), (row_block - 2, 8), (row_block - 1, 9))
    for out_ref, owner in ((mine_ref, core), (other_ref, 1 - core)):
        for part, owner_side in enumerate((1 - side if remote else side,)):
            out_ref[part, MOMENTS * EDGE_ROWS:MOMENTS * EDGE_ROWS + SUB, :] = compact_ref[...]

            def column_tile(tile, carry, out_ref=out_ref, part=part, first=(owner_side * 2 + owner) * quarter):
                at = first + tile
                left_keep = jnp.where(at > 0, 1.0, 0.0)
                right_keep = jnp.where(at < tiles - 1, 1.0, 0.0)
                here = pl.ds(pl.multiple_of(at * LANES, LANES), LANES)
                before = pl.ds(pl.multiple_of(jnp.maximum(at - 1, 0) * LANES, LANES), LANES)
                after = pl.ds(pl.multiple_of(jnp.minimum(at + 1, tiles - 1) * LANES, LANES), LANES)
                col = (lane + at * LANES).astype(F32)
                out_lanes = pl.ds(pl.multiple_of(tile * LANES, LANES), LANES)
                for edge, (row, source) in enumerate(edges):
                    cosine = cosine_ref[row:row + 1, :]
                    inverse_square = 1.0 / (cosine * cosine)
                    sums = zero_terms()
                    for group in range(strip_count // SUB):
                        strips = slice(group * SUB, (group + 1) * SUB)

                        def load(shift, where):
                            refs, index = sources[source + shift]
                            values = [ref[index, strips, where] for ref in refs]
                            return jnp.where(even, values[0], values[-1]) if len(refs) == 2 else values[0]

                        z = load(0, here)
                        cols = shifted_columns(
                            z, load(0, before) * left_keep, load(0, after) * right_keep, lane
                        )
                        limits = [limits_ref[kind, strips, :] for kind in range(4)]
                        at_row = (row_start + row).astype(F32)
                        inside = (limits[0] <= at_row) & (limits[1] > at_row)
                        inside = inside & (col >= limits[2]) & (col < limits[3])
                        mask = jnp.where(inside, limits_ref[4, strips, :], 0.0)
                        shifts = tuple(load(shift, here) for shift in (-2, -1, 1, 2))
                        terms = stencil_terms(z, shifts, cols, inverse_square, mask)
                        sums = [total + term for total, term in zip(sums, terms)]
                    for moment in range(MOMENTS):
                        spot = moment * EDGE_ROWS + edge
                        out_ref[part, spot:spot + 1, out_lanes] = jnp.sum(sums[moment], axis=0, keepdims=True)
                return carry

            lax.fori_loop(0, quarter, column_tile, 0)


def edge_moments(limits, compact, cosine, arrived, sent, inner, order, remote):
    pair, strip_count, col_count = inner.shape
    out = jax.ShapeDtypeStruct((1, MOMENTS * EDGE_ROWS + SUB, col_count // 4), F32)
    vmem = pl.BlockSpec(memory_space=pltpu.VMEM)
    return pl.pallas_call(
        functools.partial(edge_kernel, remote=remote),
        out_shape=(out, out, jax.ShapeDtypeStruct((SUB, LANES), F32)),
        in_specs=[vmem] * 9,
        out_specs=(vmem, vmem, vmem),
        compiler_params=pltpu.CompilerParams(vmem_limit_bytes=SMALL_VMEM_BYTES),
        cost_estimate=SMALL_COST,
        name="edges_remote" if remote else "edges_own",
    )(limits, compact, cosine, *arrived, *sent, inner, order)


def combine_kernel(mine_ref, *refs, pieces, edges):
    near_refs, rest = refs[:pieces], refs[pieces:]
    out_ref, token_ref = rest[-2:]
    token_ref[...] = jnp.zeros((SUB, LANES), F32)
    share, row_count, width = near_refs[0].shape
    for piece, near_ref in enumerate(near_refs):
        for moment in range(share):
            at = piece * share + moment
            out_ref[at * row_count:(at + 1) * row_count, :] = mine_ref[at] + near_ref[moment]
    if edges:
        edge_mine_ref, edge_core_ref = rest[:2]
        start, count = pieces * share * row_count, MOMENTS * EDGE_ROWS
        out_ref[start:start + count, :] = edge_mine_ref[0, :count] + edge_core_ref[0, :count]
        out_ref[start + count:start + count + SUB, :] = edge_mine_ref[0, count:]
        out_ref[start + count + SUB:, :] = edge_core_ref[0, count:]


def combine(mine, near, edges, order):
    moments, row_count, width = mine.shape
    rows = moments * row_count + sum(edge.shape[1] + SUB for edge in edges[:1])
    vmem = pl.BlockSpec(memory_space=pltpu.VMEM)
    return pl.pallas_call(
        functools.partial(combine_kernel, pieces=len(near), edges=bool(edges)),
        out_shape=(jax.ShapeDtypeStruct((rows, width), F32), jax.ShapeDtypeStruct((SUB, LANES), F32)),
        in_specs=[vmem] * (1 + len(near) + len(edges) + len(order)),
        out_specs=(vmem, vmem),
        compiler_params=pltpu.CompilerParams(vmem_limit_bytes=SMALL_VMEM_BYTES),
        cost_estimate=SMALL_COST,
        name="combine",
    )(mine, *near, *edges, *order)


def finish_kernel(pieces, cosine_ref, mine_ref, edge_mine_ref, edge_core_ref, *refs):
    far_refs, core_refs = refs[:len(pieces)], refs[len(pieces):-6]
    mean_out, covariance_out, mean_ref, covariance_ref, available_ref, sems = refs[-6:]
    row_block, width = mean_ref.shape
    share = MOMENTS // len(core_refs)
    edge_start = MOMENTS * row_block
    compact_start = edge_start + MOMENTS * EDGE_ROWS
    at_row = lax.broadcasted_iota(jnp.int32, (row_block, LANES), 0) + lax.axis_index("tile") * row_block
    at_col = lax.broadcasted_iota(jnp.int32, (width, LANES), 0) + lax.axis_index("acq") * width
    at_row, at_col = at_row.astype(F32), at_col.astype(F32)
    near_start = compact_start - edge_start
    compacts = [ref[0, near_start:near_start + SUB, :LANES] for ref in (edge_mine_ref, edge_core_ref)]
    compacts += [far_refs[-1][compact_start + SUB * part:compact_start + SUB * (part + 1), :LANES] for part in range(2)]
    rows_in, cols_in = [], []
    for compact in compacts:
        row_low, row_high, col_low, col_high, quality = (compact[kind:kind + 1, :] for kind in range(5))
        rows_in.append(jnp.where((at_row >= row_low) & (at_row < row_high), quality, 0.0))
        cols_in.append(jnp.where((at_col >= col_low) & (at_col < col_high), 1.0, 0.0))
    available = lax.dot_general(
        jnp.concatenate(rows_in, axis=1), jnp.concatenate(cols_in, axis=1), (((1,), (1,)), ((), ())),
        precision=lax.Precision.HIGHEST, preferred_element_type=F32,
    )
    available_ref[...] = available
    sub = lax.broadcasted_iota(jnp.int32, (SUB, LANES), 0)
    piece_rows = row_block // len(pieces)
    copies = []
    for first_row, far_ref in zip(pieces, far_refs):
        for tile_row in range(first_row, first_row + piece_rows, SUB):
            rows = slice(tile_row, tile_row + SUB)
            cosine = cosine_ref[rows, :]
            scales = (1.0, 1.0 / (12.0 * cosine), 1.0 / 12.0, 1.0 / 12.0)
            spots = {0: ((0, 0), (1, 1)), row_block - SUB: ((SUB - 2, 2), (SUB - 1, 3))}.get(tile_row, ())
            for tile in range(width // LANES):
                lanes = slice(tile * LANES, (tile + 1) * LANES)

                def total(moment):
                    near = core_refs[moment // share][moment % share, rows, lanes]
                    far_row = moment * piece_rows + tile_row - first_row
                    value = (mine_ref[moment, rows, lanes] + near) + far_ref[far_row:far_row + SUB, lanes]
                    for at, edge in spots:
                        spot = moment * EDGE_ROWS + edge
                        edge_far = far_refs[-1][edge_start + spot:edge_start + spot + 1, lanes]
                        spot = slice(spot, spot + 1)
                        line = (edge_mine_ref[0, spot, lanes] + edge_core_ref[0, spot, lanes]) + edge_far
                        value = jnp.where(sub == at, line, value)
                    return value

                along, across = total(FEATURES + 4), total(FEATURES + 7)
                steep = along / (cosine * cosine) + across
                inverse = 144.0 / jnp.maximum(available_ref[rows, lanes] - steep, 1.0)
                means = [total(first) * inverse * scales[first] for first in range(FEATURES)]
                mean_ref[rows, lanes] = means[0]
                entry = 0
                for first in range(FEATURES):
                    for second in range(first, FEATURES):
                        scale = scales[first] * scales[second]
                        covariance_ref[entry, rows, lanes] = (
                            total(FEATURES + entry) * inverse * scale - means[first] * means[second]
                        )
                        entry += 1
            if (tile_row + SUB) % (row_block // 2) == 0:
                which = tile_row // (row_block // 2)
                block = pl.ds(which * (row_block // 2), row_block // 2)
                copies += [
                    pltpu.make_async_copy(mean_ref.at[block], mean_out.at[block], sems.at[0, which]),
                    pltpu.make_async_copy(
                        covariance_ref.at[:, block], covariance_out.at[:, block], sems.at[1, which]
                    ),
                ]
                for copy in copies[-2:]:
                    copy.start()
    for copy in copies:
        copy.wait()


def finish(pieces, cosine, mine, edge_mine, edge_core, far, core):
    moments, row_block, width = mine.shape
    vmem = pl.BlockSpec(memory_space=pltpu.VMEM)
    entries = FEATURES * (FEATURES + 1) // 2
    return pl.pallas_call(
        functools.partial(finish_kernel, pieces),
        out_shape=(
            jax.ShapeDtypeStruct((row_block, width), F32),
            jax.ShapeDtypeStruct((entries, row_block, width), F32),
        ),
        in_specs=[vmem] * (4 + len(far) + len(core)),
        out_specs=(pl.BlockSpec(memory_space=pl.ANY),) * 2,
        scratch_shapes=[
            pltpu.VMEM((row_block, width), F32),
            pltpu.VMEM((entries, row_block, width), F32),
            pltpu.VMEM((row_block, width), F32),
            pltpu.SemaphoreType.DMA((2, 2)),
        ],
        compiler_params=pltpu.CompilerParams(vmem_limit_bytes=SMALL_VMEM_BYTES),
        cost_estimate=SMALL_COST,
        name="finish",
    )(cosine, mine, edge_mine, edge_core, *far, *core)


def exchange(value, distance):
    count = lax.axis_size("acq")
    return lax.ppermute(value, "acq", [(source, source ^ distance) for source in range(count)])


def local(strips, strip_quality, valid_ranges):
    strip_count, row_block, col_count = strips.shape
    tile_count = lax.axis_size("tile")
    ranges = valid_ranges.T

    *sent, inner, cosine, weights, token = halo_rows(strips)
    arrived = []
    for first, value in enumerate(sent):
        pairs = [(i, i + 1) for i in range(first, tile_count - 1, 2)]
        swaps = pairs + [(target, source) for source, target in pairs]
        arrived.append(lax.ppermute(value, "tile", swaps))

    def compute(order, remote, source):
        return moments_of(source, remote, cosine, weights, strips, order, remote, 0, row_block, PIECES)

    def edges(order, remote):
        return edge_moments(limits, compact, cosine, arrived, sent, inner, order, remote)

    def swap(parts):
        return [exchange(part, 1) for part in parts]

    mine, *other, token, limits, compact, mask = compute((token, token), True, (strip_quality, ranges))
    near = swap(other)
    edge_mine, edge_other, token = edges(token, True)
    payload, token = combine(mine, near, (edge_mine, exchange(edge_other, 1)), (token,))
    far = exchange(payload, 2)
    edge_mine, edge_other, token = edges(token, False)
    mine, *other, token = compute((token, token), False, (limits, mask))
    return finish((0,), cosine, mine, edge_mine, exchange(edge_other, 1), [far], swap(other))


def solution(mesh):
    return jax.shard_map(
        local,
        mesh=mesh,
        in_specs=(P("acq", "tile", None), P("acq"), P("acq", None)),
        out_specs=(P("tile", "acq"), P(None, "tile", "acq")),
        check_vma=False,
    )
```

```python
import functools
import jax
import jax.numpy as jnp
from jax import lax
from jax.experimental import pallas as pl
from jax.experimental.pallas import tpu as pltpu
from jax.sharding import PartitionSpec as P

MOMENTS = 14
FEATURES = 4
SUB = 8
LANES = 128
EDGE_ROWS = 4
VMEM_BYTES = 50 * 1024 * 1024
SMALL_VMEM_BYTES = 50 * 1024 * 1024
F32 = jnp.float32
LOAD_PARTS = 4
PIECES = 2
SMALL_COST = pl.CostEstimate(flops=1, bytes_accessed=1, transcendentals=0)


def moment_terms(z, slope_x, second_x, rows, inverse_square, mask):
    row_m2, row_m1, row_p1, row_p2 = rows
    slope_y = 8.0 * (row_p1 - row_m1) - (row_p2 - row_m2)
    second_y = 16.0 * (row_p1 + row_m1) - (row_p2 + row_m2) - 30.0 * z
    curvature = second_x * inverse_square + second_y
    steepness = (144.0 + slope_y * slope_y) + slope_x * slope_x * inverse_square
    weight = mask / steepness
    features = (z, slope_x, slope_y, curvature)
    weighted = [weight * feature for feature in features]
    terms = list(weighted)
    for first in range(FEATURES):
        for second in range(first, FEATURES):
            terms.append(weighted[first] * features[second])
    return terms


def stencil_terms(z, rows, cols, inverse_square, mask):
    col_m2, col_m1, col_p1, col_p2 = cols
    slope_x = 8.0 * (col_p1 - col_m1) - (col_p2 - col_m2)
    second_x = 16.0 * (col_p1 + col_m1) - (col_p2 + col_m2) - 30.0 * z
    return moment_terms(z, slope_x, second_x, rows, inverse_square, mask)


def shifted_columns(z, left, right, lane):
    return (
        pltpu.roll(jnp.where(lane >= LANES - 2, left, z), 2, 1),
        pltpu.roll(jnp.where(lane == LANES - 1, left, z), 1, 1),
        pltpu.roll(jnp.where(lane == 0, right, z), LANES - 1, 1),
        pltpu.roll(jnp.where(lane < 2, right, z), LANES - 2, 1),
    )


def zero_terms():
    return tuple(jnp.zeros((SUB, LANES), F32) for _ in range(MOMENTS))


def halo_kernel(
    strips_ref, first_out, second_out, inner_ref, cosine_ref, weights_ref, token_ref,
    first_ref, last_ref, sems,
):
    token_ref[...] = jnp.zeros((SUB, LANES), F32)
    strip_count, row_block, col_count = strips_ref.shape
    copies = []
    for tile in range(col_count // LANES):
        lanes = pl.ds(tile * LANES, LANES)
        for which, (start, target) in enumerate(((0, first_ref), (row_block - SUB, last_ref))):
            copies.append(
                pltpu.make_async_copy(
                    strips_ref.at[:, pl.ds(start, SUB), lanes], target.at[tile], sems.at[which, tile]
                )
            )
    for copy in copies:
        copy.start()
    weights_ref[...] = column_weights()
    total_rows = row_block * lax.axis_size("tile")
    row_start = lax.axis_index("tile") * row_block
    even = lax.axis_index("tile") % 2 == 0
    for tile in range(row_block // SUB):
        row = lax.broadcasted_iota(jnp.int32, (SUB, LANES), 0) + (row_start + tile * SUB)
        latitude = -1.0 + 2.0 * (row.astype(F32) + 0.5) / total_rows
        cosine_ref[tile * SUB:(tile + 1) * SUB, :] = jnp.cos(latitude)

    first_rows = first_ref.reshape(col_count // LANES, strip_count * SUB, LANES)
    last_rows = last_ref.reshape(col_count // LANES, strip_count * SUB, LANES)
    for tile in range(col_count // LANES):
        copies[2 * tile].wait()
        copies[2 * tile + 1].wait()
        lanes = slice(tile * LANES, (tile + 1) * LANES)
        for group in range(strip_count // SUB):
            strips = slice(group * SUB, (group + 1) * SUB)
            for row in range(2):
                at = group * SUB * SUB
                top = first_rows[tile, pl.ds(at + row, SUB, stride=SUB), :]
                bottom = last_rows[tile, pl.ds(at + 6 + row, SUB, stride=SUB), :]
                first_out[row, strips, lanes] = jnp.where(even, bottom, top)
                second_out[row, strips, lanes] = jnp.where(even, top, bottom)
                inner_ref[row, strips, lanes] = first_rows[tile, pl.ds(at + 2 + row, SUB, stride=SUB), :]
                inner_ref[2 + row, strips, lanes] = last_rows[tile, pl.ds(at + 4 + row, SUB, stride=SUB), :]


def halo_rows(strips):
    strip_count, row_block, col_count = strips.shape
    tiles = col_count // LANES
    pair = jax.ShapeDtypeStruct((2, strip_count, col_count), F32)
    inner = jax.ShapeDtypeStruct((4, strip_count, col_count), F32)
    cosine = jax.ShapeDtypeStruct((row_block, LANES), F32)
    weights = jax.ShapeDtypeStruct((4 * LANES, 2 * LANES), jnp.bfloat16)
    vmem = pl.BlockSpec(memory_space=pltpu.VMEM)
    hbm = pl.BlockSpec(memory_space=pltpu.HBM)
    return pl.pallas_call(
        halo_kernel,
        out_shape=(pair, pair, inner, cosine, weights, jax.ShapeDtypeStruct((SUB, LANES), F32)),
        in_specs=[hbm],
        out_specs=(vmem,) * 6,
        scratch_shapes=[
            pltpu.VMEM((tiles, strip_count, SUB, LANES), F32),
            pltpu.VMEM((tiles, strip_count, SUB, LANES), F32),
            pltpu.SemaphoreType.DMA((2, tiles)),
        ],
        compiler_params=pltpu.CompilerParams(vmem_limit_bytes=SMALL_VMEM_BYTES),
        cost_estimate=SMALL_COST,
        name="halo_rows",
    )(strips)


def column_weights():
    source = lax.broadcasted_iota(jnp.int32, (4 * LANES, 2 * LANES), 0)
    target = lax.broadcasted_iota(jnp.int32, (4 * LANES, 2 * LANES), 1)
    lane = source % LANES
    lane = jnp.where(source < 2 * LANES, lane, jnp.where(lane < LANES // 2, lane + LANES, lane - LANES))
    distance = lane - target % LANES
    near, far = jnp.abs(distance) == 1, jnp.abs(distance) == 2
    sign = jnp.where(distance > 0, 1.0, -1.0)
    slope = jnp.where(near, 8.0 * sign, jnp.where(far, -sign, 0.0))
    second = jnp.where(near, 16.0, jnp.where(far, -1.0, jnp.where(distance == 0, -30.0, 0.0)))
    return jnp.where(target < LANES, slope, second).astype(jnp.bfloat16)


def moment_kernel(*refs, remote, first_row, row_count, pieces, spread):
    if spread:
        small_sems = refs[-1]
        quality_ref, ranges_ref = refs[-3:-1]
        small_copies = [
            pltpu.make_async_copy(refs[kind], refs[kind - 3], small_sems.at[kind]) for kind in range(2)
        ]
        refs = refs[2:-3]
    else:
        limits_ref, row_mask = refs[:2]
        refs = refs[2:]
    cosine_ref, weights, strips_ref, first_order_ref, second_order_ref, mine_ref = refs[:6]
    refs = refs[6:]
    other_refs, token_ref = refs[:pieces], refs[pieces]
    if spread:
        limits_ref, compact_ref, row_mask = refs[pieces + 1:pieces + 4]
        refs = refs[3:]
    elevation, high_part, low_part, col_mask, first_slot, second_slot, sems = refs[pieces + 1:]
    del first_order_ref, second_order_ref
    token_ref[...] = jnp.zeros((SUB, LANES), F32)
    strip_count, row_block, col_count = strips_ref.shape
    tiles = col_count // LANES
    half = tiles // 2
    quarter = half // 2
    position = lax.axis_index("acq")
    side = position // 2
    core = position % 2
    base = (1 - side if remote else side) * half
    row_start = lax.axis_index("tile") * row_block + first_row
    low = max(first_row - SUB, 0)
    high = min(first_row + row_count + SUB, row_block)
    offset = SUB - (first_row - low)

    part = strip_count // LOAD_PARTS

    def fetch(index, which):
        lanes = pl.ds(pl.multiple_of((base + index - 1) * LANES, LANES), LANES)
        strips = pl.ds(which * part, part)
        return pltpu.make_async_copy(
            strips_ref.at[strips, pl.ds(low, high - low), lanes],
            elevation.at[strips, index, pl.ds(offset, high - low), :],
            sems.at[index, which],
        )

    def present(index):
        return (base + index >= 1) & (base + index <= tiles)

    def start(index, which):
        @pl.when(present(index))
        def _():
            fetch(index, which).start()

    zero = jnp.zeros((SUB, LANES), F32)

    def blank(index):
        @pl.when(jnp.logical_not(present(index)))
        def _():
            def body(strip, carry):
                for row in range(1, row_count // SUB + 1):
                    elevation[strip, index, row * SUB:(row + 1) * SUB, :] = zero
                return carry

            lax.fori_loop(0, strip_count, body, 0)

    def arrive(index, which):
        @pl.when(present(index))
        def _():
            fetch(index, which).wait()

        def split(step, carry):
            strip = which * part + step
            value = elevation[strip, index, SUB:SUB + row_count, :]
            upper = value.astype(jnp.bfloat16)
            high_part[strip, index] = upper
            low_part[strip, index] = (value - upper.astype(F32)).astype(jnp.bfloat16)
            return carry

        lax.fori_loop(0, part, split, 0, unroll=4)

    initial = (1 - core) * quarter
    later = core * quarter
    final = later + 2 * core
    for which in range(LOAD_PARTS):
        for step in range(3):
            start(initial + step, which)
    if spread:
        for copy in small_copies:
            copy.start()
    blank(0)
    blank(half + 1)

    def spread_out(strip, rows):
        here = pl.ds(strip, 1)
        values = [ranges_ref[kind, strip].astype(F32) for kind in range(4)] + [quality_ref[strip]]
        lane = lax.broadcasted_iota(jnp.int32, (1, LANES), 1)
        for kind, value in enumerate(values):
            limits_ref[kind, here, :] = jnp.full((1, LANES), value, F32)
        return tuple(jnp.where(lane == strip, value, row) for row, value in zip(rows, values))

    if spread:
        for copy in small_copies:
            copy.wait()
        rows = lax.fori_loop(0, strip_count, spread_out, (jnp.zeros((1, LANES), F32),) * 5)
        compact_ref[...] = jnp.zeros((SUB, 2 * LANES), F32)
        for kind, row in enumerate(rows):
            compact_ref[kind:kind + 1, :LANES] = row

    def prepare(strip, carry):
        row_low, row_high, col_low, col_high, quality = (
            limits_ref[kind, pl.ds(strip, 1), :] for kind in range(5)
        )
        for tile in range(row_count // SUB if spread else 0):
            row = (lax.broadcasted_iota(jnp.int32, (SUB, LANES), 0) + (row_start + tile * SUB)).astype(F32)
            row_mask[strip, tile * SUB:(tile + 1) * SUB, :] = jnp.where(
                (row >= row_low) & (row < row_high), quality, 0.0
            )
        for tile in range(half):
            col = (lax.broadcasted_iota(jnp.int32, (SUB, LANES), 1) + (base + tile) * LANES).astype(F32)
            col_mask[strip, tile] = jnp.where((col >= col_low) & (col < col_high), 1.0, 0.0)
        if low == first_row:
            for tile in range(half + 2):
                elevation[strip, tile, 0:SUB, :] = zero
        if high == first_row + row_count:
            for tile in range(half + 2):
                elevation[strip, tile, SUB + row_count:2 * SUB + row_count, :] = zero
        return carry

    lax.fori_loop(0, strip_count, prepare, 0)

    tile_rows = row_count // SUB
    share = strip_count // tile_rows
    slots = (first_slot, second_slot)

    def columns_into(slot, at, first, count):
        strips = pl.ds(first, count)
        lane = lax.broadcasted_iota(jnp.int32, (count * row_count, LANES), 1)

        def load(ref, tile):
            return ref[strips, tile].reshape(count * row_count, LANES)

        edges = [
            jnp.where(lane < LANES // 2, load(ref, at + 1), load(ref, at - 1))
            for ref in (high_part, low_part)
        ]
        left = jnp.concatenate([load(high_part, at), load(low_part, at)] + edges, axis=1)
        product = jnp.dot(left, weights[...], preferred_element_type=F32)
        slots[slot][strips] = product.reshape(count, row_count, 2 * LANES)

    def column_tile(slot, at, following, store, lanes):
        def row_tile(tile, carry):
            row = pl.multiple_of(tile * SUB, SUB)
            cosine = cosine_ref[pl.ds(first_row + row, SUB), :]
            inverse_square = 1.0 / (cosine * cosine)

            unroll = strip_count if following is not None else strip_count // 2

            def add_strips(chunk, sums):
                for index in range(unroll):
                    if following is not None and index in (0, 16):
                        columns_into(1 - slot, following, tile * share + (share // 2) * (index > 0), share // 2)
                    strip = chunk * unroll + index

                    def load(shift):
                        return elevation[strip, at, pl.ds(SUB + row + shift, SUB), :]

                    slope_x = slots[slot][strip, pl.ds(row, SUB), :LANES]
                    second_x = slots[slot][strip, pl.ds(row, SUB), LANES:]
                    mask = row_mask[strip, pl.ds(row, SUB), :] * col_mask[strip, at - 1]
                    shifts = (load(-2), load(-1), load(1), load(2))
                    terms = moment_terms(load(0), slope_x, second_x, shifts, inverse_square, mask)
                    sums = [total + term for total, term in zip(sums, terms)]
                return tuple(sums)

            if following is not None:
                sums = add_strips(0, zero_terms())
            else:
                sums = lax.fori_loop(0, strip_count // unroll, add_strips, zero_terms())
            for moment in range(MOMENTS):
                store(moment, pl.ds(row, SUB), lanes, sums[moment])
            return carry

        lax.fori_loop(0, tile_rows, row_tile, 0)

    for which in range(LOAD_PARTS):
        start(initial + 3, which)
    for which in range(LOAD_PARTS):
        for step in range(2):
            start(final + step, which)

    def first_columns(which, carry):
        for step in range(3):
            arrive(initial + step, which)
        for step in range(2):
            columns_into(0, initial + 1, which * part + step * (part // 2), part // 2)
        return carry

    lax.fori_loop(0, LOAD_PARTS, first_columns, 0)

    def arrive_whole(index):
        def body(which, carry):
            arrive(index, which)
            return carry

        lax.fori_loop(0, LOAD_PARTS, body, 0)

    def store_other(moment, rows, lanes, value):
        share = MOMENTS // pieces
        other_refs[moment // share][moment % share, rows, lanes] = value

    def store_mine(moment, rows, lanes, value):
        mine_ref[moment, rows, lanes] = value

    arrive_whole(initial + 3)
    column_tile(0, initial + 1, initial + 2, store_other, slice(0, LANES))
    arrive_whole(final)
    arrive_whole(final + 1)
    column_tile(1, initial + 2, later + 1, store_other, slice(LANES, 2 * LANES))
    column_tile(0, later + 1, later + 2, store_mine, slice(0, LANES))
    column_tile(1, later + 2, None, store_mine, slice(LANES, 2 * LANES))


def moments_of(limits, spread, cosine, weights, strips, order, remote, first_row, row_count, pieces):
    strip_count, row_block, col_count = strips.shape
    half = col_count // LANES // 2
    out = jax.ShapeDtypeStruct((MOMENTS, row_count, col_count // 4), F32)
    piece = jax.ShapeDtypeStruct((MOMENTS // pieces, row_count, col_count // 4), F32)
    token = jax.ShapeDtypeStruct((SUB, LANES), F32)
    vmem = pl.BlockSpec(memory_space=pltpu.VMEM)
    anywhere = pl.BlockSpec(memory_space=pl.ANY)
    lanes = jax.ShapeDtypeStruct((5, strip_count, LANES), F32)
    compact = jax.ShapeDtypeStruct((SUB, 2 * LANES), F32)
    mask = jax.ShapeDtypeStruct((strip_count, row_count, LANES), F32)
    parts = pltpu.VMEM((strip_count, half + 2, row_count, LANES), jnp.bfloat16)
    slot = pltpu.VMEM((strip_count, row_count, 2 * LANES), F32)
    return pl.pallas_call(
        functools.partial(moment_kernel, remote=remote, first_row=first_row, row_count=row_count, pieces=pieces, spread=spread),
        out_shape=(out,) + (piece,) * pieces + (token,) + (lanes, compact, mask) * spread,
        in_specs=[anywhere if spread else vmem] * 2 + [vmem, vmem, anywhere, vmem, vmem],
        out_specs=(vmem,) * (pieces + 2 + 3 * spread),
        scratch_shapes=[
            pltpu.VMEM((strip_count, half + 2, row_count + 2 * SUB, LANES), F32),
            parts,
            parts,
            pltpu.VMEM((strip_count, half, SUB, LANES), F32),
            slot,
            slot,
            pltpu.SemaphoreType.DMA((half + 2, LOAD_PARTS)),
        ]
        + [
            pltpu.SMEM((strip_count,), F32),
            pltpu.SMEM((4, strip_count), jnp.int32),
            pltpu.SemaphoreType.DMA((2,)),
        ]
        * spread,
        compiler_params=pltpu.CompilerParams(vmem_limit_bytes=VMEM_BYTES),
        cost_estimate=SMALL_COST,
        name="moments_remote" if remote else "moments_own",
    )(*limits, cosine, weights, strips, *order)


def edge_kernel(
    limits_ref, compact_ref, cosine_ref, first_in, second_in, first_out, second_out, inner_ref,
    order_ref, mine_ref, other_ref, token_ref, *, remote,
):
    del order_ref
    token_ref[...] = jnp.zeros((SUB, LANES), F32)
    pair, strip_count, col_count = first_out.shape
    row_block = cosine_ref.shape[0]
    even = lax.axis_index("tile") % 2 == 0
    tiles = col_count // LANES
    quarter = tiles // 4
    position = lax.axis_index("acq")
    side = position // 2
    core = position % 2
    row_start = lax.axis_index("tile") * row_block
    lane = lax.broadcasted_iota(jnp.int32, (SUB, LANES), 1)
    above, top = (second_in, first_in), (second_out, first_out)
    below, bottom = (first_in, second_in), (first_out, second_out)
    inner = (inner_ref,)
    sources = [(above, 0), (above, 1), (top, 0), (top, 1), (inner, 0), (inner, 1)]
    sources += [(inner, 2), (inner, 3), (bottom, 0), (bottom, 1), (below, 0), (below, 1)]
    edges = ((0, 2), (1, 3), (row_block - 2, 8), (row_block - 1, 9))
    for out_ref, owner in ((mine_ref, core), (other_ref, 1 - core)):
        for part, owner_side in enumerate((1 - side if remote else side,)):
            out_ref[part, MOMENTS * EDGE_ROWS:MOMENTS * EDGE_ROWS + SUB, :] = compact_ref[...]

            def column_tile(tile, carry, out_ref=out_ref, part=part, first=(owner_side * 2 + owner) * quarter):
                at = first + tile
                left_keep = jnp.where(at > 0, 1.0, 0.0)
                right_keep = jnp.where(at < tiles - 1, 1.0, 0.0)
                here = pl.ds(pl.multiple_of(at * LANES, LANES), LANES)
                before = pl.ds(pl.multiple_of(jnp.maximum(at - 1, 0) * LANES, LANES), LANES)
                after = pl.ds(pl.multiple_of(jnp.minimum(at + 1, tiles - 1) * LANES, LANES), LANES)
                col = (lane + at * LANES).astype(F32)
                out_lanes = pl.ds(pl.multiple_of(tile * LANES, LANES), LANES)
                for edge, (row, source) in enumerate(edges):
                    cosine = cosine_ref[row:row + 1, :]
                    inverse_square = 1.0 / (cosine * cosine)
                    sums = zero_terms()
                    for group in range(strip_count // SUB):
                        strips = slice(group * SUB, (group + 1) * SUB)

                        def load(shift, where):
                            refs, index = sources[source + shift]
                            values = [ref[index, strips, where] for ref in refs]
                            return jnp.where(even, values[0], values[-1]) if len(refs) == 2 else values[0]

                        z = load(0, here)
                        cols = shifted_columns(
                            z, load(0, before) * left_keep, load(0, after) * right_keep, lane
                        )
                        limits = [limits_ref[kind, strips, :] for kind in range(4)]
                        at_row = (row_start + row).astype(F32)
                        inside = (limits[0] <= at_row) & (limits[1] > at_row)
                        inside = inside & (col >= limits[2]) & (col < limits[3])
                        mask = jnp.where(inside, limits_ref[4, strips, :], 0.0)
                        shifts = tuple(load(shift, here) for shift in (-2, -1, 1, 2))
                        terms = stencil_terms(z, shifts, cols, inverse_square, mask)
                        sums = [total + term for total, term in zip(sums, terms)]
                    for moment in range(MOMENTS):
                        spot = moment * EDGE_ROWS + edge
                        out_ref[part, spot:spot + 1, out_lanes] = jnp.sum(sums[moment], axis=0, keepdims=True)
                return carry

            lax.fori_loop(0, quarter, column_tile, 0)


def edge_moments(limits, compact, cosine, arrived, sent, inner, order, remote):
    pair, strip_count, col_count = inner.shape
    out = jax.ShapeDtypeStruct((1, MOMENTS * EDGE_ROWS + SUB, col_count // 4), F32)
    vmem = pl.BlockSpec(memory_space=pltpu.VMEM)
    return pl.pallas_call(
        functools.partial(edge_kernel, remote=remote),
        out_shape=(out, out, jax.ShapeDtypeStruct((SUB, LANES), F32)),
        in_specs=[vmem] * 9,
        out_specs=(vmem, vmem, vmem),
        compiler_params=pltpu.CompilerParams(vmem_limit_bytes=SMALL_VMEM_BYTES),
        cost_estimate=SMALL_COST,
        name="edges_remote" if remote else "edges_own",
    )(limits, compact, cosine, *arrived, *sent, inner, order)


def combine_kernel(mine_ref, *refs, pieces, edges):
    near_refs, rest = refs[:pieces], refs[pieces:]
    out_ref, token_ref = rest[-2:]
    token_ref[...] = jnp.zeros((SUB, LANES), F32)
    share, row_count, width = near_refs[0].shape
    for piece, near_ref in enumerate(near_refs):
        for moment in range(share):
            at = piece * share + moment
            out_ref[at * row_count:(at + 1) * row_count, :] = mine_ref[at] + near_ref[moment]
    if edges:
        edge_mine_ref, edge_core_ref = rest[:2]
        start, count = pieces * share * row_count, MOMENTS * EDGE_ROWS
        out_ref[start:start + count, :] = edge_mine_ref[0, :count] + edge_core_ref[0, :count]
        out_ref[start + count:, :LANES] = edge_mine_ref[0, count:, :LANES]
        out_ref[start + count:, LANES:] = edge_core_ref[0, count:, :LANES]


def combine(mine, near, edges, order):
    moments, row_count, width = mine.shape
    rows = moments * row_count + sum(edge.shape[1] for edge in edges[:1])
    vmem = pl.BlockSpec(memory_space=pltpu.VMEM)
    return pl.pallas_call(
        functools.partial(combine_kernel, pieces=len(near), edges=bool(edges)),
        out_shape=(jax.ShapeDtypeStruct((rows, width), F32), jax.ShapeDtypeStruct((SUB, LANES), F32)),
        in_specs=[vmem] * (1 + len(near) + len(edges) + len(order)),
        out_specs=(vmem, vmem),
        compiler_params=pltpu.CompilerParams(vmem_limit_bytes=SMALL_VMEM_BYTES),
        cost_estimate=SMALL_COST,
        name="combine",
    )(mine, *near, *edges, *order)


def finish_kernel(pieces, cosine_ref, mine_ref, edge_mine_ref, edge_core_ref, *refs):
    far_refs, core_refs = refs[:len(pieces)], refs[len(pieces):-6]
    mean_out, covariance_out, mean_ref, covariance_ref, available_ref, sems = refs[-6:]
    row_block, width = mean_ref.shape
    share = MOMENTS // len(core_refs)
    edge_start = MOMENTS * row_block
    compact_start = edge_start + MOMENTS * EDGE_ROWS
    at_row = lax.broadcasted_iota(jnp.int32, (row_block, LANES), 0) + lax.axis_index("tile") * row_block
    at_col = lax.broadcasted_iota(jnp.int32, (width, LANES), 0) + lax.axis_index("acq") * width
    at_row, at_col = at_row.astype(F32), at_col.astype(F32)
    near_start = compact_start - edge_start
    compacts = [ref[0, near_start:near_start + SUB, :LANES] for ref in (edge_mine_ref, edge_core_ref)]
    compacts += [far_refs[-1][compact_start:, part * LANES:(part + 1) * LANES] for part in range(2)]
    rows_in, cols_in = [], []
    for compact in compacts:
        row_low, row_high, col_low, col_high, quality = (compact[kind:kind + 1, :] for kind in range(5))
        rows_in.append(jnp.where((at_row >= row_low) & (at_row < row_high), quality, 0.0))
        cols_in.append(jnp.where((at_col >= col_low) & (at_col < col_high), 1.0, 0.0))
    rest = jnp.concatenate(rows_in, axis=1)
    cols_in = jnp.concatenate(cols_in, axis=1).astype(jnp.bfloat16)
    available = jnp.zeros((row_block, width), F32)
    for _ in range(3):
        part = rest.astype(jnp.bfloat16)
        rest = rest - part.astype(F32)
        available += lax.dot_general(
            part, cols_in, (((1,), (1,)), ((), ())), preferred_element_type=F32
        )
    available_ref[...] = available
    sub = lax.broadcasted_iota(jnp.int32, (SUB, LANES), 0)
    piece_rows = row_block // len(pieces)
    copies = []
    for first_row, far_ref in zip(pieces, far_refs):
        for tile_row in range(first_row, first_row + piece_rows, SUB):
            rows = slice(tile_row, tile_row + SUB)
            cosine = cosine_ref[rows, :]
            scales = (1.0, 1.0 / (12.0 * cosine), 1.0 / 12.0, 1.0 / 12.0)
            spots = {0: ((0, 0), (1, 1)), row_block - SUB: ((SUB - 2, 2), (SUB - 1, 3))}.get(tile_row, ())
            for tile in range(width // LANES):
                lanes = slice(tile * LANES, (tile + 1) * LANES)

                def total(moment):
                    near = core_refs[moment // share][moment % share, rows, lanes]
                    far_row = moment * piece_rows + tile_row - first_row
                    value = (mine_ref[moment, rows, lanes] + near) + far_ref[far_row:far_row + SUB, lanes]
                    for at, edge in spots:
                        spot = moment * EDGE_ROWS + edge
                        edge_far = far_refs[-1][edge_start + spot:edge_start + spot + 1, lanes]
                        spot = slice(spot, spot + 1)
                        line = (edge_mine_ref[0, spot, lanes] + edge_core_ref[0, spot, lanes]) + edge_far
                        value = jnp.where(sub == at, line, value)
                    return value

                along, across = total(FEATURES + 4), total(FEATURES + 7)
                steep = along / (cosine * cosine) + across
                inverse = 144.0 / jnp.maximum(available_ref[rows, lanes] - steep, 1.0)
                means = [total(first) * inverse * scales[first] for first in range(FEATURES)]
                mean_ref[rows, lanes] = means[0]
                entry = 0
                for first in range(FEATURES):
                    for second in range(first, FEATURES):
                        scale = scales[first] * scales[second]
                        covariance_ref[entry, rows, lanes] = (
                            total(FEATURES + entry) * inverse * scale - means[first] * means[second]
                        )
                        entry += 1
            if (tile_row + SUB) % (row_block // 2) == 0:
                which = tile_row // (row_block // 2)
                block = pl.ds(which * (row_block // 2), row_block // 2)
                copies += [
                    pltpu.make_async_copy(mean_ref.at[block], mean_out.at[block], sems.at[0, which]),
                    pltpu.make_async_copy(
                        covariance_ref.at[:, block], covariance_out.at[:, block], sems.at[1, which]
                    ),
                ]
                for copy in copies[-2:]:
                    copy.start()
    for copy in copies:
        copy.wait()


def finish(pieces, cosine, mine, edge_mine, edge_core, far, core):
    moments, row_block, width = mine.shape
    vmem = pl.BlockSpec(memory_space=pltpu.VMEM)
    entries = FEATURES * (FEATURES + 1) // 2
    return pl.pallas_call(
        functools.partial(finish_kernel, pieces),
        out_shape=(
            jax.ShapeDtypeStruct((row_block, width), F32),
            jax.ShapeDtypeStruct((entries, row_block, width), F32),
        ),
        in_specs=[vmem] * (4 + len(far) + len(core)),
        out_specs=(pl.BlockSpec(memory_space=pl.ANY),) * 2,
        scratch_shapes=[
            pltpu.VMEM((row_block, width), F32),
            pltpu.VMEM((entries, row_block, width), F32),
            pltpu.VMEM((row_block, width), F32),
            pltpu.SemaphoreType.DMA((2, 2)),
        ],
        compiler_params=pltpu.CompilerParams(vmem_limit_bytes=SMALL_VMEM_BYTES),
        cost_estimate=SMALL_COST,
        name="finish",
    )(cosine, mine, edge_mine, edge_core, *far, *core)


def exchange(value, distance):
    count = lax.axis_size("acq")
    return lax.ppermute(value, "acq", [(source, source ^ distance) for source in range(count)])


def local(strips, strip_quality, valid_ranges):
    strip_count, row_block, col_count = strips.shape
    tile_count = lax.axis_size("tile")
    ranges = valid_ranges.T

    *sent, inner, cosine, weights, token = halo_rows(strips)
    arrived = []
    for first, value in enumerate(sent):
        pairs = [(i, i + 1) for i in range(first, tile_count - 1, 2)]
        swaps = pairs + [(target, source) for source, target in pairs]
        arrived.append(lax.ppermute(value, "tile", swaps))

    def compute(order, remote, source):
        return moments_of(source, remote, cosine, weights, strips, order, remote, 0, row_block, PIECES)

    def edges(order, remote):
        return edge_moments(limits, compact, cosine, arrived, sent, inner, order, remote)

    def swap(parts):
        return [exchange(part, 1) for part in parts]

    mine, *other, token, limits, compact, mask = compute((token, token), True, (strip_quality, ranges))
    near = swap(other)
    edge_mine, edge_other, token = edges(token, True)
    payload, token = combine(mine, near, (edge_mine, exchange(edge_other, 1)), (token,))
    far = exchange(payload, 2)
    edge_mine, edge_other, token = edges(token, False)
    mine, *other, token = compute((token, token), False, (limits, mask))
    return finish((0,), cosine, mine, edge_mine, exchange(edge_other, 1), [far], swap(other))


def solution(mesh):
    return jax.shard_map(
        local,
        mesh=mesh,
        in_specs=(P("acq", "tile", None), P("acq"), P("acq", None)),
        out_specs=(P("tile", "acq"), P(None, "tile", "acq")),
        check_vma=False,
    )
```
